128 devices in a mesh: story: 16 (over z, y), plan: 8 (over x, core).
Axes of the slice: x: 4, y: 4, z: 4, core: 2. Of those that a mesh axis runs over, the one named last changes fastest.
Arguments:
- schur_blocks: float32 [16, 8, 4, 1, 6, 128, 128], P('story', 'plan'), may hold values from -4 to 19, as said below
- off_pattern: int32 [16, 8, 4, 1, 2, 2], P('story', 'plan'), may hold values from 0 to 3, as said below
- face_owner: int32 [16, 8, 4, 1], P('story', 'plan'), may hold values from 0 to 1, as said below
- residual: float32 [16, 8, 4, 1, 64, 512], P('story', 'plan'), may hold values from -6 to 6
- coarse_basis: float32 [16, 8, 4, 1, 30, 512], P('story', 'plan'), may hold values from -0.25 to 0.25
- coarse_inverse: float32 [768, 768], replicated, may hold values from -1 to 9, as said below
Outputs:
- averaged: float32 [16, 8, 4, 1, 64, 512], P('story', 'plan')
- coarse_part: float32 [16, 8, 4, 1, 64, 512], P('story', 'plan')
The draws below stay inside these ranges and needn't reach their ends.
Inputs may be any that keep to these rules, and one draw needn't show every extreme that they name: `off_pattern`: the two entries of a pair differ, and both sides of a face carry the same pairs; entries on sides without a face are arbitrary. `face_owner`: each face has exactly one owner among its two sharers; sides without a face hold 0. `schur_blocks`: each side's piece is symmetric positive definite. `coarse_inverse`: Symmetric.
All inputs are finite; a program needn't handle non-finite values.
Results may differ from the reference program's by a relative error of at most 0.0003.
Values sent between devices are 32-bit elements; how exact they have to be, the bound alone decides.
A program may use at most 128 MiB of HBM per device.

```python
import math
import jax
import jax.numpy as jnp
from jax import lax

BLK = 128
NBLK = 4
OFFP = 2
RHS = 64
NFACE = 1
CPD = 6
ITERS = 6
FD = 512
KC = 30
STORIES = 16
PLANS = 8
NCOARSE = 768


def face_pairs(key):
    key = jax.random.fold_in(key, 101)
    first_key, offset_key = jax.random.split(key)
    draw_shape = (STORIES, PLANS, 2, NFACE, OFFP)
    first_block = jax.random.randint(first_key, draw_shape, 0, NBLK)
    offset = jax.random.randint(offset_key, draw_shape, 1, NBLK)
    second = (first_block + offset) % NBLK
    joined = jnp.stack([first_block, second], -1)
    above_face = joined[:, :, 0]
    right_face = joined[:, :, 1]
    below_face = jnp.roll(above_face, 1, axis=0)
    left_face = jnp.roll(right_face, 1, axis=1)
    return jnp.stack([below_face, above_face, left_face, right_face], 2).astype(jnp.int32)


def draw_off_pattern(key, part):
    return face_pairs(key)


def draw_schur_blocks(key, part):
    block_pairs = face_pairs(key)
    key = jax.random.fold_in(key, 3)
    scale_key, diagonal_key, coupling_key = jax.random.split(key, 3)
    face_grid = (STORIES, PLANS, 4, NFACE)
    stiffness = jnp.exp(jax.random.uniform(scale_key, face_grid + (NBLK, BLK), jnp.float32, 0.0, math.log(10.0)))
    roots = jnp.sqrt(stiffness)
    halfwidth = 0.554 / math.sqrt(BLK * (1.0 + 2.0 * OFFP / NBLK))
    diagonal_noise = jax.random.uniform(diagonal_key, face_grid + (NBLK, BLK, BLK), jnp.float32, -halfwidth, halfwidth)
    symmetric = (diagonal_noise + jnp.swapaxes(diagonal_noise, -1, -2)) * 0.70710678
    identity = jnp.eye(BLK, dtype=jnp.float32)
    diagonal_blocks = roots[..., :, None] * (identity + symmetric) * roots[..., None, :]
    coupling = jax.random.uniform(coupling_key, face_grid + (OFFP, BLK, BLK), jnp.float32, -halfwidth, halfwidth)
    index_shape = face_grid + (OFFP, BLK)
    row_roots = jnp.take_along_axis(roots, jnp.broadcast_to(block_pairs[..., 0:1], index_shape), axis=-2)
    column_roots = jnp.take_along_axis(roots, jnp.broadcast_to(block_pairs[..., 1:2], index_shape), axis=-2)
    off_blocks = row_roots[..., :, None] * coupling * column_roots[..., None, :]
    return jnp.concatenate([diagonal_blocks, off_blocks], axis=4)


def draw_face_owner(key, part):
    key = jax.random.fold_in(key, 7)
    rank_key, coin_key = jax.random.split(key)
    ranks = jax.random.permutation(rank_key, STORIES * PLANS).reshape(STORIES, PLANS)
    coins = jax.random.randint(coin_key, (STORIES, PLANS, 2, NFACE), 0, 4)
    flips = coins == 0
    above_rank = jnp.roll(ranks, -1, axis=0)
    right_rank = jnp.roll(ranks, -1, axis=1)
    owns_above = jnp.where((ranks > above_rank)[:, :, None] != flips[:, :, 0], 1, 0)
    owns_right = jnp.where((ranks > right_rank)[:, :, None] != flips[:, :, 1], 1, 0)
    storey = jnp.arange(STORIES)[:, None, None]
    below_flag = jnp.roll(1 - owns_above, 1, axis=0) * (storey > 0)
    above_flag = owns_above * (storey < STORIES - 1)
    left_flag = jnp.roll(1 - owns_right, 1, axis=1)
    return jnp.stack([below_flag, above_flag, left_flag, owns_right], 2).astype(jnp.int32)


def draw_coarse_inverse(key, part):
    key = jax.random.fold_in(key, 9)
    noise_key, diagonal_key = jax.random.split(key)
    spread = 1.0 / math.sqrt(NCOARSE)
    coarse_noise = jax.random.uniform(noise_key, (NCOARSE, NCOARSE), jnp.float32, -spread, spread)
    symmetric = (coarse_noise + coarse_noise.T) * 0.70710678
    diagonal = jnp.exp(jax.random.uniform(diagonal_key, (NCOARSE,), jnp.float32, 0.0, math.log(4.0)))
    return symmetric + jnp.diag(diagonal)


def levels(key, dims, shards, low, top_value):
    gain, own = 1.0, jax.random.fold_in(key, 6)
    for axis_at, blocks in shards:
        draws = jnp.exp(jax.random.uniform(jax.random.fold_in(own, axis_at), (blocks,), jnp.float32, low / len(shards), top_value / len(shards)))
        gain = gain * jnp.repeat(draws, dims[axis_at] // blocks).reshape([-1 if axis == axis_at else 1 for axis in range(len(dims))])
    return gain


def centred(rng, shape, scale, bound, shards=(), kind=jnp.bfloat16):
    level = levels(rng, shape, shards, -0.22, 0.18) if shards else 1.0
    entries = jax.random.normal(rng, shape, jnp.float32) * scale * level
    return jnp.minimum(jnp.maximum(entries, -bound), bound).astype(kind)


def setup_inputs(seed: int = 0) -> dict:
    arg_keys = jax.random.split(jax.random.key(seed), 7)
    schur_blocks = draw_schur_blocks(jax.random.fold_in(arg_keys[6], 71), 0)
    off_pattern = draw_off_pattern(jax.random.fold_in(arg_keys[6], 71), 0)
    face_owner = draw_face_owner(jax.random.fold_in(arg_keys[6], 71), 0)
    residual = centred(arg_keys[3], (STORIES, PLANS, 4, NFACE, RHS, FD), 1.0, 6.0, ((0, 16), (1, 8)), jnp.float32)
    coarse_basis = centred(arg_keys[4], (STORIES, PLANS, 4, NFACE, KC, FD), 0.04, 0.25, ((0, 16), (1, 8)), jnp.float32)
    coarse_inverse = draw_coarse_inverse(jax.random.fold_in(arg_keys[6], 71), 0)
    return dict(schur_blocks=schur_blocks, off_pattern=off_pattern, face_owner=face_owner, residual=residual, coarse_basis=coarse_basis, coarse_inverse=coarse_inverse)


DAMPING = 0.3
PRECISE = lax.Precision.HIGHEST


def one_hot(indices, width):
    return (indices[..., None] == jnp.arange(width, dtype=jnp.int32)).astype(jnp.float32)


def apply_side(blocks, select_row, select_column, vector):
    block_count = select_row.shape[-1]
    block_size = blocks.shape[-1]
    split_rows = vector.reshape(vector.shape[:-1] + (block_count, block_size))
    diagonal_blocks = blocks[..., :block_count, :, :]
    off_blocks = blocks[..., block_count:, :, :]
    result = jnp.einsum('...rnb,...nbc->...rnc', split_rows, diagonal_blocks, precision=PRECISE)
    column_parts = jnp.einsum('...kn,...rnb->...krb', select_column, split_rows, precision=PRECISE)
    row_parts = jnp.einsum('...kn,...rnb->...krb', select_row, split_rows, precision=PRECISE)
    into_rows = jnp.einsum('...krb,...kab->...kra', column_parts, off_blocks, precision=PRECISE)
    into_columns = jnp.einsum('...krb,...kba->...kra', row_parts, off_blocks, precision=PRECISE)
    result = result + jnp.einsum('...kn,...kra->...rna', select_row, into_rows, precision=PRECISE)
    result = result + jnp.einsum('...kn,...kra->...rna', select_column, into_columns, precision=PRECISE)
    return result.reshape(vector.shape)


def deluxe(first_blocks, first_rows, second_blocks, second_rows, block_pairs):
    block_count = first_blocks.shape[-3] - block_pairs.shape[-2]
    select_row = one_hot(block_pairs[..., 0], block_count)
    select_column = one_hot(block_pairs[..., 1], block_count)

    def apply_both(vector):
        return apply_side(first_blocks, select_row, select_column, vector) + apply_side(second_blocks, select_row, select_column, vector)

    right_side = apply_side(first_blocks, select_row, select_column, first_rows) + apply_side(second_blocks, select_row, select_column, second_rows)
    first_diagonal = jnp.diagonal(first_blocks[..., :block_count, :, :], axis1=-2, axis2=-1)
    second_diagonal = jnp.diagonal(second_blocks[..., :block_count, :, :], axis1=-2, axis2=-1)
    step_scale = (DAMPING / (first_diagonal + second_diagonal)).reshape(first_rows.shape[:-2] + (1, first_rows.shape[-1]))
    iterate = right_side * step_scale
    for iteration in range(ITERS - 1):
        iterate = iterate + (right_side - apply_both(iterate)) * step_scale
    return iterate


def solve_row(operands):
    first_blocks, first_rows, second_blocks, second_rows, block_pairs = operands
    return deluxe(first_blocks, first_rows, second_blocks, second_rows, block_pairs)


def reference(schur_blocks, off_pattern, face_owner, residual, coarse_basis, coarse_inverse):
    vertical = lax.map(solve_row, (schur_blocks[:-1, :, 1], residual[:-1, :, 1], schur_blocks[1:, :, 0], residual[1:, :, 0], off_pattern[:-1, :, 1]))
    across = lax.map(solve_row, (schur_blocks[:, :, 3], residual[:, :, 3], jnp.roll(schur_blocks[:, :, 2], -1, axis=1), jnp.roll(residual[:, :, 2], -1, axis=1), off_pattern[:, :, 3]))
    empty_faces = jnp.zeros_like(vertical[:1])
    below_side = jnp.concatenate([empty_faces, vertical], axis=0)
    above_side = jnp.concatenate([vertical, empty_faces], axis=0)
    left_side = jnp.roll(across, 1, axis=1)
    averaged = jnp.stack([below_side, above_side, left_side, across], axis=2)
    owner_mask = face_owner.astype(jnp.float32)
    contribution = jnp.einsum('ijspkf,ijsprf->ijrk', coarse_basis * owner_mask[..., None, None], averaged, precision=PRECISE)
    groups = contribution.reshape(STORIES, PLANS, RHS, 5, CPD)
    zero_row = jnp.zeros_like(groups[:1, :, :, 0])
    coarse_sum = groups[:, :, :, 0]
    coarse_sum = coarse_sum + jnp.concatenate([zero_row, groups[:-1, :, :, 2]], axis=0)
    coarse_sum = coarse_sum + jnp.concatenate([groups[1:, :, :, 1], zero_row], axis=0)
    coarse_sum = coarse_sum + jnp.roll(groups[:, :, :, 4], 1, axis=1)
    coarse_sum = coarse_sum + jnp.roll(groups[:, :, :, 3], -1, axis=1)
    coarse_vector = coarse_sum.transpose(2, 0, 1, 3).reshape(RHS, NCOARSE)
    coarse_values = jnp.dot(coarse_vector, coarse_inverse, precision=PRECISE, preferred_element_type=jnp.float32)
    coarse_field = coarse_values.reshape(RHS, STORIES, PLANS, CPD).transpose(1, 2, 0, 3)
    zero_field = jnp.zeros_like(coarse_field[:1])
    needed = jnp.concatenate([coarse_field, jnp.concatenate([zero_field, coarse_field[:-1]], axis=0), jnp.concatenate([coarse_field[1:], zero_field], axis=0), jnp.roll(coarse_field, 1, axis=1), jnp.roll(coarse_field, -1, axis=1)], axis=-1)
    storey = jnp.arange(STORIES)[:, None]
    side_ids = jnp.arange(4)[None, :]
    present = jnp.where(side_ids == 0, storey > 0, jnp.where(side_ids == 1, storey < STORIES - 1, True)).astype(jnp.float32)
    coarse_part = jnp.einsum('ijrk,ijspkf->ijsprf', needed, coarse_basis, precision=PRECISE) * present[:, None, :, None, None, None]
    return averaged, coarse_part
```

```python
import jax
import jax.numpy as jnp
from jax import lax
from jax.experimental import pallas as pl
from jax.experimental.pallas import tpu as pltpu
from jax.sharding import PartitionSpec as P

ITERS = 6
DAMPING = 0.3
BLK = 128
NBLK = 4
RHS = 64
FD = 512
CPD = 6
KC = 30
STORIES = 16
PLANS = 8
ROW = PLANS * CPD
NCOARSE = STORIES * ROW
MESH = pl.DeviceIdType.MESH
F32 = jnp.float32
BF16 = jnp.bfloat16


def iota(shape, dim):
    return lax.broadcasted_iota(jnp.int32, shape, dim)


def split(value):
    high = value.astype(BF16)
    return high, (value - high.astype(F32)).astype(BF16)


def dot(left, right):
    return jnp.dot(left, right, preferred_element_type=F32)


def dot_first(left, right):
    return lax.dot_general(left, right, (((0,), (0,)), ((), ())), preferred_element_type=F32)


def product(value, high, low):
    rows = value.shape[0]
    first, second = split(value)
    both = dot(jnp.concatenate([first, second], axis=0), high)
    return both[:rows] + both[rows:] + dot(first, low)


def fill(table, first, second):
    zero = jnp.zeros_like(first)
    for a, left in enumerate((zero, first, first.T)):
        for b, right in enumerate((zero, second, second.T)):
            table[3 * a + b] = left + right


def choice(pattern, side, q, t):
    index = 0
    for k in range(2):
        row, column = pattern[side, k, 0], pattern[side, k, 1]
        plain = jnp.where((row == q) & (column == t), 1, 0)
        turned = jnp.where((row == t) & (column == q), 2, 0)
        index = 3 * index + plain + turned
    return index


def place(pattern, side, table, diagonal, scales, high, low):
    for q in range(NBLK):
        for t in range(NBLK):
            if q == t:
                block = diagonal[q]
            else:
                block = table[choice(pattern, side, q, t)]
                if scales is not None:
                    block = block * scales[t]
            here = (pl.ds(q * BLK, BLK), pl.ds(t * BLK, BLK))
            high[here], low[here] = split(block)


def scatter(plan, shift):
    shape = (32, 256)
    dof, lane = iota(shape, 0), iota(shape, 1)
    group = (dof * 43) >> 8
    member = dof - CPD * group
    storey = jnp.where(group == 1, 1, jnp.where(group == 2, 3, 2)) + shift
    column = (plan + jnp.where(group == 4, 1, 0) + jnp.where(group == 3, PLANS - 1, 0)) & (PLANS - 1)
    target = storey * ROW + column * CPD + member
    return jnp.where((lane == target) & (dof < KC), 1.0, 0.0).astype(BF16)


def gather(story):
    shape = (3 * ROW, 256)
    row, lane = iota(shape, 0), iota(shape, 1)
    plan, dof = lane >> 5, lane & 31
    group = (dof * 43) >> 8
    member = dof - CPD * group
    storey = jnp.where(group == 1, 0, jnp.where(group == 2, 2, 1))
    column = (plan + jnp.where(group == 4, 1, 0) + jnp.where(group == 3, PLANS - 1, 0)) & (PLANS - 1)
    target = storey * ROW + column * CPD + member
    at = story + storey - 1
    kept = (dof < KC) & (at >= 0) & (at < STORIES)
    return jnp.where((row == target) & kept, 1.0, 0.0).astype(BF16)


def kernel(
    schur, pattern, owner, residual, basis, inverse,
    averaged, coarse_part,
    raw, rows, local, slab, table, high, low, ready_high, ready_low,
    pack_out, pack_in, coupling_in, product_out, product_in, product_own, basis_in,
    wide, solved, spread_high, spread_low, weight_high, weight_low, basis_pack,
    sent_first, got_first, sent_second, got_second, sent_third, got_third, result,
    load_sem, face_send, face_recv, back_send, back_recv, store_sem,
    send_first, recv_first, send_second, recv_second, send_third, recv_third,
):
    story, plan = lax.axis_index("story"), lax.axis_index("plan")
    odd = lax.rem(plan, 2)
    step = 1 - 2 * odd
    in_side = (1 - odd, 3)
    out_side = (odd, 2)
    sides = (out_side[0], out_side[1], in_side[0], in_side[1])
    in_device = ((lax.rem(story + step + STORIES, STORIES), plan), (story, lax.rem(plan + 1, PLANS)))
    out_device = (
        (lax.rem(story - step + STORIES, STORIES), plan),
        (story, lax.rem(plan + PLANS - 1, PLANS)),
    )
    plan_peers = [(story, lax.rem(plan + r, PLANS)) for r in range(1, PLANS)]
    story_peers = [(lax.rem(story + r, STORIES), plan) for r in range(1, STORIES)]

    barrier = pltpu.get_barrier_semaphore()
    for peer in plan_peers + story_peers:
        pl.semaphore_signal(barrier, inc=1, device_id=peer, device_id_type=MESH)

    loads = []
    for k in range(4):
        loads.append(pltpu.make_async_copy(schur.at[sides[k]], raw.at[k], load_sem.at[k]))
        loads.append(pltpu.make_async_copy(residual.at[sides[k]], rows.at[k], load_sem.at[4 + k]))
    loads.append(pltpu.make_async_copy(basis, local, load_sem.at[8]))
    for o in range(3):
        at = jnp.clip(story + o - 1, 0, STORIES - 1) * ROW
        loads.append(
            pltpu.make_async_copy(
                inverse.at[pl.ds(pl.multiple_of(at, 8), ROW)],
                slab.at[pl.ds(o * ROW, ROW)],
                load_sem.at[9 + o],
            )
        )
    for load in loads:
        load.start()

    line, lane = iota((BLK, BLK), 0), iota((BLK, BLK), 1)
    upper, equal = line <= lane, line == lane

    def diagonal_of(block):
        return jnp.sum(jnp.where(equal, block, 0.0), axis=0, keepdims=True)

    for f in range(2):
        loads[2 * f].wait()
        for h in range(2):
            first, second = raw[f, 2 * h], raw[f, 2 * h + 1]
            pack_out[f, h * BLK : (h + 1) * BLK] = jnp.where(upper, first, second)
            pack_out[f, 2 * BLK + h : 2 * BLK + h + 1] = diagonal_of(second)
        pack_out[f, 2 * BLK + 2 : 2 * BLK + 8] = jnp.zeros((6, BLK), F32)

    def to_sharer(f, m, source, target):
        return pltpu.make_async_remote_copy(
            src_ref=source, dst_ref=target, send_sem=face_send.at[f, m], recv_sem=face_recv.at[f, m],
            device_id=out_device[f], device_id_type=MESH,
        )

    pl.semaphore_wait(barrier, PLANS - 1 + STORIES - 1)
    packs = [to_sharer(f, 0, pack_out.at[f], pack_in.at[f]) for f in range(2)]
    couplings = [to_sharer(f, 1, raw.at[f, pl.ds(NBLK, 2)], coupling_in.at[f]) for f in range(2)]
    products = [to_sharer(f, 2, product_out.at[f], product_in.at[f]) for f in range(2)]
    bases = [to_sharer(f, 3, basis.at[out_side[f]], basis_in.at[f]) for f in range(2)]
    for f in range(2):
        packs[f].start()
        couplings[f].start()

    for k in range(4):
        if k >= 2:
            loads[2 * k].wait()
        loads[2 * k + 1].wait()
        fill(table, raw[k, NBLK], raw[k, NBLK + 1])
        place(pattern, sides[k], table, [raw[k, n] for n in range(NBLK)], None, high, low)
        target = product_out.at[k] if k < 2 else product_own.at[k - 2]
        target[...] = product(rows[k], high[...], low[...])
        if k < 2:
            products[k].start()
    for f in range(2):
        bases[f].start()

    loads[8].wait()
    for o in range(3):
        loads[9 + o].wait()
    columns = gather(story)
    slab_high, slab_low = split(slab[...])
    weight_high[...] = dot_first(slab_high, columns).astype(BF16)
    weight_low[...] = dot_first(slab_low, columns).astype(BF16)
    exists = jnp.where(odd == 0, story < STORIES - 1, story > 0)
    wide[...] = jnp.zeros_like(wide)
    for s in range(4):
        wide[s, 0:KC] = local[s]
    present = (jnp.where(story > 0, 1.0, 0.0), jnp.where(story < STORIES - 1, 1.0, 0.0), 1.0, 1.0)
    for s in range(4):
        basis_high, basis_low = split(wide[s] * present[s])
        here = pl.ds(s * FD, FD)
        basis_pack[:, here] = jnp.concatenate(
            [basis_high, basis_high, basis_low, jnp.zeros_like(basis_low)], axis=0
        )

    scaled = []
    for f in range(2):
        packs[f].wait_recv()
        couplings[f].wait_recv()
        diagonal, scales = [], []
        for h in range(2):
            first, second = raw[2 + f, 2 * h], raw[2 + f, 2 * h + 1]
            packed = jnp.where(upper, first, second) + pack_in[f, h * BLK : (h + 1) * BLK]
            turned = packed.T
            second_diagonal = diagonal_of(second) + pack_in[f, 2 * BLK + h : 2 * BLK + h + 1]
            scales += [-DAMPING / diagonal_of(packed), -DAMPING / second_diagonal]
            diagonal.append(
                jnp.where(equal, 1.0 - DAMPING, jnp.where(upper, packed, turned) * scales[-2])
            )
            diagonal.append(
                jnp.where(equal, 1.0 - DAMPING, jnp.where(upper, turned, packed) * scales[-1])
            )
        fill(
            table,
            raw[2 + f, NBLK] + coupling_in[f, 0],
            raw[2 + f, NBLK + 1] + coupling_in[f, 1],
        )
        place(pattern, in_side[f], table, diagonal, scales, ready_high.at[f], ready_low.at[f])
        scaled.append(jnp.concatenate(scales, axis=1))

    starts = []
    for f in range(2):
        products[f].wait_recv()
        product_own[f] = -(product_own[f] + product_in[f]) * scaled[f]
        solved[f] = product_own[f]

    def sweep(_, carry):
        for f in range(2):
            solved[f] = product_own[f] + product(solved[f], ready_high[f], ready_low[f])
        return carry

    lax.fori_loop(0, ITERS - 1, sweep, 0)
    solved[0] = jnp.where(exists, solved[0], 0.0)

    def to_owner(f):
        return pltpu.make_async_remote_copy(
            src_ref=solved.at[f], dst_ref=averaged.at[out_side[f]],
            send_sem=back_send.at[f], recv_sem=back_recv.at[f],
            device_id=in_device[f], device_id_type=MESH,
        )

    backs = [to_owner(f) for f in range(2)]
    keeps = [
        pltpu.make_async_copy(solved.at[f], averaged.at[in_side[f]], store_sem.at[f]) for f in range(2)
    ]
    for f in range(2):
        backs[f].start()
        keeps[f].start()

    own_places = scatter(plan, 0)
    other_places = (scatter(plan, step), scatter(plan + 1, 0))
    for f in range(2):
        bases[f].wait_recv()
        wide[4 + f, 0:KC] = basis_in[f]
        mine = owner[in_side[f], 0].astype(F32)
        both = jnp.concatenate([wide[in_side[f]] * mine, wide[4 + f] * (1.0 - mine)], axis=0)
        places = jnp.concatenate([own_places, other_places[f]], axis=0)
        both_high, both_low = split(both)
        here = pl.ds(f * FD, FD)
        spread_high[here] = dot_first(both_high, places).astype(BF16)
        spread_low[here] = dot_first(both_low, places).astype(BF16)
    values = jnp.concatenate([solved[0], solved[1]], axis=1)
    contribution = product(values, spread_high[...], spread_low[...])
    sent_first[...] = contribution.reshape(PLANS, RHS // PLANS, 256)

    def exchange(peers, source, target, send_sem, recv_sem):
        copies = []
        for r, peer in enumerate(peers):
            copies.append(
                pltpu.make_async_remote_copy(
                    src_ref=source(peer), dst_ref=target, send_sem=send_sem.at[r],
                    recv_sem=recv_sem.at[r], device_id=peer, device_id_type=MESH,
                )
            )
            copies[-1].start()
        return copies

    firsts = exchange(
        plan_peers, lambda peer: sent_first.at[peer[1]], got_first.at[plan], send_first, recv_first
    )
    got_first[plan] = sent_first[plan]
    for copy in firsts:
        copy.wait_recv()
    total = got_first[0]
    for p in range(1, PLANS):
        total = total + got_first[p]
    sent_second[...] = total
    seconds = exchange(
        story_peers, lambda peer: sent_second, got_second.at[story], send_second, recv_second
    )
    got_second[story] = total
    for copy in seconds:
        copy.wait_recv()
    tile_lane = iota((8, BLK), 1)
    tiles = [jnp.zeros((8, BLK), F32) for _ in range(NCOARSE // BLK)]
    for i in range(STORIES):
        left, right = got_second[i, :, :BLK], got_second[i, :, BLK:]
        first, shift = divmod((i - 2) * ROW, BLK)
        parts = [left, right]
        if shift:
            left, right = pltpu.roll(left, shift, 1), pltpu.roll(right, shift, 1)
            inside = tile_lane >= shift
            parts = [
                jnp.where(inside, left, 0.0), jnp.where(inside, right, left), jnp.where(inside, 0.0, right)
            ]
        for n, part in enumerate(parts):
            if 0 <= first + n < len(tiles):
                tiles[first + n] = tiles[first + n] + part
    vector = jnp.concatenate(tiles, axis=1)
    vector_high, vector_low = split(vector)
    coarse = (
        dot(vector_high, weight_high[...]) + dot(vector_low, weight_high[...])
        + dot(vector_high, weight_low[...])
    )
    for p in range(PLANS):
        half = coarse[:, (p // 4) * BLK : (p // 4 + 1) * BLK]
        turn = (BLK - 32 * (p % 4)) % BLK
        sent_third[p] = pltpu.roll(half, turn, 1) if turn else half
    thirds = exchange(
        plan_peers, lambda peer: sent_third.at[peer[1]], got_third.at[plan], send_third, recv_third
    )
    got_third[plan] = sent_third[plan]
    for copy in thirds:
        copy.wait_recv()
    needed = got_third[...].reshape(RHS, BLK)
    needed = jnp.where(iota((RHS, BLK), 1) < KC, needed, 0.0)
    needed_high, needed_low = split(needed)
    needed_high, needed_low = needed_high.astype(F32), needed_low.astype(F32)
    operand = needed_high + pltpu.roll(needed_low, 32, 1) + pltpu.roll(needed_high, 64, 1)
    operand = operand.astype(BF16)
    stores = []
    for s in range(4):
        result[s] = dot(operand, basis_pack[:, s * FD : (s + 1) * FD])
        stores.append(pltpu.make_async_copy(result.at[s], coarse_part.at[s], store_sem.at[2 + s]))
        stores[-1].start()

    for copy in packs + couplings + products + bases + firsts + seconds + thirds:
        copy.wait_send()
    for copy in backs:
        copy.wait()
    for copy in keeps + stores:
        copy.wait()


def on_device(schur_blocks, off_pattern, face_owner, residual, coarse_basis, coarse_inverse):
    hbm = pl.BlockSpec(memory_space=pl.ANY)
    smem = pl.BlockSpec(memory_space=pltpu.SMEM)
    dma = pltpu.SemaphoreType.DMA
    out = jax.ShapeDtypeStruct((4, RHS, FD), F32)
    averaged, coarse_part = pl.pallas_call(
        kernel,
        out_shape=(out, out),
        in_specs=[hbm, smem, smem, hbm, hbm, hbm],
        out_specs=(hbm, hbm),
        scratch_shapes=[
            pltpu.VMEM((4, 6, BLK, BLK), F32),
            pltpu.VMEM((4, RHS, FD), F32),
            pltpu.VMEM((4, KC, FD), F32),
            pltpu.VMEM((3 * ROW, NCOARSE), F32),
            pltpu.VMEM((9, BLK, BLK), F32),
            pltpu.VMEM((FD, FD), BF16),
            pltpu.VMEM((FD, FD), BF16),
            pltpu.VMEM((2, FD, FD), BF16),
            pltpu.VMEM((2, FD, FD), BF16),
            pltpu.VMEM((2, 2 * BLK + 8, BLK), F32),
            pltpu.VMEM((2, 2 * BLK + 8, BLK), F32),
            pltpu.VMEM((2, 2, BLK, BLK), F32),
            pltpu.VMEM((2, RHS, FD), F32),
            pltpu.VMEM((2, RHS, FD), F32),
            pltpu.VMEM((2, RHS, FD), F32),
            pltpu.VMEM((2, KC, FD), F32),
            pltpu.VMEM((6, 32, FD), F32),
            pltpu.VMEM((2, RHS, FD), F32),
            pltpu.VMEM((2 * FD, 256), BF16),
            pltpu.VMEM((2 * FD, 256), BF16),
            pltpu.VMEM((NCOARSE, 256), BF16),
            pltpu.VMEM((NCOARSE, 256), BF16),
            pltpu.VMEM((BLK, 4 * FD), BF16),
            pltpu.VMEM((PLANS, 8, 256), F32),
            pltpu.VMEM((PLANS, 8, 256), F32),
            pltpu.VMEM((8, 256), F32),
            pltpu.VMEM((STORIES, 8, 256), F32),
            pltpu.VMEM((PLANS, 8, BLK), F32),
            pltpu.VMEM((PLANS, 8, BLK), F32),
            pltpu.VMEM((4, RHS, FD), F32),
            dma((12,)),
            dma((2, 4)),
            dma((2, 4)),
            dma((2,)),
            dma((2,)),
            dma((6,)),
            dma((PLANS - 1,)),
            dma((PLANS - 1,)),
            dma((STORIES - 1,)),
            dma((STORIES - 1,)),
            dma((PLANS - 1,)),
            dma((PLANS - 1,)),
        ],
        compiler_params=pltpu.CompilerParams(
            collective_id=0, has_side_effects=True, vmem_limit_bytes=40 * 1024 * 1024
        ),
    )(
        schur_blocks.reshape(4, 6, BLK, BLK),
        off_pattern.reshape(4, 2, 2),
        face_owner.reshape(4, 1),
        residual.reshape(4, RHS, FD),
        coarse_basis.reshape(4, KC, FD),
        coarse_inverse,
    )
    shape = (1, 1, 4, 1, RHS, FD)
    return averaged.reshape(shape), coarse_part.reshape(shape)


def solution(mesh):
    in_specs = (
        P("story", "plan", None, None, None, None, None),
        P("story", "plan", None, None, None, None),
        P("story", "plan", None, None),
        P("story", "plan", None, None, None, None),
        P("story", "plan", None, None, None, None),
        P(),
    )
    out_specs = (
        P("story", "plan", None, None, None, None),
        P("story", "plan", None, None, None, None),
    )
    return jax.shard_map(
        on_device, mesh=mesh, in_specs=in_specs, out_specs=out_specs, check_vma=False
    )
```

```python
import jax
import jax.numpy as jnp
from jax import lax
from jax.experimental import pallas as pl
from jax.experimental.pallas import tpu as pltpu
from jax.sharding import PartitionSpec as P

ITERS = 6
DAMPING = 0.3
BLK = 128
NBLK = 4
RHS = 64
FD = 512
CPD = 6
KC = 30
STORIES = 16
PLANS = 8
ROW = PLANS * CPD
NCOARSE = STORIES * ROW
MESH = pl.DeviceIdType.MESH
F32 = jnp.float32
BF16 = jnp.bfloat16


def iota(shape, dim):
    return lax.broadcasted_iota(jnp.int32, shape, dim)


def split(value):
    high = value.astype(BF16)
    return high, (value - high.astype(F32)).astype(BF16)


def dot(left, right):
    return jnp.dot(left, right, preferred_element_type=F32)


def dot_last(left, right):
    return lax.dot_general(left, right, (((1,), (1,)), ((), ())), preferred_element_type=F32)


def product(value, high, low, dot=dot):
    rows = value.shape[0]
    first, second = split(value)
    both = dot(jnp.concatenate([first, second], axis=0), high)
    return both[:rows] + both[rows:] + dot(first, low)


def fill(table, first, second):
    zero = jnp.zeros_like(first)
    for a, left in enumerate((zero, first, first.T)):
        for b, right in enumerate((zero, second, second.T)):
            table[3 * a + b] = left + right


def choice(pattern, side, q, t):
    index = 0
    for k in range(2):
        row, column = pattern[k, 0, side], pattern[k, 1, side]
        plain = jnp.where((row == q) & (column == t), 1, 0)
        turned = jnp.where((row == t) & (column == q), 2, 0)
        index = 3 * index + plain + turned
    return index


def place(pattern, side, table, diagonal, scales, high, low):
    for q in range(NBLK):
        for t in range(NBLK):
            if q == t:
                block = diagonal[q]
            else:
                block = table[choice(pattern, side, q, t)]
                if scales is not None:
                    block = block * scales[t]
            here = (pl.ds(q * BLK, BLK), pl.ds(t * BLK, BLK))
            high[here], low[here] = split(block)


def places(dof):
    group = (dof * 43) >> 8
    storey = jnp.where(group == 1, -1, jnp.where(group == 2, 1, 0))
    column = jnp.where(group == 4, 1, jnp.where(group == 3, PLANS - 1, 0))
    return storey, column, dof - CPD * group


def scatter(plan, shift):
    dof, lane = iota((32, 256), 0), iota((32, 256), 1)
    storey, column, member = places(dof)
    target = (storey + shift + 2) * ROW + ((plan + column) & (PLANS - 1)) * CPD + member
    return jnp.where((lane == target) & (dof < KC), 1.0, 0.0)


def gather(plan):
    lane = iota((1, STORIES * 32), 1)
    dof = lane & 31
    storey, column, member = places(dof)
    storey = storey + (lane >> 5)
    target = storey * ROW + ((plan + column) & (PLANS - 1)) * CPD + member
    target = jnp.where((dof < KC) & (storey >= 0) & (storey < STORIES), target, -1)
    return jnp.where(iota((NCOARSE, STORIES * 32), 0) == target, 1.0, 0.0).astype(BF16)


def kernel(
    schur, pattern_far, owner_far, residual, basis, inverse,
    averaged, coarse_part,
    pattern, owner, raw, rows, local, slab, table, high, low, ready_high, ready_low,
    pack_out, pack_in, coupling_in, product_out, product_in, product_own, basis_in,
    wide, solved, owned_high, owned_low, weight_high, weight_low, basis_pack, flag, flags,
    sent_first, got_first, sent_second, got_second, result,
    load_sem, face_send, face_recv, back_send, back_recv, store_sem,
    send_flag, recv_flag, send_first, recv_first, send_second, recv_second,
):
    story, plan = lax.axis_index("story"), lax.axis_index("plan")
    odd = lax.rem(plan, 2)
    step = 1 - 2 * odd
    in_side = (1 - odd, 3)
    out_side = (odd, 2)
    sides = (out_side[0], out_side[1], in_side[0], in_side[1])
    in_device = ((lax.rem(story + step + STORIES, STORIES), plan), (story, lax.rem(plan + 1, PLANS)))
    out_device = (
        (lax.rem(story - step + STORIES, STORIES), plan),
        (story, lax.rem(plan + PLANS - 1, PLANS)),
    )
    plan_peers = [(story, lax.rem(plan + r, PLANS)) for r in range(1, PLANS)]
    story_peers = [(lax.rem(story + r, STORIES), plan) for r in range(1, STORIES)]

    barrier = pltpu.get_barrier_semaphore()
    for peer in plan_peers + story_peers:
        pl.semaphore_signal(barrier, inc=1, device_id=peer, device_id_type=MESH)

    small = (
        pltpu.make_async_copy(pattern_far, pattern, load_sem.at[14]),
        pltpu.make_async_copy(owner_far, owner, load_sem.at[15]),
    )
    loads = []
    for k in range(4):
        loads.append(pltpu.make_async_copy(schur.at[sides[k]], raw.at[k], load_sem.at[k]))
        loads.append(pltpu.make_async_copy(residual.at[sides[k]], rows.at[k], load_sem.at[4 + k]))
    loads.append(pltpu.make_async_copy(basis, local, load_sem.at[8]))
    for o in range(5):
        at = jnp.clip(story + o - 2, 0, STORIES - 1) * ROW
        loads.append(
            pltpu.make_async_copy(
                inverse.at[pl.ds(pl.multiple_of(at, 8), ROW)],
                slab.at[pl.ds(o * ROW, ROW)],
                load_sem.at[9 + o],
            )
        )
    for load in loads[:4] + list(small) + loads[4:]:
        load.start()

    line, lane = iota((BLK, BLK), 0), iota((BLK, BLK), 1)
    upper, equal = line <= lane, line == lane

    def diagonal_of(block):
        return jnp.sum(jnp.where(equal, block, 0.0), axis=0, keepdims=True)

    def to_sharer(f, m, source, target):
        return pltpu.make_async_remote_copy(
            src_ref=source, dst_ref=target, send_sem=face_send.at[f, m], recv_sem=face_recv.at[f, m],
            device_id=out_device[f], device_id_type=MESH,
        )

    def exchange(peers, source, target, send_sem, recv_sem):
        copies = []
        for r, peer in enumerate(peers):
            copies.append(
                pltpu.make_async_remote_copy(
                    src_ref=source(peer), dst_ref=target, send_sem=send_sem.at[r],
                    recv_sem=recv_sem.at[r], device_id=peer, device_id_type=MESH,
                )
            )
            copies[-1].start()
        return copies

    for copy in small:
        copy.wait()
    mine = [owner[0, in_side[f]].astype(F32) for f in range(2)]
    for f in range(2):
        flag[f : f + 1] = jnp.full((1, BLK), mine[f], F32)
    flag[2:8] = jnp.zeros((6, BLK), F32)
    flags[plan] = flag[...]

    pl.semaphore_wait(barrier, PLANS - 1 + STORIES - 1)
    couplings = [
        to_sharer(f, 1, schur.at[out_side[f], pl.ds(NBLK, 2)], coupling_in.at[f]) for f in range(2)
    ]
    packs = [to_sharer(f, 0, pack_out.at[f], pack_in.at[f]) for f in range(2)]
    products = [to_sharer(f, 2, product_out.at[f], product_in.at[f]) for f in range(2)]
    bases = [to_sharer(f, 3, basis.at[out_side[f]], basis_in.at[f]) for f in range(2)]
    for f in range(2):
        couplings[f].start()

    for f in range(2):
        loads[2 * f].wait()
        for h in range(2):
            first, second = raw[f, 2 * h], raw[f, 2 * h + 1]
            pack_out[f, h * BLK : (h + 1) * BLK] = jnp.where(upper, first, second)
            pack_out[f, 2 * BLK + h : 2 * BLK + h + 1] = diagonal_of(second)
        pack_out[f, 2 * BLK + 2 : 2 * BLK + 8] = jnp.zeros((6, BLK), F32)
        packs[f].start()
    noted = exchange(plan_peers, lambda peer: flag, flags.at[plan], send_flag, recv_flag)

    for k in range(4):
        if k >= 2:
            loads[2 * k].wait()
        loads[2 * k + 1].wait()
        fill(table, raw[k, NBLK], raw[k, NBLK + 1])
        place(pattern, sides[k], table, [raw[k, n] for n in range(NBLK)], None, high, low)
        target = product_out.at[k] if k < 2 else product_own.at[k - 2]
        target[...] = product(rows[k], high[...], low[...])
        if k < 2:
            products[k].start()
    for f in range(2):
        bases[f].start()

    exists = jnp.where(odd == 0, story < STORIES - 1, story > 0)
    present = (jnp.where(story > 0, 1.0, 0.0), jnp.where(story < STORIES - 1, 1.0, 0.0), 1.0, 1.0)
    loads[8].wait()
    wide[...] = jnp.zeros_like(wide)

    def widen(source, s, target):
        for n in range(NBLK):
            wide[target, 0:KC, n * BLK : (n + 1) * BLK] = source[s, pl.ds(n, KC, stride=NBLK)]

    for s in range(4):
        widen(local, s, s)
        basis_high, basis_low = split(wide[s] * present[s])
        here = pl.ds(s * FD, FD)
        basis_pack[:, here] = jnp.concatenate(
            [basis_high, basis_high, basis_low, jnp.zeros_like(basis_low)], axis=0
        )

    pieces = []
    for o in range(5):
        loads[9 + o].wait()
        at = story + o - 2
        pieces.append(jnp.where((at >= 0) & (at < STORIES), slab[o * ROW : (o + 1) * ROW], 0.0))
    pieces.append(jnp.zeros((16, NCOARSE), F32))
    slab_high, slab_low = split(jnp.concatenate(pieces, axis=0))
    columns = dot(jnp.concatenate([slab_high, slab_low], axis=0), gather(plan)).astype(BF16)
    for copy in noted:
        copy.wait_recv()
    chosen = []
    for p in range(PLANS):
        for f in range(2):
            kept = jnp.concatenate([flags[p, f : f + 1]] * 2, axis=1)
            other = scatter(p, 1 - 2 * (p % 2)) if f == 0 else scatter(p + 1, 0)
            chosen.append((scatter(p, 0) * kept + other * (1.0 - kept)).astype(BF16))
    chosen = jnp.concatenate(chosen, axis=0)
    weight_high[...] = dot(chosen, columns[:256]).astype(BF16)
    weight_low[...] = dot(chosen, columns[256:]).astype(BF16)

    scaled = []
    for f in range(2):
        packs[f].wait_recv()
        couplings[f].wait_recv()
        diagonal, scales = [], []
        for h in range(2):
            first, second = raw[2 + f, 2 * h], raw[2 + f, 2 * h + 1]
            packed = jnp.where(upper, first, second) + pack_in[f, h * BLK : (h + 1) * BLK]
            turned = packed.T
            second_diagonal = diagonal_of(second) + pack_in[f, 2 * BLK + h : 2 * BLK + h + 1]
            scales += [-DAMPING / diagonal_of(packed), -DAMPING / second_diagonal]
            diagonal.append(
                jnp.where(equal, 1.0 - DAMPING, jnp.where(upper, packed, turned) * scales[-2])
            )
            diagonal.append(
                jnp.where(equal, 1.0 - DAMPING, jnp.where(upper, turned, packed) * scales[-1])
            )
        fill(
            table,
            raw[2 + f, NBLK] + coupling_in[f, 0],
            raw[2 + f, NBLK + 1] + coupling_in[f, 1],
        )
        place(pattern, in_side[f], table, diagonal, scales, ready_high.at[f], ready_low.at[f])
        scaled.append(jnp.concatenate(scales, axis=1))

    for f in range(2):
        products[f].wait_recv()
        product_own[f] = -(product_own[f] + product_in[f]) * scaled[f]
        solved[f] = product_own[f]

    def sweep(_, carry):
        for f in range(2):
            solved[f] = product_own[f] + product(solved[f], ready_high[f], ready_low[f])
        return carry

    lax.fori_loop(0, ITERS - 2, sweep, 0)
    owned_high[...] = jnp.zeros_like(owned_high)
    owned_low[...] = jnp.zeros_like(owned_low)
    for f in range(2):
        bases[f].wait_recv()
        widen(basis_in, f, 4 + f)
        basis_high, basis_low = split(wide[in_side[f]] * mine[f] + wide[4 + f] * (1.0 - mine[f]))
        for n in range(2):
            here = (pl.ds(64 * n + 32 * f, 32), pl.ds(f * FD, FD))
            owned_high[here], owned_low[here] = basis_high, basis_low
    sweep(0, 0)
    solved[0] = jnp.where(exists, solved[0], 0.0)

    values = jnp.concatenate([solved[0], solved[1]], axis=1)
    contribution = product(values, owned_high[...], owned_low[...], dot_last)
    left = iota((RHS // 2, BLK), 1) < 64
    packed = jnp.where(left, contribution[: RHS // 2], contribution[RHS // 2 :])
    sent_first[...] = packed
    firsts = exchange(plan_peers, lambda peer: sent_first, got_first.at[plan], send_first, recv_first)

    def to_owner(f):
        return pltpu.make_async_remote_copy(
            src_ref=solved.at[f], dst_ref=averaged.at[out_side[f]],
            send_sem=back_send.at[f], recv_sem=back_recv.at[f],
            device_id=in_device[f], device_id_type=MESH,
        )

    backs = [to_owner(f) for f in range(2)]
    keeps = [
        pltpu.make_async_copy(solved.at[f], averaged.at[in_side[f]], store_sem.at[f]) for f in range(2)
    ]
    backs[0].start()
    for f in range(2):
        keeps[f].start()

    got_first[plan] = packed
    for copy in firsts:
        copy.wait_recv()
    halves = ([], [])
    for p in range(0, PLANS, 2):
        first, second = got_first[p], got_first[p + 1]
        halves[0].append(jnp.where(left, first, pltpu.roll(second, 64, 1)))
        halves[1].append(jnp.where(left, pltpu.roll(first, 64, 1), second))
    gathered = jnp.concatenate([jnp.concatenate(half, axis=1) for half in halves], axis=0)
    coarse = product(gathered, weight_high[...], weight_low[...])
    quarter = iota((16, BLK), 1) >> 5
    for n in range(STORIES // 4):
        tile = coarse[:, n * BLK : (n + 1) * BLK]
        turned = [pltpu.roll(tile, 32 * g, 1) if g else tile for g in range(4)]
        for q in range(4):
            message = turned[(3 - q) % 4][48:64]
            for g in range(3):
                message = jnp.where(quarter == g, turned[(g - q) % 4][16 * g : 16 * g + 16], message)
            sent_second[4 * n + q] = message
    seconds = exchange(
        story_peers, lambda peer: sent_second.at[peer[0]], got_second.at[story], send_second, recv_second
    )
    backs[1].start()
    got_second[story] = sent_second[story]
    for copy in seconds:
        copy.wait_recv()
    total = got_second[0]
    for i in range(1, STORIES):
        total = total + got_second[i]
    parts = [total] + [pltpu.roll(total, BLK - 32 * g, 1) for g in range(1, 4)]
    needed = jnp.concatenate(parts, axis=0)
    needed = jnp.where(iota((RHS, BLK), 1) < 32, needed, 0.0)
    needed_high, needed_low = split(needed)
    needed_high, needed_low = needed_high.astype(F32), needed_low.astype(F32)
    operand = needed_high + pltpu.roll(needed_low, 32, 1) + pltpu.roll(needed_high, 64, 1)
    operand = operand.astype(BF16)
    stores = []
    for s in range(4):
        result[s] = dot(operand, basis_pack[:, s * FD : (s + 1) * FD])
        stores.append(pltpu.make_async_copy(result.at[s], coarse_part.at[s], store_sem.at[2 + s]))
        stores[-1].start()

    for copy in packs + couplings + products + bases + noted + firsts + seconds:
        copy.wait_send()
    for copy in backs:
        copy.wait()
    for copy in keeps + stores:
        copy.wait()


def on_device(schur_blocks, off_pattern, face_owner, residual, coarse_basis, coarse_inverse):
    hbm = pl.BlockSpec(memory_space=pltpu.HBM)
    operands = [
        pltpu.with_memory_space_constraint(operand, pltpu.HBM)
        for operand in (
            schur_blocks.reshape(4, 6, BLK, BLK),
            off_pattern.reshape(4, 2, 2).transpose(1, 2, 0),
            face_owner.reshape(1, 4),
            residual.reshape(4, RHS, FD),
            coarse_basis.reshape(4, KC * NBLK, BLK),
            coarse_inverse,
        )
    ]
    free = pl.BlockSpec(memory_space=pl.ANY)
    dma = pltpu.SemaphoreType.DMA
    out = jax.ShapeDtypeStruct((4, RHS, FD), F32)
    averaged, coarse_part = pl.pallas_call(
        kernel,
        out_shape=(out, out),
        in_specs=[hbm] * 6,
        out_specs=(free, free),
        scratch_shapes=[
            pltpu.SMEM((2, 2, 4), jnp.int32),
            pltpu.SMEM((1, 4), jnp.int32),
            pltpu.VMEM((4, 6, BLK, BLK), F32),
            pltpu.VMEM((4, RHS, FD), F32),
            pltpu.VMEM((4, KC * NBLK, BLK), F32),
            pltpu.VMEM((5 * ROW, NCOARSE), F32),
            pltpu.VMEM((9, BLK, BLK), F32),
            pltpu.VMEM((FD, FD), BF16),
            pltpu.VMEM((FD, FD), BF16),
            pltpu.VMEM((2, FD, FD), BF16),
            pltpu.VMEM((2, FD, FD), BF16),
            pltpu.VMEM((2, 2 * BLK + 8, BLK), F32),
            pltpu.VMEM((2, 2 * BLK + 8, BLK), F32),
            pltpu.VMEM((2, 2, BLK, BLK), F32),
            pltpu.VMEM((2, RHS, FD), F32),
            pltpu.VMEM((2, RHS, FD), F32),
            pltpu.VMEM((2, RHS, FD), F32),
            pltpu.VMEM((2, KC * NBLK, BLK), F32),
            pltpu.VMEM((6, 32, FD), F32),
            pltpu.VMEM((2, RHS, FD), F32),
            pltpu.VMEM((BLK, 2 * FD), BF16),
            pltpu.VMEM((BLK, 2 * FD), BF16),
            pltpu.VMEM((PLANS * 64, STORIES * 32), BF16),
            pltpu.VMEM((PLANS * 64, STORIES * 32), BF16),
            pltpu.VMEM((BLK, 4 * FD), BF16),
            pltpu.VMEM((8, BLK), F32),
            pltpu.VMEM((PLANS, 8, BLK), F32),
            pltpu.VMEM((RHS // 2, BLK), F32),
            pltpu.VMEM((PLANS, RHS // 2, BLK), F32),
            pltpu.VMEM((STORIES, 16, BLK), F32),
            pltpu.VMEM((STORIES, 16, BLK), F32),
            pltpu.VMEM((4, RHS, FD), F32),
            dma((16,)),
            dma((2, 4)),
            dma((2, 4)),
            dma((2,)),
            dma((2,)),
            dma((6,)),
            dma((PLANS - 1,)),
            dma((PLANS - 1,)),
            dma((PLANS - 1,)),
            dma((PLANS - 1,)),
            dma((STORIES - 1,)),
            dma((STORIES - 1,)),
        ],
        compiler_params=pltpu.CompilerParams(
            collective_id=0, has_side_effects=True, vmem_limit_bytes=40 * 1024 * 1024
        ),
    )(*operands)
    shape = (1, 1, 4, 1, RHS, FD)
    return averaged.reshape(shape), coarse_part.reshape(shape)


def solution(mesh):
    in_specs = (
        P("story", "plan", None, None, None, None, None),
        P("story", "plan", None, None, None, None),
        P("story", "plan", None, None),
        P("story", "plan", None, None, None, None),
        P("story", "plan", None, None, None, None),
        P(),
    )
    out_specs = (
        P("story", "plan", None, None, None, None),
        P("story", "plan", None, None, None, None),
    )
    return jax.shard_map(
        on_device, mesh=mesh, in_specs=in_specs, out_specs=out_specs, check_vma=False
    )
```

```python
import jax
import jax.numpy as jnp
from jax import lax
from jax.experimental import pallas as pl
from jax.experimental.pallas import tpu as pltpu
from jax.sharding import PartitionSpec as P

ITERS = 6
DAMPING = 0.3
BLK = 128
NBLK = 4
RHS = 64
FD = 512
CPD = 6
KC = 30
STORIES = 16
PLANS = 8
ROW = PLANS * CPD
NCOARSE = STORIES * ROW
MESH = pl.DeviceIdType.MESH
F32 = jnp.float32
BF16 = jnp.bfloat16


def iota(shape, dim):
    return lax.broadcasted_iota(jnp.int32, shape, dim)


def split(value):
    high = value.astype(BF16)
    return high, (value - high.astype(F32)).astype(BF16)


def dot(left, right):
    return jnp.dot(left, right, preferred_element_type=F32)


def dot_last(left, right):
    return lax.dot_general(left, right, (((1,), (1,)), ((), ())), preferred_element_type=F32)


def product(value, high, low, dot=dot):
    rows = value.shape[0]
    first, second = split(value)
    both = dot(jnp.concatenate([first, second], axis=0), high)
    return both[:rows] + both[rows:] + dot(first, low)


def fill(table, first, second):
    zero = jnp.zeros_like(first)
    for a, left in enumerate((zero, first, first.T)):
        for b, right in enumerate((zero, second, second.T)):
            table[3 * a + b] = left + right


def choice(pattern, side, q, t):
    index = 0
    for k in range(2):
        row, column = pattern[k, 0, side], pattern[k, 1, side]
        plain = jnp.where((row == q) & (column == t), 1, 0)
        turned = jnp.where((row == t) & (column == q), 2, 0)
        index = 3 * index + plain + turned
    return index


def place(pattern, side, table, diagonal, scales, high, low):
    for q in range(NBLK):
        for t in range(NBLK):
            if q == t:
                block = diagonal[q]
            else:
                block = table[choice(pattern, side, q, t)]
                if scales is not None:
                    block = block * scales[t]
            here = (pl.ds(q * BLK, BLK), pl.ds(t * BLK, BLK))
            high[here], low[here] = split(block)


def places(dof):
    group = (dof * 43) >> 8
    storey = jnp.where(group == 1, -1, jnp.where(group == 2, 1, 0))
    column = jnp.where(group == 4, 1, jnp.where(group == 3, PLANS - 1, 0))
    return storey, column, dof - CPD * group


def scatter(plan, shift):
    dof, lane = iota((32, 256), 0), iota((32, 256), 1)
    storey, column, member = places(dof)
    target = (storey + shift + 2) * ROW + ((plan + column) & (PLANS - 1)) * CPD + member
    return jnp.where((lane == target) & (dof < KC), 1.0, 0.0)


def gather(plan):
    lane = iota((1, STORIES * 32), 1)
    dof = lane & 31
    storey, column, member = places(dof)
    storey = storey + (lane >> 5)
    target = storey * ROW + ((plan + column) & (PLANS - 1)) * CPD + member
    target = jnp.where((dof < KC) & (storey >= 0) & (storey < STORIES), target, -1)
    return jnp.where(iota((NCOARSE, STORIES * 32), 0) == target, 1.0, 0.0).astype(BF16)


def kernel(
    schur, pattern_far, owner_far, residual, basis, inverse,
    averaged, coarse_part,
    pattern, owner, raw, rows, local, slab, table, high, low, ready_high, ready_low,
    pack_out, pack_in, coupling_in, product_out, product_in, product_own, basis_in,
    wide, owned_high, owned_low, weight_high, weight_low, basis_pack, flag, flags,
    sent_first, got_first, sent_second, got_second,
    load_sem, face_send, face_recv, back_send, back_recv,
    send_flag, recv_flag, send_first, recv_first, send_second, recv_second,
):
    story, plan = lax.axis_index("story"), lax.axis_index("plan")
    odd = lax.rem(plan, 2)
    step = 1 - 2 * odd
    in_side = (1 - odd, 3)
    out_side = (odd, 2)
    sides = (out_side[0], out_side[1], in_side[0], in_side[1])
    in_device = ((lax.rem(story + step + STORIES, STORIES), plan), (story, lax.rem(plan + 1, PLANS)))
    out_device = (
        (lax.rem(story - step + STORIES, STORIES), plan),
        (story, lax.rem(plan + PLANS - 1, PLANS)),
    )
    plan_peers = [(story, lax.rem(plan + r, PLANS)) for r in range(1, PLANS)]
    story_peers = [(lax.rem(story + r, STORIES), plan) for r in range(1, STORIES)]

    barrier = pltpu.get_barrier_semaphore()
    nearest = [plan_peers[0], plan_peers[-1], story_peers[0], story_peers[-1]]
    for peer in nearest + plan_peers[1:-1] + story_peers[1:-1]:
        pl.semaphore_signal(barrier, inc=1, device_id=peer, device_id_type=MESH)

    small = (
        pltpu.make_async_copy(pattern_far, pattern, load_sem.at[14]),
        pltpu.make_async_copy(owner_far, owner, load_sem.at[15]),
    )
    loads = []
    for k in range(4):
        loads.append(pltpu.make_async_copy(schur.at[sides[k]], raw.at[k], load_sem.at[k]))
        loads.append(pltpu.make_async_copy(residual.at[sides[k]], rows.at[k], load_sem.at[4 + k]))
    loads.append(pltpu.make_async_copy(basis, local, load_sem.at[8]))
    for o in range(5):
        at = jnp.clip(story + o - 2, 0, STORIES - 1) * ROW
        loads.append(
            pltpu.make_async_copy(
                inverse.at[pl.ds(pl.multiple_of(at, 8), ROW)],
                slab.at[pl.ds(o * ROW, ROW)],
                load_sem.at[9 + o],
            )
        )
    for load in loads[:4] + list(small) + loads[4:]:
        load.start()

    line, lane = iota((BLK, BLK), 0), iota((BLK, BLK), 1)
    upper, equal = line <= lane, line == lane

    def diagonal_of(block):
        return jnp.sum(jnp.where(equal, block, 0.0), axis=0, keepdims=True)

    def to_sharer(f, m, source, target):
        return pltpu.make_async_remote_copy(
            src_ref=source, dst_ref=target, send_sem=face_send.at[f, m], recv_sem=face_recv.at[f, m],
            device_id=out_device[f], device_id_type=MESH,
        )

    def exchange(peers, source, target, send_sem, recv_sem):
        copies = []
        for r, peer in enumerate(peers):
            copies.append(
                pltpu.make_async_remote_copy(
                    src_ref=source(peer), dst_ref=target, send_sem=send_sem.at[r],
                    recv_sem=recv_sem.at[r], device_id=peer, device_id_type=MESH,
                )
            )
            copies[-1].start()
        return copies

    for copy in small:
        copy.wait()
    mine = [owner[0, in_side[f]].astype(F32) for f in range(2)]
    for f in range(2):
        flag[f : f + 1] = jnp.full((1, BLK), mine[f], F32)
    flag[2:8] = jnp.zeros((6, BLK), F32)
    flags[plan] = flag[...]

    pl.semaphore_wait(barrier, PLANS - 1 + STORIES - 1)
    couplings = [
        to_sharer(f, 1, schur.at[out_side[f], pl.ds(NBLK, 2)], coupling_in.at[f]) for f in range(2)
    ]
    packs = [to_sharer(f, 0, pack_out.at[f], pack_in.at[f]) for f in range(2)]
    products = [to_sharer(f, 2, product_out.at[f], product_in.at[f]) for f in range(2)]
    bases = [to_sharer(f, 3, basis.at[out_side[f]], basis_in.at[f]) for f in range(2)]
    for f in range(2):
        couplings[f].start()

    for f in range(2):
        loads[2 * f].wait()
        for h in range(2):
            first, second = raw[f, 2 * h], raw[f, 2 * h + 1]
            pack_out[f, h * BLK : (h + 1) * BLK] = jnp.where(upper, first, second)
            pack_out[f, 2 * BLK + h : 2 * BLK + h + 1] = diagonal_of(second)
        pack_out[f, 2 * BLK + 2 : 2 * BLK + 8] = jnp.zeros((6, BLK), F32)
        packs[f].start()
    noted = exchange(plan_peers, lambda peer: flag, flags.at[plan], send_flag, recv_flag)

    for k in range(4):
        if k >= 2:
            loads[2 * k].wait()
        loads[2 * k + 1].wait()
        fill(table, raw[k, NBLK], raw[k, NBLK + 1])
        place(pattern, sides[k], table, [raw[k, n] for n in range(NBLK)], None, high, low)
        target = product_out.at[k] if k < 2 else product_own.at[k - 2]
        target[...] = product(rows[k], high[...], low[...])
        if k < 2:
            products[k].start()
    for f in range(2):
        bases[f].start()

    exists = jnp.where(odd == 0, story < STORIES - 1, story > 0)
    present = (jnp.where(story > 0, 1.0, 0.0), jnp.where(story < STORIES - 1, 1.0, 0.0), 1.0, 1.0)
    loads[8].wait()
    wide[...] = jnp.zeros_like(wide)

    def widen(source, s, target):
        for n in range(NBLK):
            wide[target, 0:KC, n * BLK : (n + 1) * BLK] = source[s, pl.ds(n, KC, stride=NBLK)]

    for s in range(4):
        widen(local, s, s)
        basis_high, basis_low = split(wide[s] * present[s])
        here = pl.ds(s * FD, FD)
        basis_pack[:, here] = jnp.concatenate(
            [basis_high, basis_high, basis_low, jnp.zeros_like(basis_low)], axis=0
        )

    pieces = []
    for o in range(5):
        loads[9 + o].wait()
        at = story + o - 2
        pieces.append(jnp.where((at >= 0) & (at < STORIES), slab[o * ROW : (o + 1) * ROW], 0.0))
    pieces.append(jnp.zeros((16, NCOARSE), F32))
    slab_high, slab_low = split(jnp.concatenate(pieces, axis=0))
    columns = dot(jnp.concatenate([slab_high, slab_low], axis=0), gather(plan)).astype(BF16)
    scaled = []
    for f in range(2):
        packs[f].wait_recv()
        couplings[f].wait_recv()
        diagonal, scales = [], []
        for h in range(2):
            first, second = raw[2 + f, 2 * h], raw[2 + f, 2 * h + 1]
            packed = jnp.where(upper, first, second) + pack_in[f, h * BLK : (h + 1) * BLK]
            turned = packed.T
            second_diagonal = diagonal_of(second) + pack_in[f, 2 * BLK + h : 2 * BLK + h + 1]
            scales += [-DAMPING / diagonal_of(packed), -DAMPING / second_diagonal]
            diagonal.append(
                jnp.where(equal, 1.0 - DAMPING, jnp.where(upper, packed, turned) * scales[-2])
            )
            diagonal.append(
                jnp.where(equal, 1.0 - DAMPING, jnp.where(upper, turned, packed) * scales[-1])
            )
        fill(
            table,
            raw[2 + f, NBLK] + coupling_in[f, 0],
            raw[2 + f, NBLK + 1] + coupling_in[f, 1],
        )
        place(pattern, in_side[f], table, diagonal, scales, ready_high.at[f], ready_low.at[f])
        scaled.append(jnp.concatenate(scales, axis=1))

    for f in range(2):
        products[f].wait_recv()
        product_own[f] = -(product_own[f] + product_in[f]) * scaled[f]

    def sweep(values):
        return [
            product_own[f] + product(values[f], ready_high[f], ready_low[f]) for f in range(2)
        ]

    solved = [product_own[f] for f in range(2)]
    for _ in range(ITERS - 2):
        solved = sweep(solved)
    owned_high[...] = jnp.zeros_like(owned_high)
    owned_low[...] = jnp.zeros_like(owned_low)
    for f in range(2):
        bases[f].wait_recv()
        widen(basis_in, f, 4 + f)
        basis_high, basis_low = split(wide[in_side[f]] * mine[f] + wide[4 + f] * (1.0 - mine[f]))
        for n in range(2):
            here = (pl.ds(64 * n + 32 * f, 32), pl.ds(f * FD, FD))
            owned_high[here], owned_low[here] = basis_high, basis_low
    solved = sweep(solved)
    solved[0] = jnp.where(exists, solved[0], 0.0)
    for f in range(2):
        averaged[in_side[f]] = solved[f]
    values = jnp.concatenate(solved, axis=1)
    contribution = product(values, owned_high[...], owned_low[...], dot_last)
    left = iota((RHS // 2, BLK), 1) < 64
    packed = jnp.where(left, contribution[: RHS // 2], contribution[RHS // 2 :])
    sent_first[...] = packed
    firsts = exchange(plan_peers, lambda peer: sent_first, got_first.at[plan], send_first, recv_first)

    def to_owner(f):
        return pltpu.make_async_remote_copy(
            src_ref=averaged.at[in_side[f]], dst_ref=averaged.at[out_side[f]],
            send_sem=back_send.at[f], recv_sem=back_recv.at[f],
            device_id=in_device[f], device_id_type=MESH,
        )

    backs = [to_owner(f) for f in range(2)]
    backs[0].start()

    got_first[plan] = packed
    for copy in noted:
        copy.wait_recv()
    chosen = []
    for p in range(PLANS):
        for f in range(2):
            kept = jnp.concatenate([flags[p, f : f + 1]] * 2, axis=1)
            other = scatter(p, 1 - 2 * (p % 2)) if f == 0 else scatter(p + 1, 0)
            chosen.append((scatter(p, 0) * kept + other * (1.0 - kept)).astype(BF16))
    chosen = jnp.concatenate(chosen, axis=0)
    weight_high[...] = dot(chosen, columns[:256]).astype(BF16)
    weight_low[...] = dot(chosen, columns[256:]).astype(BF16)
    for copy in firsts:
        copy.wait_recv()
    halves = ([], [])
    for p in range(0, PLANS, 2):
        first, second = got_first[p], got_first[p + 1]
        halves[0].append(jnp.where(left, first, pltpu.roll(second, 64, 1)))
        halves[1].append(jnp.where(left, pltpu.roll(first, 64, 1), second))
    gathered = jnp.concatenate([jnp.concatenate(half, axis=1) for half in halves], axis=0)
    coarse = product(gathered, weight_high[...], weight_low[...])
    quarter = iota((16, BLK), 1) >> 5
    for n in range(STORIES // 4):
        tile = coarse[:, n * BLK : (n + 1) * BLK]
        turned = [pltpu.roll(tile, 32 * g, 1) if g else tile for g in range(4)]
        for q in range(4):
            message = turned[(3 - q) % 4][48:64]
            for g in range(3):
                message = jnp.where(quarter == g, turned[(g - q) % 4][16 * g : 16 * g + 16], message)
            sent_second[4 * n + q] = message
    seconds = exchange(
        story_peers, lambda peer: sent_second.at[peer[0]], got_second.at[story], send_second, recv_second
    )
    backs[1].start()
    got_second[story] = sent_second[story]
    for copy in seconds:
        copy.wait_recv()
    total = got_second[0]
    for i in range(1, STORIES):
        total = total + got_second[i]
    parts = [total] + [pltpu.roll(total, BLK - 32 * g, 1) for g in range(1, 4)]
    needed = jnp.concatenate(parts, axis=0)
    needed = jnp.where(iota((RHS, BLK), 1) < 32, needed, 0.0)
    needed_high, needed_low = split(needed)
    needed_high, needed_low = needed_high.astype(F32), needed_low.astype(F32)
    operand = needed_high + pltpu.roll(needed_low, 32, 1) + pltpu.roll(needed_high, 64, 1)
    operand = operand.astype(BF16)
    for s in range(4):
        coarse_part[s] = dot(operand, basis_pack[:, s * FD : (s + 1) * FD])

    for copy in packs + couplings + products + bases + noted + firsts + seconds:
        copy.wait_send()
    for copy in backs:
        copy.wait()


def store(averaged, coarse_part, averaged_out, coarse_part_out, sem):
    copies = []
    for s in range(4):
        copies.append(pltpu.make_async_copy(averaged.at[s], averaged_out.at[s], sem.at[0, s]))
        copies.append(pltpu.make_async_copy(coarse_part.at[s], coarse_part_out.at[s], sem.at[1, s]))
    for copy in copies:
        copy.start()
    for copy in copies:
        copy.wait()


def on_device(schur_blocks, off_pattern, face_owner, residual, coarse_basis, coarse_inverse):
    hbm = pl.BlockSpec(memory_space=pltpu.HBM)
    operands = [
        pltpu.with_memory_space_constraint(operand, pltpu.HBM)
        for operand in (
            schur_blocks.reshape(4, 6, BLK, BLK),
            off_pattern.reshape(4, 2, 2).transpose(1, 2, 0),
            face_owner.reshape(1, 4),
            residual.reshape(4, RHS, FD),
            coarse_basis.reshape(4, KC * NBLK, BLK),
            coarse_inverse,
        )
    ]
    vmem = pl.BlockSpec(memory_space=pltpu.VMEM)
    dma = pltpu.SemaphoreType.DMA
    out = pltpu.VMEM((4, RHS, FD), F32)
    averaged, coarse_part = pl.pallas_call(
        kernel,
        out_shape=(out, out),
        in_specs=[hbm] * 6,
        out_specs=(vmem, vmem),
        scratch_shapes=[
            pltpu.SMEM((2, 2, 4), jnp.int32),
            pltpu.SMEM((1, 4), jnp.int32),
            pltpu.VMEM((4, 6, BLK, BLK), F32),
            pltpu.VMEM((4, RHS, FD), F32),
            pltpu.VMEM((4, KC * NBLK, BLK), F32),
            pltpu.VMEM((5 * ROW, NCOARSE), F32),
            pltpu.VMEM((9, BLK, BLK), F32),
            pltpu.VMEM((FD, FD), BF16),
            pltpu.VMEM((FD, FD), BF16),
            pltpu.VMEM((2, FD, FD), BF16),
            pltpu.VMEM((2, FD, FD), BF16),
            pltpu.VMEM((2, 2 * BLK + 8, BLK), F32),
            pltpu.VMEM((2, 2 * BLK + 8, BLK), F32),
            pltpu.VMEM((2, 2, BLK, BLK), F32),
            pltpu.VMEM((2, RHS, FD), F32),
            pltpu.VMEM((2, RHS, FD), F32),
            pltpu.VMEM((2, RHS, FD), F32),
            pltpu.VMEM((2, KC * NBLK, BLK), F32),
            pltpu.VMEM((6, 32, FD), F32),
            pltpu.VMEM((BLK, 2 * FD), BF16),
            pltpu.VMEM((BLK, 2 * FD), BF16),
            pltpu.VMEM((PLANS * 64, STORIES * 32), BF16),
            pltpu.VMEM((PLANS * 64, STORIES * 32), BF16),
            pltpu.VMEM((BLK, 4 * FD), BF16),
            pltpu.VMEM((8, BLK), F32),
            pltpu.VMEM((PLANS, 8, BLK), F32),
            pltpu.VMEM((RHS // 2, BLK), F32),
            pltpu.VMEM((PLANS, RHS // 2, BLK), F32),
            pltpu.VMEM((STORIES, 16, BLK), F32),
            pltpu.VMEM((STORIES, 16, BLK), F32),
            dma((16,)),
            dma((2, 4)),
            dma((2, 4)),
            dma((2,)),
            dma((2,)),
            dma((PLANS - 1,)),
            dma((PLANS - 1,)),
            dma((PLANS - 1,)),
            dma((PLANS - 1,)),
            dma((STORIES - 1,)),
            dma((STORIES - 1,)),
        ],
        compiler_params=pltpu.CompilerParams(
            collective_id=0, has_side_effects=True, vmem_limit_bytes=40 * 1024 * 1024
        ),
    )(*operands)
    free = pl.BlockSpec(memory_space=pl.ANY)
    out = pltpu.HBM((4, RHS, FD), F32)
    averaged, coarse_part = pl.pallas_call(
        store,
        out_shape=(out, out),
        in_specs=[free, free],
        out_specs=(free, free),
        scratch_shapes=[dma((2, 4))],
    )(*[pltpu.with_memory_space_constraint(value, pltpu.VMEM) for value in (averaged, coarse_part)])
    shape = (1, 1, 4, 1, RHS, FD)
    return averaged.reshape(shape), coarse_part.reshape(shape)


def solution(mesh):
    in_specs = (
        P("story", "plan", None, None, None, None, None),
        P("story", "plan", None, None, None, None),
        P("story", "plan", None, None),
        P("story", "plan", None, None, None, None),
        P("story", "plan", None, None, None, None),
        P(),
    )
    out_specs = (
        P("story", "plan", None, None, None, None),
        P("story", "plan", None, None, None, None),
    )
    return jax.shard_map(
        on_device, mesh=mesh, in_specs=in_specs, out_specs=out_specs, check_vma=False
    )
```

```python
import jax
import jax.numpy as jnp
from jax import lax
from jax.experimental import pallas as pl
from jax.experimental.pallas import tpu as pltpu
from jax.sharding import PartitionSpec as P

ITERS = 6
DAMPING = 0.3
BLK = 128
NBLK = 4
RHS = 64
FD = 512
CPD = 6
KC = 30
STORIES = 16
PLANS = 8
ROW = PLANS * CPD
NCOARSE = STORIES * ROW
MESH = pl.DeviceIdType.MESH
F32 = jnp.float32
BF16 = jnp.bfloat16


def iota(shape, dim):
    return lax.broadcasted_iota(jnp.int32, shape, dim)


def split(value):
    high = value.astype(BF16)
    return high, (value - high.astype(F32)).astype(BF16)


def dot(left, right):
    return jnp.dot(left, right, preferred_element_type=F32)


def dot_last(left, right):
    return lax.dot_general(left, right, (((1,), (1,)), ((), ())), preferred_element_type=F32)


def product(value, high, low, dot=dot):
    rows = value.shape[0]
    first, second = split(value)
    both = dot(jnp.concatenate([first, second], axis=0), high)
    return both[:rows] + both[rows:] + dot(first, low)


def fill(table, first, second):
    zero = jnp.zeros_like(first)
    for a, left in enumerate((zero, first, first.T)):
        for b, right in enumerate((zero, second, second.T)):
            table[3 * a + b] = left + right


def choice(pattern, side, q, t):
    index = 0
    for k in range(2):
        row, column = pattern[k, 0, side], pattern[k, 1, side]
        plain = jnp.where((row == q) & (column == t), 1, 0)
        turned = jnp.where((row == t) & (column == q), 2, 0)
        index = 3 * index + plain + turned
    return index


def place(pattern, side, table, diagonal, scales, high, low):
    for q in range(NBLK):
        for t in range(NBLK):
            if q == t:
                block = diagonal[q]
            else:
                block = table[choice(pattern, side, q, t)]
                if scales is not None:
                    block = block * scales[t]
            here = (pl.ds(q * BLK, BLK), pl.ds(t * BLK, BLK))
            high[here], low[here] = split(block)


def places(dof):
    group = (dof * 43) >> 8
    storey = jnp.where(group == 1, -1, jnp.where(group == 2, 1, 0))
    column = jnp.where(group == 4, 1, jnp.where(group == 3, PLANS - 1, 0))
    return storey, column, dof - CPD * group


def scatter(plan, shift):
    dof, lane = iota((32, 256), 0), iota((32, 256), 1)
    storey, column, member = places(dof)
    target = (storey + shift) * ROW + ((plan + column) & (PLANS - 1)) * CPD + member
    return jnp.where((lane == target) & (dof < KC), 1.0, 0.0)


def gather(plan):
    lane = iota((1, STORIES * 32), 1)
    dof = lane & 31
    storey, column, member = places(dof)
    storey = storey + (lane >> 5)
    target = storey * ROW + ((plan + column) & (PLANS - 1)) * CPD + member
    target = jnp.where((dof < KC) & (storey >= 0) & (storey < STORIES), target, -1)
    return jnp.where(iota((NCOARSE, STORIES * 32), 0) == target, 1.0, 0.0).astype(BF16)


def kernel(
    schur, pattern_far, owner_far, residual, basis, inverse,
    averaged, coarse_part,
    pattern, owner, raw, rows, local, slab, table, high, low, ready_high, ready_low,
    pack_out, pack_in, coupling_in, product_out, product_in, product_own, basis_in,
    wide, owned_high, owned_low, weight_high, weight_low, basis_pack, flag, flags,
    sent_first, got_first, sent_second, got_second,
    load_sem, face_send, face_recv, back_send, back_recv,
    send_flag, recv_flag, send_first, recv_first, send_second, recv_second, near, middle, far, last,
):
    story, plan = lax.axis_index("story"), lax.axis_index("plan")
    odd = lax.rem(plan, 2)
    step = 1 - 2 * odd
    in_side = (1 - odd, 3)
    out_side = (odd, 2)
    sides = (out_side[0], out_side[1], in_side[0], in_side[1])
    in_device = ((lax.rem(story + step + STORIES, STORIES), plan), (story, lax.rem(plan + 1, PLANS)))
    out_device = (
        (lax.rem(story - step + STORIES, STORIES), plan),
        (story, lax.rem(plan + PLANS - 1, PLANS)),
    )
    plan_peers = [(story, lax.rem(plan + r, PLANS)) for r in (4, 3, 5, 2, 6, 1, 7)]
    story_peers = [
        (lax.rem(story + r, STORIES), plan) for r in (10, 6, 9, 7, 11, 5, 8, 2, 14, 13, 3, 12, 4, 1, 15)
    ]

    barrier = pltpu.get_barrier_semaphore()

    def around(distance):
        peers = [(story, lax.rem(plan + r, PLANS)) for r in sorted({distance, PLANS - distance}) if 0 < r < PLANS]
        if distance > PLANS // 2:
            peers = []
        peers = [(None, peer) for peer in peers]
        peers.append((story >= distance, (lax.rem(story + STORIES - distance, STORIES), plan)))
        peers.append((story < STORIES - distance, (lax.rem(story + distance, STORIES), plan)))
        return peers

    def announce(semaphore, distance):
        for condition, peer in around(distance):
            def signal(peer=peer):
                pl.semaphore_signal(semaphore, inc=1, device_id=peer, device_id_type=MESH)

            if condition is None:
                signal()
            else:
                pl.when(condition)(signal)

    def hear(semaphore, distance):
        count = 0
        for condition, _ in around(distance):
            count = count + (1 if condition is None else jnp.where(condition, 1, 0))
        pl.semaphore_wait(semaphore, count)

    announce(barrier, 1)

    small = (
        pltpu.make_async_copy(pattern_far, pattern, load_sem.at[10]),
        pltpu.make_async_copy(owner_far, owner, load_sem.at[11]),
    )
    loads = []
    for k in range(4):
        loads.append(pltpu.make_async_copy(schur.at[sides[k]], raw.at[k], load_sem.at[k]))
        loads.append(pltpu.make_async_copy(residual.at[sides[k]], rows.at[k], load_sem.at[4 + k]))
    loads.append(pltpu.make_async_copy(basis, local, load_sem.at[8]))
    lowest = jnp.clip(story - 2, 0, STORIES - 5)
    loads.append(
        pltpu.make_async_copy(
            inverse.at[pl.ds(pl.multiple_of(lowest * ROW, 8), 5 * ROW)], slab, load_sem.at[9]
        )
    )
    for load in loads[:4]:
        load.start()

    line, lane = iota((BLK, BLK), 0), iota((BLK, BLK), 1)
    upper, equal = line <= lane, line == lane

    def diagonal_of(block):
        return jnp.sum(jnp.where(equal, block, 0.0), axis=0, keepdims=True)

    def to_sharer(f, m, source, target):
        return pltpu.make_async_remote_copy(
            src_ref=source, dst_ref=target, send_sem=face_send.at[f, m], recv_sem=face_recv.at[f, m],
            device_id=out_device[f], device_id_type=MESH,
        )

    def exchange(peers, source, target, send_sem, recv_sem):
        copies = []
        for r, peer in enumerate(peers):
            copies.append(
                pltpu.make_async_remote_copy(
                    src_ref=source(peer), dst_ref=target, send_sem=send_sem.at[r],
                    recv_sem=recv_sem.at[r], device_id=peer, device_id_type=MESH,
                )
            )
            copies[-1].start()
        return copies

    hear(barrier, 1)
    couplings = [
        to_sharer(f, 1, schur.at[out_side[f], pl.ds(NBLK, 2)], coupling_in.at[f]) for f in range(2)
    ]
    packs = [to_sharer(f, 0, pack_out.at[f], pack_in.at[f]) for f in range(2)]
    products = [to_sharer(f, 2, product_out.at[f], product_in.at[f]) for f in range(2)]
    bases = [to_sharer(f, 3, basis.at[out_side[f]], basis_in.at[f]) for f in range(2)]
    exists = jnp.where(odd == 0, story < STORIES - 1, story > 0)
    leaves = jnp.where(odd == 0, story > 0, story < STORIES - 1)

    def when(condition, f, action):
        if f == 0:
            pl.when(condition)(action)
        else:
            action()

    for f in range(2):
        when(leaves, f, couplings[f].start)
    for load in list(small) + loads[4:]:
        load.start()

    for f in range(2):
        loads[2 * f].wait()
        for h in range(2):
            first, second = raw[f, 2 * h], raw[f, 2 * h + 1]
            pack_out[f, h * BLK : (h + 1) * BLK] = jnp.where(upper, first, second)
            pack_out[f, 2 * BLK + h : 2 * BLK + h + 1] = diagonal_of(second)
        pack_out[f, 2 * BLK + 2 : 2 * BLK + 8] = jnp.zeros((6, BLK), F32)
        when(leaves, f, packs[f].start)
    for copy in small:
        copy.wait()
    mine = [owner[0, in_side[f]].astype(F32) for f in range(2)]
    for f in range(2):
        flag[f : f + 1] = jnp.full((1, BLK), mine[f], F32)
    flag[2:8] = jnp.zeros((6, BLK), F32)
    flags[plan] = flag[...]

    for k in range(4):
        if k >= 2:
            loads[2 * k].wait()
        loads[2 * k + 1].wait()
        fill(table, raw[k, NBLK], raw[k, NBLK + 1])
        place(pattern, sides[k], table, [raw[k, n] for n in range(NBLK)], None, high, low)
        target = product_out.at[k] if k < 2 else product_own.at[k - 2]
        target[...] = product(rows[k], high[...], low[...])
        if k < 2:
            when(leaves, k, products[k].start)
        if k == 0:
            announce(near, 1)
    for f in range(2):
        when(leaves, f, bases[f].start)
    hear(near, 1)
    announce(middle, 2)

    present = (jnp.where(story > 0, 1.0, 0.0), jnp.where(story < STORIES - 1, 1.0, 0.0), 1.0, 1.0)
    loads[8].wait()
    wide[...] = jnp.zeros_like(wide)

    def widen(source, s, target):
        for n in range(NBLK):
            wide[target, 0:KC, n * BLK : (n + 1) * BLK] = source[s, pl.ds(n, KC, stride=NBLK)]

    for s in range(4):
        widen(local, s, s)
        basis_high, basis_low = split(wide[s] * present[s])
        here = pl.ds(s * FD, FD)
        basis_pack[:, here] = jnp.concatenate(
            [basis_high, basis_high, basis_low, jnp.zeros_like(basis_low)], axis=0
        )

    loads[9].wait()
    slab_high, slab_low = split(jnp.concatenate([slab[...], jnp.zeros((16, NCOARSE), F32)], axis=0))
    columns = dot(jnp.concatenate([slab_high, slab_low], axis=0), gather(plan)).astype(BF16)
    hear(middle, 2)
    announce(far, 4)
    noted = exchange(plan_peers, lambda peer: flag, flags.at[plan], send_flag, recv_flag)
    scaled = []
    for f in range(2):
        when(exists, f, packs[f].wait_recv)
        when(exists, f, couplings[f].wait_recv)
        diagonal, scales = [], []
        for h in range(2):
            first, second = raw[2 + f, 2 * h], raw[2 + f, 2 * h + 1]
            packed = jnp.where(upper, first, second) + pack_in[f, h * BLK : (h + 1) * BLK]
            turned = packed.T
            second_diagonal = diagonal_of(second) + pack_in[f, 2 * BLK + h : 2 * BLK + h + 1]
            scales += [-DAMPING / diagonal_of(packed), -DAMPING / second_diagonal]
            diagonal.append(
                jnp.where(equal, 1.0 - DAMPING, jnp.where(upper, packed, turned) * scales[-2])
            )
            diagonal.append(
                jnp.where(equal, 1.0 - DAMPING, jnp.where(upper, turned, packed) * scales[-1])
            )
        fill(
            table,
            raw[2 + f, NBLK] + coupling_in[f, 0],
            raw[2 + f, NBLK + 1] + coupling_in[f, 1],
        )
        place(pattern, in_side[f], table, diagonal, scales, ready_high.at[f], ready_low.at[f])
        scaled.append(jnp.concatenate(scales, axis=1))

    for f in range(2):
        when(exists, f, products[f].wait_recv)
        product_own[f] = -(product_own[f] + product_in[f]) * scaled[f]

    def sweep(values):
        return [
            product_own[f] + product(values[f], ready_high[f], ready_low[f]) for f in range(2)
        ]

    solved = [product_own[f] for f in range(2)]
    for _ in range(ITERS - 2):
        solved = sweep(solved)
    owned_high[...] = jnp.zeros_like(owned_high)
    owned_low[...] = jnp.zeros_like(owned_low)
    for f in range(2):
        when(exists, f, bases[f].wait_recv)
        widen(basis_in, f, 4 + f)
        chosen = wide[in_side[f]] * mine[f] + wide[4 + f] * (1.0 - mine[f])
        if f == 0:
            chosen = jnp.where(exists, chosen, 0.0)
        basis_high, basis_low = split(chosen)
        for n in range(2):
            here = (pl.ds(64 * n + 32 * f, 32), pl.ds(f * FD, FD))
            owned_high[here], owned_low[here] = basis_high, basis_low
    solved = sweep(solved)
    solved[0] = jnp.where(exists, solved[0], 0.0)
    for f in range(2):
        averaged[in_side[f]] = solved[f]
    values = jnp.concatenate(solved, axis=1)
    contribution = product(values, owned_high[...], owned_low[...], dot_last)
    left = iota((RHS // 2, BLK), 1) < 64
    packed = jnp.where(left, contribution[: RHS // 2], contribution[RHS // 2 :])
    sent_first[...] = packed
    firsts = exchange(plan_peers, lambda peer: sent_first, got_first.at[plan], send_first, recv_first)

    def to_owner(f):
        return pltpu.make_async_remote_copy(
            src_ref=averaged.at[in_side[f]], dst_ref=averaged.at[out_side[f]],
            send_sem=back_send.at[f], recv_sem=back_recv.at[f],
            device_id=in_device[f], device_id_type=MESH,
        )

    backs = [to_owner(f) for f in range(2)]
    when(exists, 0, backs[0].start)

    @pl.when(jnp.logical_not(leaves))
    def _():
        averaged[out_side[0]] = jnp.zeros((RHS, FD), F32)


    got_first[plan] = packed
    hear(far, 4)
    announce(last, 8)
    for copy in noted:
        copy.wait_recv()
    height = story - lowest
    chosen = []
    for p in range(PLANS):
        for f in range(2):
            kept = jnp.concatenate([flags[p, f : f + 1]] * 2, axis=1)
            other = scatter(p, height + 1 - 2 * (p % 2)) if f == 0 else scatter(p + 1, height)
            chosen.append((scatter(p, height) * kept + other * (1.0 - kept)).astype(BF16))
    chosen = jnp.concatenate(chosen, axis=0)
    weight_high[...] = dot(chosen, columns[:256]).astype(BF16)
    weight_low[...] = dot(chosen, columns[256:]).astype(BF16)
    for copy in firsts:
        copy.wait_recv()
    halves = ([], [])
    for p in range(0, PLANS, 2):
        first, second = got_first[p], got_first[p + 1]
        halves[0].append(jnp.where(left, first, pltpu.roll(second, 64, 1)))
        halves[1].append(jnp.where(left, pltpu.roll(first, 64, 1), second))
    gathered = jnp.concatenate([jnp.concatenate(half, axis=1) for half in halves], axis=0)
    coarse = product(gathered, weight_high[...], weight_low[...])
    quarter = iota((16, BLK), 1) >> 5
    for n in range(STORIES // 4):
        tile = coarse[:, n * BLK : (n + 1) * BLK]
        turned = [pltpu.roll(tile, 32 * g, 1) if g else tile for g in range(4)]
        for q in range(4):
            message = turned[(3 - q) % 4][48:64]
            for g in range(3):
                message = jnp.where(quarter == g, turned[(g - q) % 4][16 * g : 16 * g + 16], message)
            sent_second[4 * n + q] = message
    hear(last, 8)
    seconds = exchange(
        story_peers, lambda peer: sent_second.at[peer[0]], got_second.at[story], send_second, recv_second
    )
    backs[1].start()
    got_second[story] = sent_second[story]
    for copy in seconds:
        copy.wait_recv()
    total = got_second[0]
    for i in range(1, STORIES):
        total = total + got_second[i]
    parts = [total] + [pltpu.roll(total, BLK - 32 * g, 1) for g in range(1, 4)]
    needed = jnp.concatenate(parts, axis=0)
    needed = jnp.where(iota((RHS, BLK), 1) < 32, needed, 0.0)
    needed_high, needed_low = split(needed)
    needed_high, needed_low = needed_high.astype(F32), needed_low.astype(F32)
    operand = needed_high + pltpu.roll(needed_low, 32, 1) + pltpu.roll(needed_high, 64, 1)
    operand = operand.astype(BF16)
    for s in range(4):
        coarse_part[s] = dot(operand, basis_pack[:, s * FD : (s + 1) * FD])

    for copies in (packs, couplings, products, bases):
        for f in range(2):
            when(leaves, f, copies[f].wait_send)
    for copy in noted + firsts + seconds:
        copy.wait_send()
    for f in range(2):
        when(exists, f, backs[f].wait_send)
        when(leaves, f, backs[f].wait_recv)


def store(averaged, coarse_part, averaged_out, coarse_part_out, sem):
    copies = []
    for s in range(4):
        copies.append(pltpu.make_async_copy(averaged.at[s], averaged_out.at[s], sem.at[0, s]))
        copies.append(pltpu.make_async_copy(coarse_part.at[s], coarse_part_out.at[s], sem.at[1, s]))
    for copy in copies:
        copy.start()
    for copy in copies:
        copy.wait()


def on_device(schur_blocks, off_pattern, face_owner, residual, coarse_basis, coarse_inverse):
    hbm = pl.BlockSpec(memory_space=pltpu.HBM)
    operands = [
        pltpu.with_memory_space_constraint(operand, pltpu.HBM)
        for operand in (
            schur_blocks.reshape(4, 6, BLK, BLK),
            off_pattern.reshape(4, 2, 2).transpose(1, 2, 0),
            face_owner.reshape(1, 4),
            residual.reshape(4, RHS, FD),
            coarse_basis.reshape(4, KC * NBLK, BLK),
            coarse_inverse,
        )
    ]
    vmem = pl.BlockSpec(memory_space=pltpu.VMEM)
    dma = pltpu.SemaphoreType.DMA
    out = pltpu.VMEM((4, RHS, FD), F32)
    averaged, coarse_part = pl.pallas_call(
        kernel,
        out_shape=(out, out),
        in_specs=[hbm] * 6,
        out_specs=(vmem, vmem),
        scratch_shapes=[
            pltpu.SMEM((2, 2, 4), jnp.int32),
            pltpu.SMEM((1, 4), jnp.int32),
            pltpu.VMEM((4, 6, BLK, BLK), F32),
            pltpu.VMEM((4, RHS, FD), F32),
            pltpu.VMEM((4, KC * NBLK, BLK), F32),
            pltpu.VMEM((5 * ROW, NCOARSE), F32),
            pltpu.VMEM((9, BLK, BLK), F32),
            pltpu.VMEM((FD, FD), BF16),
            pltpu.VMEM((FD, FD), BF16),
            pltpu.VMEM((2, FD, FD), BF16),
            pltpu.VMEM((2, FD, FD), BF16),
            pltpu.VMEM((2, 2 * BLK + 8, BLK), F32),
            pltpu.VMEM((2, 2 * BLK + 8, BLK), F32),
            pltpu.VMEM((2, 2, BLK, BLK), F32),
            pltpu.VMEM((2, RHS, FD), F32),
            pltpu.VMEM((2, RHS, FD), F32),
            pltpu.VMEM((2, RHS, FD), F32),
            pltpu.VMEM((2, KC * NBLK, BLK), F32),
            pltpu.VMEM((6, 32, FD), F32),
            pltpu.VMEM((BLK, 2 * FD), BF16),
            pltpu.VMEM((BLK, 2 * FD), BF16),
            pltpu.VMEM((PLANS * 64, STORIES * 32), BF16),
            pltpu.VMEM((PLANS * 64, STORIES * 32), BF16),
            pltpu.VMEM((BLK, 4 * FD), BF16),
            pltpu.VMEM((8, BLK), F32),
            pltpu.VMEM((PLANS, 8, BLK), F32),
            pltpu.VMEM((RHS // 2, BLK), F32),
            pltpu.VMEM((PLANS, RHS // 2, BLK), F32),
            pltpu.VMEM((STORIES, 16, BLK), F32),
            pltpu.VMEM((STORIES, 16, BLK), F32),
            dma((12,)),
            dma((2, 4)),
            dma((2, 4)),
            dma((2,)),
            dma((2,)),
            dma((PLANS - 1,)),
            dma((PLANS - 1,)),
            dma((PLANS - 1,)),
            dma((PLANS - 1,)),
            dma((STORIES - 1,)),
            dma((STORIES - 1,)),
            pltpu.SemaphoreType.REGULAR,
            pltpu.SemaphoreType.REGULAR,
            pltpu.SemaphoreType.REGULAR,
            pltpu.SemaphoreType.REGULAR,
        ],
        compiler_params=pltpu.CompilerParams(
            collective_id=0, has_side_effects=True, vmem_limit_bytes=40 * 1024 * 1024
        ),
    )(*operands)
    free = pl.BlockSpec(memory_space=pl.ANY)
    out = pltpu.HBM((4, RHS, FD), F32)
    averaged, coarse_part = pl.pallas_call(
        store,
        out_shape=(out, out),
        in_specs=[free, free],
        out_specs=(free, free),
        scratch_shapes=[dma((2, 4))],
    )(*[pltpu.with_memory_space_constraint(value, pltpu.VMEM) for value in (averaged, coarse_part)])
    shape = (1, 1, 4, 1, RHS, FD)
    return averaged.reshape(shape), coarse_part.reshape(shape)


def solution(mesh):
    in_specs = (
        P("story", "plan", None, None, None, None, None),
        P("story", "plan", None, None, None, None),
        P("story", "plan", None, None),
        P("story", "plan", None, None, None, None),
        P("story", "plan", None, None, None, None),
        P(),
    )
    out_specs = (
        P("story", "plan", None, None, None, None),
        P("story", "plan", None, None, None, None),
    )
    return jax.shard_map(
        on_device, mesh=mesh, in_specs=in_specs, out_specs=out_specs, check_vma=False
    )
```

```python
import jax
import jax.numpy as jnp
from jax import lax
from jax.experimental import pallas as pl
from jax.experimental.pallas import tpu as pltpu
from jax.sharding import PartitionSpec as P

ITERS = 6
DAMPING = 0.3
BLK = 128
NBLK = 4
RHS = 64
FD = 512
CPD = 6
KC = 30
STORIES = 16
PLANS = 8
ROW = PLANS * CPD
NCOARSE = STORIES * ROW
MESH = pl.DeviceIdType.MESH
F32 = jnp.float32
BF16 = jnp.bfloat16


def iota(shape, dim):
    return lax.broadcasted_iota(jnp.int32, shape, dim)


def split(value):
    high = value.astype(BF16)
    return high, (value - high.astype(F32)).astype(BF16)


def dot(left, right):
    return jnp.dot(left, right, preferred_element_type=F32)


def dot_last(left, right):
    return lax.dot_general(left, right, (((1,), (1,)), ((), ())), preferred_element_type=F32)


def product(value, high, low, dot=dot):
    rows = value.shape[0]
    first, second = split(value)
    both = dot(jnp.concatenate([first, second], axis=0), high)
    return both[:rows] + both[rows:] + dot(first, low)


def fill(table, first, second):
    zero = jnp.zeros_like(first)
    for a, left in enumerate((zero, first, first.T)):
        for b, right in enumerate((zero, second, second.T)):
            table[3 * a + b] = left + right


def choice(pattern, side, q, t):
    index = 0
    for k in range(2):
        row, column = pattern[k, 0, side], pattern[k, 1, side]
        plain = jnp.where((row == q) & (column == t), 1, 0)
        turned = jnp.where((row == t) & (column == q), 2, 0)
        index = 3 * index + plain + turned
    return index


def place(pattern, side, table, diagonal, scales, high, low):
    for q in range(NBLK):
        for t in range(NBLK):
            if q == t:
                block = diagonal[q]
            else:
                block = table[choice(pattern, side, q, t)]
                if scales is not None:
                    block = block * scales[t]
            here = (pl.ds(q * BLK, BLK), pl.ds(t * BLK, BLK))
            high[here], low[here] = split(block)


def places(dof):
    group = (dof * 43) >> 8
    storey = jnp.where(group == 1, -1, jnp.where(group == 2, 1, 0))
    column = jnp.where(group == 4, 1, jnp.where(group == 3, PLANS - 1, 0))
    return storey, column, dof - CPD * group


def scatter(plan, shift):
    dof, lane = iota((32, 256), 0), iota((32, 256), 1)
    storey, column, member = places(dof)
    target = (storey + shift) * ROW + ((plan + column) & (PLANS - 1)) * CPD + member
    return jnp.where((lane == target) & (dof < KC), 1.0, 0.0)


def gather(plan):
    lane = iota((1, STORIES * 32), 1)
    dof = lane & 31
    storey, column, member = places(dof)
    storey = storey + (lane >> 5)
    target = storey * ROW + ((plan + column) & (PLANS - 1)) * CPD + member
    target = jnp.where((dof < KC) & (storey >= 0) & (storey < STORIES), target, -1)
    return jnp.where(iota((NCOARSE, STORIES * 32), 0) == target, 1.0, 0.0).astype(BF16)


def kernel(
    schur, pattern_far, owner_far, residual, basis, inverse,
    averaged, coarse_part,
    pattern, owner, raw, rows, local, slab, table, high, low, ready_high, ready_low,
    pack_out, pack_in, coupling_in, product_out, product_in, product_own, basis_in,
    wide, owned_high, owned_low, weight_high, weight_low, basis_pack, flag, flags,
    sent_first, got_first, sent_second, got_second,
    load_sem, face_send, face_recv, back_send, back_recv,
    send_flag, recv_flag, send_first, recv_first, send_second, recv_second, near, middle, far, last,
):
    story, plan = lax.axis_index("story"), lax.axis_index("plan")
    odd = lax.rem(plan, 2)
    step = 1 - 2 * odd
    in_side = (1 - odd, 3)
    out_side = (odd, 2)
    sides = (out_side[0], out_side[1], in_side[0], in_side[1])
    in_device = ((lax.rem(story + step + STORIES, STORIES), plan), (story, lax.rem(plan + 1, PLANS)))
    out_device = (
        (lax.rem(story - step + STORIES, STORIES), plan),
        (story, lax.rem(plan + PLANS - 1, PLANS)),
    )
    plan_peers = [(story, lax.rem(plan + r, PLANS)) for r in (4, 3, 5, 2, 6, 1, 7)]
    story_peers = [
        (lax.rem(story + r, STORIES), plan) for r in (10, 6, 9, 7, 11, 5, 8, 2, 14, 13, 3, 12, 4, 1, 15)
    ]

    barrier = pltpu.get_barrier_semaphore()

    def around(distance):
        peers = [(story, lax.rem(plan + r, PLANS)) for r in sorted({distance, PLANS - distance}) if 0 < r < PLANS]
        if distance > PLANS // 2:
            peers = []
        peers = [(None, peer) for peer in peers]
        peers.append((story >= distance, (lax.rem(story + STORIES - distance, STORIES), plan)))
        peers.append((story < STORIES - distance, (lax.rem(story + distance, STORIES), plan)))
        return peers

    def announce(semaphore, distance):
        for condition, peer in around(distance):
            def signal(peer=peer):
                pl.semaphore_signal(semaphore, inc=1, device_id=peer, device_id_type=MESH)

            if condition is None:
                signal()
            else:
                pl.when(condition)(signal)

    def hear(semaphore, distance):
        count = 0
        for condition, _ in around(distance):
            count = count + (1 if condition is None else jnp.where(condition, 1, 0))
        pl.semaphore_wait(semaphore, count)

    announce(barrier, 1)

    small = (
        pltpu.make_async_copy(pattern_far, pattern, load_sem.at[10]),
        pltpu.make_async_copy(owner_far, owner, load_sem.at[11]),
    )
    loads = []
    for k in range(4):
        loads.append(pltpu.make_async_copy(schur.at[sides[k]], raw.at[k], load_sem.at[k]))
        loads.append(pltpu.make_async_copy(residual.at[sides[k]], rows.at[k], load_sem.at[4 + k]))
    loads.append(pltpu.make_async_copy(basis, local, load_sem.at[8]))
    lowest = jnp.clip(story - 2, 0, STORIES - 5)
    loads.append(
        pltpu.make_async_copy(
            inverse.at[pl.ds(pl.multiple_of(lowest * ROW, 8), 5 * ROW)], slab, load_sem.at[9]
        )
    )
    for load in loads[:4]:
        load.start()

    line, lane = iota((BLK, BLK), 0), iota((BLK, BLK), 1)
    upper, equal = line <= lane, line == lane

    def diagonal_of(block):
        return jnp.sum(jnp.where(equal, block, 0.0), axis=0, keepdims=True)

    def to_sharer(f, m, source, target):
        return pltpu.make_async_remote_copy(
            src_ref=source, dst_ref=target, send_sem=face_send.at[f, m], recv_sem=face_recv.at[f, m],
            device_id=out_device[f], device_id_type=MESH,
        )

    def exchange(peers, source, target, send_sem, recv_sem):
        copies = []
        for r, peer in enumerate(peers):
            copies.append(
                pltpu.make_async_remote_copy(
                    src_ref=source(peer), dst_ref=target, send_sem=send_sem.at[r],
                    recv_sem=recv_sem.at[r], device_id=peer, device_id_type=MESH,
                )
            )
            copies[-1].start()
        return copies

    hear(barrier, 1)
    couplings = [
        to_sharer(f, 1, schur.at[out_side[f], pl.ds(NBLK, 2)], coupling_in.at[f]) for f in range(2)
    ]
    packs = [to_sharer(f, 0, pack_out.at[f], pack_in.at[f]) for f in range(2)]
    products = [to_sharer(f, 2, product_out.at[f], product_in.at[f]) for f in range(2)]
    bases = [to_sharer(f, 3, basis.at[out_side[f]], basis_in.at[f]) for f in range(2)]
    exists = jnp.where(odd == 0, story < STORIES - 1, story > 0)
    leaves = jnp.where(odd == 0, story > 0, story < STORIES - 1)

    def when(condition, f, action):
        if f == 0:
            pl.when(condition)(action)
        else:
            action()

    for f in range(2):
        when(leaves, f, couplings[f].start)
    for load in list(small) + loads[4:]:
        load.start()

    for f in range(2):
        loads[2 * f].wait()
        for h in range(2):
            first, second = raw[f, 2 * h], raw[f, 2 * h + 1]
            pack_out[f, h * BLK : (h + 1) * BLK] = jnp.where(upper, first, second)
            pack_out[f, 2 * BLK + h : 2 * BLK + h + 1] = diagonal_of(second)
        pack_out[f, 2 * BLK + 2 : 2 * BLK + 8] = jnp.zeros((6, BLK), F32)
        when(leaves, f, packs[f].start)
        when(leaves, f, bases[f].start)
    announce(near, 1)

    for copy in small:
        copy.wait()
    mine = [owner[0, in_side[f]].astype(F32) for f in range(2)]
    for f in range(2):
        flag[f : f + 1] = jnp.full((1, BLK), mine[f], F32)
    flag[2:8] = jnp.zeros((6, BLK), F32)
    flags[plan] = flag[...]

    for k in range(4):
        if k >= 2:
            loads[2 * k].wait()
        loads[2 * k + 1].wait()
        fill(table, raw[k, NBLK], raw[k, NBLK + 1])
        place(pattern, sides[k], table, [raw[k, n] for n in range(NBLK)], None, high, low)
        target = product_out.at[k] if k < 2 else product_own.at[k - 2]
        target[...] = product(rows[k], high[...], low[...])
        if k < 2:
            when(leaves, k, products[k].start)
    hear(near, 1)
    announce(middle, 2)

    present = (jnp.where(story > 0, 1.0, 0.0), jnp.where(story < STORIES - 1, 1.0, 0.0), 1.0, 1.0)
    loads[8].wait()
    wide[...] = jnp.zeros_like(wide)

    def widen(source, s, target):
        for n in range(NBLK):
            wide[target, 0:KC, n * BLK : (n + 1) * BLK] = source[s, pl.ds(n, KC, stride=NBLK)]

    for s in range(4):
        widen(local, s, s)
        basis_high, basis_low = split(wide[s] * present[s])
        here = pl.ds(s * FD, FD)
        basis_pack[:, here] = jnp.concatenate(
            [basis_high, basis_high, basis_low, jnp.zeros_like(basis_low)], axis=0
        )

    loads[9].wait()
    slab_high, slab_low = split(jnp.concatenate([slab[...], jnp.zeros((16, NCOARSE), F32)], axis=0))
    columns = dot(jnp.concatenate([slab_high, slab_low], axis=0), gather(plan)).astype(BF16)
    hear(middle, 2)
    announce(far, 4)
    noted = exchange(plan_peers, lambda peer: flag, flags.at[plan], send_flag, recv_flag)
    scaled = []
    for f in range(2):
        when(exists, f, packs[f].wait_recv)
        when(exists, f, couplings[f].wait_recv)
        diagonal, scales = [], []
        for h in range(2):
            first, second = raw[2 + f, 2 * h], raw[2 + f, 2 * h + 1]
            packed = jnp.where(upper, first, second) + pack_in[f, h * BLK : (h + 1) * BLK]
            turned = packed.T
            second_diagonal = diagonal_of(second) + pack_in[f, 2 * BLK + h : 2 * BLK + h + 1]
            scales += [-DAMPING / diagonal_of(packed), -DAMPING / second_diagonal]
            diagonal.append(
                jnp.where(equal, 1.0 - DAMPING, jnp.where(upper, packed, turned) * scales[-2])
            )
            diagonal.append(
                jnp.where(equal, 1.0 - DAMPING, jnp.where(upper, turned, packed) * scales[-1])
            )
        fill(
            table,
            raw[2 + f, NBLK] + coupling_in[f, 0],
            raw[2 + f, NBLK + 1] + coupling_in[f, 1],
        )
        place(pattern, in_side[f], table, diagonal, scales, ready_high.at[f], ready_low.at[f])
        scaled.append(jnp.concatenate(scales, axis=1))

    def sweeps(start):
        values = start
        for _ in range(ITERS - 1):
            values = [start[f] + product(values[f], ready_high[f], ready_low[f]) for f in range(2)]
        return values

    owned_high[...] = jnp.zeros_like(owned_high)
    owned_low[...] = jnp.zeros_like(owned_low)
    shares = []
    for f in range(2):
        when(exists, f, bases[f].wait_recv)
        widen(basis_in, f, 4 + f)
        share = wide[in_side[f]] * mine[f] + wide[4 + f] * (1.0 - mine[f])
        shares.append(-share * scaled[f])
    shares = sweeps(shares)
    shares[0] = jnp.where(exists, shares[0], 0.0)
    for f in range(2):
        share_high, share_low = split(shares[f])
        for n in range(2):
            here = (pl.ds(64 * n + 32 * f, 32), pl.ds(f * FD, FD))
            owned_high[here], owned_low[here] = share_high, share_low

    right_side = []
    for f in range(2):
        when(exists, f, products[f].wait_recv)
        right_side.append(product_own[f] + product_in[f])
    right_side[0] = jnp.where(exists, right_side[0], 0.0)
    values = jnp.concatenate(right_side, axis=1)
    contribution = product(values, owned_high[...], owned_low[...], dot_last)
    left = iota((RHS // 2, BLK), 1) < 64
    packed = jnp.where(left, contribution[: RHS // 2], contribution[RHS // 2 :])
    sent_first[...] = packed
    firsts = exchange(plan_peers, lambda peer: sent_first, got_first.at[plan], send_first, recv_first)

    solved = sweeps([-right_side[f] * scaled[f] for f in range(2)])
    solved[0] = jnp.where(exists, solved[0], 0.0)
    for f in range(2):
        averaged[in_side[f]] = solved[f]

    def to_owner(f):
        return pltpu.make_async_remote_copy(
            src_ref=averaged.at[in_side[f]], dst_ref=averaged.at[out_side[f]],
            send_sem=back_send.at[f], recv_sem=back_recv.at[f],
            device_id=in_device[f], device_id_type=MESH,
        )

    backs = [to_owner(f) for f in range(2)]
    when(exists, 0, backs[0].start)

    @pl.when(jnp.logical_not(leaves))
    def _():
        averaged[out_side[0]] = jnp.zeros((RHS, FD), F32)


    got_first[plan] = packed
    hear(far, 4)
    announce(last, 8)
    for copy in noted:
        copy.wait_recv()
    height = story - lowest
    chosen = []
    for p in range(PLANS):
        for f in range(2):
            kept = jnp.concatenate([flags[p, f : f + 1]] * 2, axis=1)
            other = scatter(p, height + 1 - 2 * (p % 2)) if f == 0 else scatter(p + 1, height)
            chosen.append((scatter(p, height) * kept + other * (1.0 - kept)).astype(BF16))
    chosen = jnp.concatenate(chosen, axis=0)
    weight_high[...] = dot(chosen, columns[:256]).astype(BF16)
    weight_low[...] = dot(chosen, columns[256:]).astype(BF16)
    for copy in firsts:
        copy.wait_recv()
    halves = ([], [])
    for p in range(0, PLANS, 2):
        first, second = got_first[p], got_first[p + 1]
        halves[0].append(jnp.where(left, first, pltpu.roll(second, 64, 1)))
        halves[1].append(jnp.where(left, pltpu.roll(first, 64, 1), second))
    gathered = jnp.concatenate([jnp.concatenate(half, axis=1) for half in halves], axis=0)
    coarse = product(gathered, weight_high[...], weight_low[...])
    quarter = iota((16, BLK), 1) >> 5
    for n in range(STORIES // 4):
        tile = coarse[:, n * BLK : (n + 1) * BLK]
        turned = [pltpu.roll(tile, 32 * g, 1) if g else tile for g in range(4)]
        for q in range(4):
            message = turned[(3 - q) % 4][48:64]
            for g in range(3):
                message = jnp.where(quarter == g, turned[(g - q) % 4][16 * g : 16 * g + 16], message)
            sent_second[4 * n + q] = message
    hear(last, 8)
    seconds = exchange(
        story_peers, lambda peer: sent_second.at[peer[0]], got_second.at[story], send_second, recv_second
    )
    backs[1].start()
    got_second[story] = sent_second[story]
    for copy in seconds:
        copy.wait_recv()
    total = got_second[0]
    for i in range(1, STORIES):
        total = total + got_second[i]
    parts = [total] + [pltpu.roll(total, BLK - 32 * g, 1) for g in range(1, 4)]
    needed = jnp.concatenate(parts, axis=0)
    needed = jnp.where(iota((RHS, BLK), 1) < 32, needed, 0.0)
    needed_high, needed_low = split(needed)
    needed_high, needed_low = needed_high.astype(F32), needed_low.astype(F32)
    operand = needed_high + pltpu.roll(needed_low, 32, 1) + pltpu.roll(needed_high, 64, 1)
    operand = operand.astype(BF16)
    for s in range(4):
        coarse_part[s] = dot(operand, basis_pack[:, s * FD : (s + 1) * FD])

    for copies in (packs, couplings, products, bases):
        for f in range(2):
            when(leaves, f, copies[f].wait_send)
    for copy in noted + firsts + seconds:
        copy.wait_send()
    for f in range(2):
        when(exists, f, backs[f].wait_send)
        when(leaves, f, backs[f].wait_recv)


def store(averaged, coarse_part, averaged_out, coarse_part_out, sem):
    copies = []
    for s in range(4):
        copies.append(pltpu.make_async_copy(averaged.at[s], averaged_out.at[s], sem.at[0, s]))
        copies.append(pltpu.make_async_copy(coarse_part.at[s], coarse_part_out.at[s], sem.at[1, s]))
    for copy in copies:
        copy.start()
    for copy in copies:
        copy.wait()


def on_device(schur_blocks, off_pattern, face_owner, residual, coarse_basis, coarse_inverse):
    hbm = pl.BlockSpec(memory_space=pltpu.HBM)
    operands = [
        pltpu.with_memory_space_constraint(operand, pltpu.HBM)
        for operand in (
            schur_blocks.reshape(4, 6, BLK, BLK),
            off_pattern.reshape(4, 2, 2).transpose(1, 2, 0),
            face_owner.reshape(1, 4),
            residual.reshape(4, RHS, FD),
            coarse_basis.reshape(4, KC * NBLK, BLK),
            coarse_inverse,
        )
    ]
    vmem = pl.BlockSpec(memory_space=pltpu.VMEM)
    dma = pltpu.SemaphoreType.DMA
    out = pltpu.VMEM((4, RHS, FD), F32)
    averaged, coarse_part = pl.pallas_call(
        kernel,
        out_shape=(out, out),
        in_specs=[hbm] * 6,
        out_specs=(vmem, vmem),
        scratch_shapes=[
            pltpu.SMEM((2, 2, 4), jnp.int32),
            pltpu.SMEM((1, 4), jnp.int32),
            pltpu.VMEM((4, 6, BLK, BLK), F32),
            pltpu.VMEM((4, RHS, FD), F32),
            pltpu.VMEM((4, KC * NBLK, BLK), F32),
            pltpu.VMEM((5 * ROW, NCOARSE), F32),
            pltpu.VMEM((9, BLK, BLK), F32),
            pltpu.VMEM((FD, FD), BF16),
            pltpu.VMEM((FD, FD), BF16),
            pltpu.VMEM((2, FD, FD), BF16),
            pltpu.VMEM((2, FD, FD), BF16),
            pltpu.VMEM((2, 2 * BLK + 8, BLK), F32),
            pltpu.VMEM((2, 2 * BLK + 8, BLK), F32),
            pltpu.VMEM((2, 2, BLK, BLK), F32),
            pltpu.VMEM((2, RHS, FD), F32),
            pltpu.VMEM((2, RHS, FD), F32),
            pltpu.VMEM((2, RHS, FD), F32),
            pltpu.VMEM((2, KC * NBLK, BLK), F32),
            pltpu.VMEM((6, 32, FD), F32),
            pltpu.VMEM((BLK, 2 * FD), BF16),
            pltpu.VMEM((BLK, 2 * FD), BF16),
            pltpu.VMEM((PLANS * 64, STORIES * 32), BF16),
            pltpu.VMEM((PLANS * 64, STORIES * 32), BF16),
            pltpu.VMEM((BLK, 4 * FD), BF16),
            pltpu.VMEM((8, BLK), F32),
            pltpu.VMEM((PLANS, 8, BLK), F32),
            pltpu.VMEM((RHS // 2, BLK), F32),
            pltpu.VMEM((PLANS, RHS // 2, BLK), F32),
            pltpu.VMEM((STORIES, 16, BLK), F32),
            pltpu.VMEM((STORIES, 16, BLK), F32),
            dma((12,)),
            dma((2, 4)),
            dma((2, 4)),
            dma((2,)),
            dma((2,)),
            dma((PLANS - 1,)),
            dma((PLANS - 1,)),
            dma((PLANS - 1,)),
            dma((PLANS - 1,)),
            dma((STORIES - 1,)),
            dma((STORIES - 1,)),
            pltpu.SemaphoreType.REGULAR,
            pltpu.SemaphoreType.REGULAR,
            pltpu.SemaphoreType.REGULAR,
            pltpu.SemaphoreType.REGULAR,
        ],
        compiler_params=pltpu.CompilerParams(
            collective_id=0, has_side_effects=True, vmem_limit_bytes=40 * 1024 * 1024
        ),
    )(*operands)
    free = pl.BlockSpec(memory_space=pl.ANY)
    out = pltpu.HBM((4, RHS, FD), F32)
    averaged, coarse_part = pl.pallas_call(
        store,
        out_shape=(out, out),
        in_specs=[free, free],
        out_specs=(free, free),
        scratch_shapes=[dma((2, 4))],
    )(*[pltpu.with_memory_space_constraint(value, pltpu.VMEM) for value in (averaged, coarse_part)])
    shape = (1, 1, 4, 1, RHS, FD)
    return averaged.reshape(shape), coarse_part.reshape(shape)


def solution(mesh):
    in_specs = (
        P("story", "plan", None, None, None, None, None),
        P("story", "plan", None, None, None, None),
        P("story", "plan", None, None),
        P("story", "plan", None, None, None, None),
        P("story", "plan", None, None, None, None),
        P(),
    )
    out_specs = (
        P("story", "plan", None, None, None, None),
        P("story", "plan", None, None, None, None),
    )
    return jax.shard_map(
        on_device, mesh=mesh, in_specs=in_specs, out_specs=out_specs, check_vma=False
    )
```

```python
import jax
import jax.numpy as jnp
from jax import lax
from jax.experimental import pallas as pl
from jax.experimental.pallas import tpu as pltpu
from jax.sharding import PartitionSpec as P

ITERS = 6
DAMPING = 0.3
BLK = 128
NBLK = 4
RHS = 64
FD = 512
CPD = 6
KC = 30
STORIES = 16
PLANS = 8
ROW = PLANS * CPD
NCOARSE = STORIES * ROW
MESH = pl.DeviceIdType.MESH
F32 = jnp.float32
BF16 = jnp.bfloat16


def iota(shape, dim):
    return lax.broadcasted_iota(jnp.int32, shape, dim)


def split(value):
    high = value.astype(BF16)
    return high, (value - high.astype(F32)).astype(BF16)


def dot(left, right):
    return jnp.dot(left, right, preferred_element_type=F32)


def dot_last(left, right):
    return lax.dot_general(left, right, (((1,), (1,)), ((), ())), preferred_element_type=F32)


def product(value, high, low, dot=dot):
    rows = value.shape[0]
    first, second = split(value)
    both = dot(jnp.concatenate([first, second], axis=0), high)
    return both[:rows] + both[rows:] + dot(first, low)


def fill(table, first, second):
    zero = jnp.zeros_like(first)
    for a, left in enumerate((zero, first, first.T)):
        for b, right in enumerate((zero, second, second.T)):
            table[3 * a + b] = left + right


def choice(pattern, side, q, t):
    index = 0
    for k in range(2):
        row, column = pattern[k, 0, side], pattern[k, 1, side]
        plain = jnp.where((row == q) & (column == t), 1, 0)
        turned = jnp.where((row == t) & (column == q), 2, 0)
        index = 3 * index + plain + turned
    return index


def place(pattern, side, table, diagonal, scales, high, low):
    for q in range(NBLK):
        for t in range(NBLK):
            if q == t:
                block = diagonal[q]
            else:
                block = table[choice(pattern, side, q, t)]
                if scales is not None:
                    block = block * scales[t]
            here = (pl.ds(q * BLK, BLK), pl.ds(t * BLK, BLK))
            high[here], low[here] = split(block)


def places(dof):
    group = (dof * 43) >> 8
    storey = jnp.where(group == 1, -1, jnp.where(group == 2, 1, 0))
    column = jnp.where(group == 4, 1, jnp.where(group == 3, PLANS - 1, 0))
    return storey, column, dof - CPD * group


def scatter(plan, shift):
    dof, lane = iota((32, 256), 0), iota((32, 256), 1)
    storey, column, member = places(dof)
    target = (storey + shift) * ROW + ((plan + column) & (PLANS - 1)) * CPD + member
    return jnp.where((lane == target) & (dof < KC), 1.0, 0.0)


def gather(plan):
    lane = iota((1, STORIES * 32), 1)
    dof = lane & 31
    storey, column, member = places(dof)
    storey = storey + (lane >> 5)
    target = storey * ROW + ((plan + column) & (PLANS - 1)) * CPD + member
    target = jnp.where((dof < KC) & (storey >= 0) & (storey < STORIES), target, -1)
    return jnp.where(iota((NCOARSE, STORIES * 32), 0) == target, 1.0, 0.0).astype(BF16)


def kernel(
    schur, pattern_far, owner_far, residual, basis, inverse,
    averaged, coarse_part,
    pattern, owner, raw, rows, local, slab, table, high, low, ready_high, ready_low,
    pack_out, pack_in, coupling_in, product_out, product_in, product_own, basis_in,
    wide, owned_high, owned_low, weight_high, weight_low, basis_pack, flag, flags,
    sent_first, got_first, sent_second, got_second,
    load_sem, face_send, face_recv, back_send, back_recv,
    send_flag, recv_flag, send_first, recv_first, send_second, recv_second, near, middle, far, last,
):
    story, plan = lax.axis_index("story"), lax.axis_index("plan")
    odd = lax.rem(plan, 2)
    step = 1 - 2 * odd
    in_side = (1 - odd, 3)
    out_side = (odd, 2)
    sides = (out_side[0], out_side[1], in_side[0], in_side[1])
    in_device = ((lax.rem(story + step + STORIES, STORIES), plan), (story, lax.rem(plan + 1, PLANS)))
    out_device = (
        (lax.rem(story - step + STORIES, STORIES), plan),
        (story, lax.rem(plan + PLANS - 1, PLANS)),
    )
    plan_peers = [(story, lax.rem(plan + r, PLANS)) for r in (4, 3, 5, 2, 6, 1, 7)]
    story_peers = [
        (lax.rem(story + r, STORIES), plan) for r in (10, 6, 9, 7, 11, 5, 8, 2, 14, 13, 3, 12, 4, 1, 15)
    ]

    barrier = pltpu.get_barrier_semaphore()

    def around(distance):
        peers = [
            (story >= distance, (lax.rem(story + STORIES - distance, STORIES), plan)),
            (story < STORIES - distance, (lax.rem(story + distance, STORIES), plan)),
        ]
        if distance <= PLANS // 2:
            for r in sorted({distance, PLANS - distance}):
                peers.append((None, (story, lax.rem(plan + r, PLANS))))
        return peers

    def announce(semaphore, distance):
        for condition, peer in around(distance):
            def signal(peer=peer):
                pl.semaphore_signal(semaphore, inc=1, device_id=peer, device_id_type=MESH)

            if condition is None:
                signal()
            else:
                pl.when(condition)(signal)

    def hear(semaphore, distance):
        count = 0
        for condition, _ in around(distance):
            count = count + (1 if condition is None else jnp.where(condition, 1, 0))
        pl.semaphore_wait(semaphore, count)

    announce(barrier, 1)

    small = (
        pltpu.make_async_copy(pattern_far, pattern, load_sem.at[10]),
        pltpu.make_async_copy(owner_far, owner, load_sem.at[11]),
    )
    loads = []
    for k in range(4):
        loads.append(pltpu.make_async_copy(schur.at[sides[k]], raw.at[k], load_sem.at[k]))
        loads.append(pltpu.make_async_copy(residual.at[sides[k]], rows.at[k], load_sem.at[4 + k]))
    loads.append(pltpu.make_async_copy(basis, local, load_sem.at[8]))
    lowest = jnp.clip(story - 2, 0, STORIES - 5)
    loads.append(
        pltpu.make_async_copy(
            inverse.at[pl.ds(pl.multiple_of(lowest * ROW, 8), 5 * ROW)], slab, load_sem.at[9]
        )
    )
    for load in loads[:4]:
        load.start()

    line, lane = iota((BLK, BLK), 0), iota((BLK, BLK), 1)
    upper, equal = line <= lane, line == lane

    def diagonal_of(block):
        return jnp.sum(jnp.where(equal, block, 0.0), axis=0, keepdims=True)

    def to_sharer(f, m, source, target):
        return pltpu.make_async_remote_copy(
            src_ref=source, dst_ref=target, send_sem=face_send.at[f, m], recv_sem=face_recv.at[f, m],
            device_id=out_device[f], device_id_type=MESH,
        )

    def exchange(peers, source, target, send_sem, recv_sem):
        copies = []
        for r, peer in enumerate(peers):
            copies.append(
                pltpu.make_async_remote_copy(
                    src_ref=source(peer), dst_ref=target, send_sem=send_sem.at[r],
                    recv_sem=recv_sem.at[r], device_id=peer, device_id_type=MESH,
                )
            )
            copies[-1].start()
        return copies

    hear(barrier, 1)
    couplings = [
        to_sharer(f, 1, schur.at[out_side[f], pl.ds(NBLK, 2)], coupling_in.at[f]) for f in range(2)
    ]
    packs = [to_sharer(f, 0, pack_out.at[f], pack_in.at[f]) for f in range(2)]
    products = [to_sharer(f, 2, product_out.at[f], product_in.at[f]) for f in range(2)]
    bases = [to_sharer(f, 3, basis.at[out_side[f]], basis_in.at[f]) for f in range(2)]
    exists = jnp.where(odd == 0, story < STORIES - 1, story > 0)
    leaves = jnp.where(odd == 0, story > 0, story < STORIES - 1)

    def when(condition, f, action):
        if f == 0:
            pl.when(condition)(action)
        else:
            action()

    for f in range(2):
        when(leaves, f, couplings[f].start)
    for load in list(small) + loads[4:]:
        load.start()

    for f in range(2):
        loads[2 * f].wait()
        for h in range(2):
            first, second = raw[f, 2 * h], raw[f, 2 * h + 1]
            pack_out[f, h * BLK : (h + 1) * BLK] = jnp.where(upper, first, second)
            pack_out[f, 2 * BLK + h : 2 * BLK + h + 1] = diagonal_of(second)
        pack_out[f, 2 * BLK + 2 : 2 * BLK + 8] = jnp.zeros((6, BLK), F32)
        when(leaves, f, packs[f].start)
        when(leaves, f, bases[f].start)
    announce(near, 1)

    for copy in small:
        copy.wait()
    mine = [owner[0, in_side[f]].astype(F32) for f in range(2)]
    for f in range(2):
        flag[f : f + 1] = jnp.full((1, BLK), mine[f], F32)
    flag[2:8] = jnp.zeros((6, BLK), F32)
    flags[plan] = flag[...]

    for k in range(4):
        if k >= 2:
            loads[2 * k].wait()
        loads[2 * k + 1].wait()
        fill(table, raw[k, NBLK], raw[k, NBLK + 1])
        place(pattern, sides[k], table, [raw[k, n] for n in range(NBLK)], None, high, low)
        target = product_out.at[k] if k < 2 else product_own.at[k - 2]
        target[...] = product(rows[k], high[...], low[...])
        if k < 2:
            when(leaves, k, products[k].start)
    hear(near, 1)
    announce(middle, 2)

    present = (jnp.where(story > 0, 1.0, 0.0), jnp.where(story < STORIES - 1, 1.0, 0.0), 1.0, 1.0)
    loads[8].wait()
    wide[...] = jnp.zeros_like(wide)

    def widen(source, s, target):
        for n in range(NBLK):
            wide[target, 0:KC, n * BLK : (n + 1) * BLK] = source[s, pl.ds(n, KC, stride=NBLK)]

    for s in range(4):
        widen(local, s, s)
        basis_high, basis_low = split(wide[s] * present[s])
        here = pl.ds(s * FD, FD)
        basis_pack[:, here] = jnp.concatenate(
            [basis_high, basis_high, basis_low, jnp.zeros_like(basis_low)], axis=0
        )

    loads[9].wait()
    slab_high, slab_low = split(jnp.concatenate([slab[...], jnp.zeros((16, NCOARSE), F32)], axis=0))
    columns = dot(jnp.concatenate([slab_high, slab_low], axis=0), gather(plan)).astype(BF16)
    hear(middle, 2)
    announce(far, 4)
    noted = exchange(plan_peers, lambda peer: flag, flags.at[plan], send_flag, recv_flag)
    def sweeps(start, f):
        values = start
        for _ in range(ITERS - 1):
            values = start + product(values, ready_high[f], ready_low[f])
        return values

    def both_sweeps(start):
        values = start
        for _ in range(ITERS - 1):
            values = [start[f] + product(values[f], ready_high[f], ready_low[f]) for f in range(2)]
        return values

    owned_high[...] = jnp.zeros_like(owned_high)
    owned_low[...] = jnp.zeros_like(owned_low)
    scaled = [None, None]
    for f in (1, 0):
        when(exists, f, packs[f].wait_recv)
        when(exists, f, couplings[f].wait_recv)
        diagonal, scales = [], []
        for h in range(2):
            first, second = raw[2 + f, 2 * h], raw[2 + f, 2 * h + 1]
            packed = jnp.where(upper, first, second) + pack_in[f, h * BLK : (h + 1) * BLK]
            turned = packed.T
            second_diagonal = diagonal_of(second) + pack_in[f, 2 * BLK + h : 2 * BLK + h + 1]
            scales += [-DAMPING / diagonal_of(packed), -DAMPING / second_diagonal]
            diagonal.append(
                jnp.where(equal, 1.0 - DAMPING, jnp.where(upper, packed, turned) * scales[-2])
            )
            diagonal.append(
                jnp.where(equal, 1.0 - DAMPING, jnp.where(upper, turned, packed) * scales[-1])
            )
        fill(
            table,
            raw[2 + f, NBLK] + coupling_in[f, 0],
            raw[2 + f, NBLK + 1] + coupling_in[f, 1],
        )
        place(pattern, in_side[f], table, diagonal, scales, ready_high.at[f], ready_low.at[f])
        scaled[f] = jnp.concatenate(scales, axis=1)
        when(exists, f, bases[f].wait_recv)
        widen(basis_in, f, 4 + f)
        share = wide[in_side[f]] * mine[f] + wide[4 + f] * (1.0 - mine[f])
        share = sweeps(-share * scaled[f], f)
        if f == 0:
            share = jnp.where(exists, share, 0.0)
        share_high, share_low = split(share)
        for n in range(2):
            here = (pl.ds(64 * n + 32 * f, 32), pl.ds(f * FD, FD))
            owned_high[here], owned_low[here] = share_high, share_low

    right_side = []
    for f in range(2):
        when(exists, f, products[f].wait_recv)
        right_side.append(product_own[f] + product_in[f])
    right_side[0] = jnp.where(exists, right_side[0], 0.0)
    values = jnp.concatenate(right_side, axis=1)
    contribution = product(values, owned_high[...], owned_low[...], dot_last)
    left = iota((RHS // 2, BLK), 1) < 64
    packed = jnp.where(left, contribution[: RHS // 2], contribution[RHS // 2 :])
    sent_first[...] = packed
    firsts = exchange(plan_peers, lambda peer: sent_first, got_first.at[plan], send_first, recv_first)

    solved = both_sweeps([-right_side[f] * scaled[f] for f in range(2)])
    solved[0] = jnp.where(exists, solved[0], 0.0)
    for f in range(2):
        averaged[in_side[f]] = solved[f]

    def to_owner(f):
        return pltpu.make_async_remote_copy(
            src_ref=averaged.at[in_side[f]], dst_ref=averaged.at[out_side[f]],
            send_sem=back_send.at[f], recv_sem=back_recv.at[f],
            device_id=in_device[f], device_id_type=MESH,
        )

    backs = [to_owner(f) for f in range(2)]
    when(exists, 0, backs[0].start)

    @pl.when(jnp.logical_not(leaves))
    def _():
        averaged[out_side[0]] = jnp.zeros((RHS, FD), F32)


    got_first[plan] = packed
    hear(far, 4)
    announce(last, 8)
    for copy in noted:
        copy.wait_recv()
    height = story - lowest
    chosen = []
    for p in range(PLANS):
        for f in range(2):
            kept = jnp.concatenate([flags[p, f : f + 1]] * 2, axis=1)
            other = scatter(p, height + 1 - 2 * (p % 2)) if f == 0 else scatter(p + 1, height)
            chosen.append((scatter(p, height) * kept + other * (1.0 - kept)).astype(BF16))
    chosen = jnp.concatenate(chosen, axis=0)
    weight_high[...] = dot(chosen, columns[:256]).astype(BF16)
    weight_low[...] = dot(chosen, columns[256:]).astype(BF16)
    for copy in firsts:
        copy.wait_recv()
    halves = ([], [])
    for p in range(0, PLANS, 2):
        first, second = got_first[p], got_first[p + 1]
        halves[0].append(jnp.where(left, first, pltpu.roll(second, 64, 1)))
        halves[1].append(jnp.where(left, pltpu.roll(first, 64, 1), second))
    gathered = jnp.concatenate([jnp.concatenate(half, axis=1) for half in halves], axis=0)
    coarse = product(gathered, weight_high[...], weight_low[...])
    quarter = iota((16, BLK), 1) >> 5
    for n in range(STORIES // 4):
        tile = coarse[:, n * BLK : (n + 1) * BLK]
        turned = [pltpu.roll(tile, 32 * g, 1) if g else tile for g in range(4)]
        for q in range(4):
            message = turned[(3 - q) % 4][48:64]
            for g in range(3):
                message = jnp.where(quarter == g, turned[(g - q) % 4][16 * g : 16 * g + 16], message)
            sent_second[4 * n + q] = message
    hear(last, 8)
    seconds = exchange(
        story_peers, lambda peer: sent_second.at[peer[0]], got_second.at[story], send_second, recv_second
    )
    backs[1].start()
    got_second[story] = sent_second[story]
    for copy in seconds:
        copy.wait_recv()
    total = got_second[0]
    for i in range(1, STORIES):
        total = total + got_second[i]
    parts = [total] + [pltpu.roll(total, BLK - 32 * g, 1) for g in range(1, 4)]
    needed = jnp.concatenate(parts, axis=0)
    needed = jnp.where(iota((RHS, BLK), 1) < 32, needed, 0.0)
    needed_high, needed_low = split(needed)
    needed_high, needed_low = needed_high.astype(F32), needed_low.astype(F32)
    operand = needed_high + pltpu.roll(needed_low, 32, 1) + pltpu.roll(needed_high, 64, 1)
    operand = operand.astype(BF16)
    for s in range(4):
        coarse_part[s] = dot(operand, basis_pack[:, s * FD : (s + 1) * FD])

    for copies in (packs, couplings, products, bases):
        for f in range(2):
            when(leaves, f, copies[f].wait_send)
    for copy in noted + firsts + seconds:
        copy.wait_send()
    for f in range(2):
        when(exists, f, backs[f].wait_send)
        when(leaves, f, backs[f].wait_recv)


def store(averaged, coarse_part, averaged_out, coarse_part_out, sem):
    copies = []
    for s in range(4):
        copies.append(pltpu.make_async_copy(averaged.at[s], averaged_out.at[s], sem.at[0, s]))
        copies.append(pltpu.make_async_copy(coarse_part.at[s], coarse_part_out.at[s], sem.at[1, s]))
    for copy in copies:
        copy.start()
    for copy in copies:
        copy.wait()


def on_device(schur_blocks, off_pattern, face_owner, residual, coarse_basis, coarse_inverse):
    hbm = pl.BlockSpec(memory_space=pltpu.HBM)
    operands = [
        pltpu.with_memory_space_constraint(operand, pltpu.HBM)
        for operand in (
            schur_blocks.reshape(4, 6, BLK, BLK),
            off_pattern.reshape(4, 2, 2).transpose(1, 2, 0),
            face_owner.reshape(1, 4),
            residual.reshape(4, RHS, FD),
            coarse_basis.reshape(4, KC * NBLK, BLK),
            coarse_inverse,
        )
    ]
    vmem = pl.BlockSpec(memory_space=pltpu.VMEM)
    dma = pltpu.SemaphoreType.DMA
    out = pltpu.VMEM((4, RHS, FD), F32)
    averaged, coarse_part = pl.pallas_call(
        kernel,
        out_shape=(out, out),
        in_specs=[hbm] * 6,
        out_specs=(vmem, vmem),
        scratch_shapes=[
            pltpu.SMEM((2, 2, 4), jnp.int32),
            pltpu.SMEM((1, 4), jnp.int32),
            pltpu.VMEM((4, 6, BLK, BLK), F32),
            pltpu.VMEM((4, RHS, FD), F32),
            pltpu.VMEM((4, KC * NBLK, BLK), F32),
            pltpu.VMEM((5 * ROW, NCOARSE), F32),
            pltpu.VMEM((9, BLK, BLK), F32),
            pltpu.VMEM((FD, FD), BF16),
            pltpu.VMEM((FD, FD), BF16),
            pltpu.VMEM((2, FD, FD), BF16),
            pltpu.VMEM((2, FD, FD), BF16),
            pltpu.VMEM((2, 2 * BLK + 8, BLK), F32),
            pltpu.VMEM((2, 2 * BLK + 8, BLK), F32),
            pltpu.VMEM((2, 2, BLK, BLK), F32),
            pltpu.VMEM((2, RHS, FD), F32),
            pltpu.VMEM((2, RHS, FD), F32),
            pltpu.VMEM((2, RHS, FD), F32),
            pltpu.VMEM((2, KC * NBLK, BLK), F32),
            pltpu.VMEM((6, 32, FD), F32),
            pltpu.VMEM((BLK, 2 * FD), BF16),
            pltpu.VMEM((BLK, 2 * FD), BF16),
            pltpu.VMEM((PLANS * 64, STORIES * 32), BF16),
            pltpu.VMEM((PLANS * 64, STORIES * 32), BF16),
            pltpu.VMEM((BLK, 4 * FD), BF16),
            pltpu.VMEM((8, BLK), F32),
            pltpu.VMEM((PLANS, 8, BLK), F32),
            pltpu.VMEM((RHS // 2, BLK), F32),
            pltpu.VMEM((PLANS, RHS // 2, BLK), F32),
            pltpu.VMEM((STORIES, 16, BLK), F32),
            pltpu.VMEM((STORIES, 16, BLK), F32),
            dma((12,)),
            dma((2, 4)),
            dma((2, 4)),
            dma((2,)),
            dma((2,)),
            dma((PLANS - 1,)),
            dma((PLANS - 1,)),
            dma((PLANS - 1,)),
            dma((PLANS - 1,)),
            dma((STORIES - 1,)),
            dma((STORIES - 1,)),
            pltpu.SemaphoreType.REGULAR,
            pltpu.SemaphoreType.REGULAR,
            pltpu.SemaphoreType.REGULAR,
            pltpu.SemaphoreType.REGULAR,
        ],
        compiler_params=pltpu.CompilerParams(
            collective_id=0, has_side_effects=True, vmem_limit_bytes=40 * 1024 * 1024
        ),
    )(*operands)
    free = pl.BlockSpec(memory_space=pl.ANY)
    out = pltpu.HBM((4, RHS, FD), F32)
    averaged, coarse_part = pl.pallas_call(
        store,
        out_shape=(out, out),
        in_specs=[free, free],
        out_specs=(free, free),
        scratch_shapes=[dma((2, 4))],
    )(*[pltpu.with_memory_space_constraint(value, pltpu.VMEM) for value in (averaged, coarse_part)])
    shape = (1, 1, 4, 1, RHS, FD)
    return averaged.reshape(shape), coarse_part.reshape(shape)


def solution(mesh):
    in_specs = (
        P("story", "plan", None, None, None, None, None),
        P("story", "plan", None, None, None, None),
        P("story", "plan", None, None),
        P("story", "plan", None, None, None, None),
        P("story", "plan", None, None, None, None),
        P(),
    )
    out_specs = (
        P("story", "plan", None, None, None, None),
        P("story", "plan", None, None, None, None),
    )
    return jax.shard_map(
        on_device, mesh=mesh, in_specs=in_specs, out_specs=out_specs, check_vma=False
    )
```

```python
import jax
import jax.numpy as jnp
from jax import lax
from jax.experimental import pallas as pl
from jax.experimental.pallas import tpu as pltpu
from jax.sharding import PartitionSpec as P

ITERS = 6
DAMPING = 0.3
BLK = 128
NBLK = 4
RHS = 64
FD = 512
CPD = 6
KC = 30
STORIES = 16
PLANS = 8
ROW = PLANS * CPD
NCOARSE = STORIES * ROW
MESH = pl.DeviceIdType.MESH
F32 = jnp.float32
BF16 = jnp.bfloat16


def iota(shape, dim):
    return lax.broadcasted_iota(jnp.int32, shape, dim)


def split(value):
    high = value.astype(BF16)
    return high, (value - high.astype(F32)).astype(BF16)


def dot(left, right):
    return jnp.dot(left, right, preferred_element_type=F32)


def dot_last(left, right):
    return lax.dot_general(left, right, (((1,), (1,)), ((), ())), preferred_element_type=F32)


def product(value, high, low, dot=dot):
    rows = value.shape[0]
    first, second = split(value)
    both = dot(jnp.concatenate([first, second], axis=0), high)
    return both[:rows] + both[rows:] + dot(first, low)


def fill(table, first, second):
    zero = jnp.zeros_like(first)
    for a, left in enumerate((zero, first, first.T)):
        for b, right in enumerate((zero, second, second.T)):
            table[3 * a + b] = left + right


def choice(pattern, side, q, t):
    index = 0
    for k in range(2):
        row, column = pattern[k, 0, side], pattern[k, 1, side]
        plain = jnp.where((row == q) & (column == t), 1, 0)
        turned = jnp.where((row == t) & (column == q), 2, 0)
        index = 3 * index + plain + turned
    return index


def place(pattern, side, table, diagonal, scales, high, low):
    for q in range(NBLK):
        for t in range(NBLK):
            if q == t:
                block = diagonal[q]
            else:
                block = table[choice(pattern, side, q, t)]
                if scales is not None:
                    block = block * scales[t]
            here = (pl.ds(q * BLK, BLK), pl.ds(t * BLK, BLK))
            high[here], low[here] = split(block)


def places(dof):
    group = (dof * 43) >> 8
    storey = jnp.where(group == 1, -1, jnp.where(group == 2, 1, 0))
    column = jnp.where(group == 4, 1, jnp.where(group == 3, PLANS - 1, 0))
    return storey, column, dof - CPD * group


def scatter(plan, shift):
    dof, lane = iota((32, 256), 0), iota((32, 256), 1)
    storey, column, member = places(dof)
    target = (storey + shift) * ROW + ((plan + column) & (PLANS - 1)) * CPD + member
    return jnp.where((lane == target) & (dof < KC), 1.0, 0.0)


def gather(plan):
    lane = iota((1, STORIES * 32), 1)
    dof = lane & 31
    storey, column, member = places(dof)
    storey = storey + (lane >> 5)
    target = storey * ROW + ((plan + column) & (PLANS - 1)) * CPD + member
    target = jnp.where((dof < KC) & (storey >= 0) & (storey < STORIES), target, -1)
    return jnp.where(iota((NCOARSE, STORIES * 32), 0) == target, 1.0, 0.0).astype(BF16)


def kernel(
    schur, pattern_far, owner_far, residual, basis, inverse,
    averaged, coarse_part,
    pattern, owner, raw, rows, local, slab, table, high, low, ready_high, ready_low,
    pack_out, pack_in, coupling_in, product_out, product_in, product_own, basis_in,
    wide, owned_high, owned_low, weight_high, weight_low, basis_pack, flag, flags,
    sent_first, got_first, sent_second, got_second,
    load_sem, face_send, face_recv, back_send, back_recv,
    send_flag, recv_flag, send_first, recv_first, send_second, recv_second, near, middle, far, last,
):
    story, plan = lax.axis_index("story"), lax.axis_index("plan")
    odd = lax.rem(plan, 2)
    step = 1 - 2 * odd
    in_side = (1 - odd, 3)
    out_side = (odd, 2)
    sides = (out_side[0], out_side[1], in_side[0], in_side[1])
    in_device = ((lax.rem(story + step + STORIES, STORIES), plan), (story, lax.rem(plan + 1, PLANS)))
    out_device = (
        (lax.rem(story - step + STORIES, STORIES), plan),
        (story, lax.rem(plan + PLANS - 1, PLANS)),
    )
    plan_peers = [(story, lax.rem(plan + r, PLANS)) for r in (4, 3, 5, 2, 6, 1, 7)]

    barrier = pltpu.get_barrier_semaphore()

    def around(distance):
        peers = [
            (story >= distance, (lax.rem(story + STORIES - distance, STORIES), plan)),
            (story < STORIES - distance, (lax.rem(story + distance, STORIES), plan)),
        ]
        if distance <= PLANS // 2:
            for r in sorted({distance, PLANS - distance}):
                peers.append((None, (story, lax.rem(plan + r, PLANS))))
        return peers

    def announce(semaphore, distance):
        for condition, peer in around(distance):
            def signal(peer=peer):
                pl.semaphore_signal(semaphore, inc=1, device_id=peer, device_id_type=MESH)

            if condition is None:
                signal()
            else:
                pl.when(condition)(signal)

    def hear(semaphore, distance):
        count = 0
        for condition, _ in around(distance):
            count = count + (1 if condition is None else jnp.where(condition, 1, 0))
        pl.semaphore_wait(semaphore, count)

    announce(barrier, 1)

    small = (
        pltpu.make_async_copy(pattern_far, pattern, load_sem.at[10]),
        pltpu.make_async_copy(owner_far, owner, load_sem.at[11]),
    )
    loads = []
    for k in range(4):
        loads.append(pltpu.make_async_copy(schur.at[sides[k]], raw.at[k], load_sem.at[k]))
        loads.append(pltpu.make_async_copy(residual.at[sides[k]], rows.at[k], load_sem.at[4 + k]))
    loads.append(pltpu.make_async_copy(basis, local, load_sem.at[8]))
    lowest = jnp.clip(story - 2, 0, STORIES - 5)
    loads.append(
        pltpu.make_async_copy(
            inverse.at[pl.ds(pl.multiple_of(lowest * ROW, 8), 5 * ROW)], slab, load_sem.at[9]
        )
    )
    for load in loads[:4]:
        load.start()

    line, lane = iota((BLK, BLK), 0), iota((BLK, BLK), 1)
    upper, equal = line <= lane, line == lane

    def diagonal_of(block):
        return jnp.sum(jnp.where(equal, block, 0.0), axis=0, keepdims=True)

    def to_sharer(f, m, source, target):
        return pltpu.make_async_remote_copy(
            src_ref=source, dst_ref=target, send_sem=face_send.at[f, m], recv_sem=face_recv.at[f, m],
            device_id=out_device[f], device_id_type=MESH,
        )

    def exchange(peers, source, target, send_sem, recv_sem):
        copies = []
        for r, peer in enumerate(peers):
            copies.append(
                pltpu.make_async_remote_copy(
                    src_ref=source(peer), dst_ref=target, send_sem=send_sem.at[r],
                    recv_sem=recv_sem.at[r], device_id=peer, device_id_type=MESH,
                )
            )
            copies[-1].start()
        return copies

    hear(barrier, 1)
    couplings = [
        to_sharer(f, 1, schur.at[out_side[f], pl.ds(NBLK, 2)], coupling_in.at[f]) for f in range(2)
    ]
    packs = [to_sharer(f, 0, pack_out.at[f], pack_in.at[f]) for f in range(2)]
    products = [to_sharer(f, 2, product_out.at[f], product_in.at[f]) for f in range(2)]
    bases = [to_sharer(f, 3, basis.at[out_side[f]], basis_in.at[f]) for f in range(2)]
    exists = jnp.where(odd == 0, story < STORIES - 1, story > 0)
    leaves = jnp.where(odd == 0, story > 0, story < STORIES - 1)

    def when(condition, f, action):
        if f == 0:
            pl.when(condition)(action)
        else:
            action()

    for f in range(2):
        when(leaves, f, couplings[f].start)
    for load in list(small) + loads[4:]:
        load.start()

    for f in range(2):
        loads[2 * f].wait()
        for h in range(2):
            first, second = raw[f, 2 * h], raw[f, 2 * h + 1]
            pack_out[f, h * BLK : (h + 1) * BLK] = jnp.where(upper, first, second)
            pack_out[f, 2 * BLK + h : 2 * BLK + h + 1] = diagonal_of(second)
        pack_out[f, 2 * BLK + 2 : 2 * BLK + 8] = jnp.zeros((6, BLK), F32)
        when(leaves, f, packs[f].start)
        when(leaves, f, bases[f].start)
    announce(near, 1)

    for copy in small:
        copy.wait()
    mine = [owner[0, in_side[f]].astype(F32) for f in range(2)]
    for f in range(2):
        flag[f : f + 1] = jnp.full((1, BLK), mine[f], F32)
    flag[2:8] = jnp.zeros((6, BLK), F32)
    flags[plan] = flag[...]

    for k in range(4):
        if k >= 2:
            loads[2 * k].wait()
        loads[2 * k + 1].wait()
        fill(table, raw[k, NBLK], raw[k, NBLK + 1])
        place(pattern, sides[k], table, [raw[k, n] for n in range(NBLK)], None, high, low)
        target = product_out.at[k] if k < 2 else product_own.at[k - 2]
        target[...] = product(rows[k], high[...], low[...])
        if k < 2:
            when(leaves, k, products[k].start)
    hear(near, 1)
    announce(middle, 2)

    present = (jnp.where(story > 0, 1.0, 0.0), jnp.where(story < STORIES - 1, 1.0, 0.0), 1.0, 1.0)
    loads[8].wait()
    wide[...] = jnp.zeros_like(wide)

    def widen(source, s, target):
        for n in range(NBLK):
            wide[target, 0:KC, n * BLK : (n + 1) * BLK] = source[s, pl.ds(n, KC, stride=NBLK)]

    for s in range(4):
        widen(local, s, s)
        basis_high, basis_low = split(wide[s] * present[s])
        here = pl.ds(s * FD, FD)
        basis_pack[:, here] = jnp.concatenate(
            [basis_high, basis_high, basis_low, jnp.zeros_like(basis_low)], axis=0
        )

    loads[9].wait()
    slab_high, slab_low = split(jnp.concatenate([slab[...], jnp.zeros((16, NCOARSE), F32)], axis=0))
    columns = dot(jnp.concatenate([slab_high, slab_low], axis=0), gather(plan)).astype(BF16)
    hear(middle, 2)
    announce(far, 4)
    noted = exchange(plan_peers, lambda peer: flag, flags.at[plan], send_flag, recv_flag)
    def sweeps(start, f):
        values = start
        for _ in range(ITERS - 1):
            values = start + product(values, ready_high[f], ready_low[f])
        return values

    def both_sweeps(start):
        values = start
        for _ in range(ITERS - 1):
            values = [start[f] + product(values[f], ready_high[f], ready_low[f]) for f in range(2)]
        return values

    owned_high[...] = jnp.zeros_like(owned_high)
    owned_low[...] = jnp.zeros_like(owned_low)
    scaled = [None, None]
    for f in (1, 0):
        when(exists, f, packs[f].wait_recv)
        when(exists, f, couplings[f].wait_recv)
        diagonal, scales = [], []
        for h in range(2):
            first, second = raw[2 + f, 2 * h], raw[2 + f, 2 * h + 1]
            packed = jnp.where(upper, first, second) + pack_in[f, h * BLK : (h + 1) * BLK]
            turned = packed.T
            second_diagonal = diagonal_of(second) + pack_in[f, 2 * BLK + h : 2 * BLK + h + 1]
            scales += [-DAMPING / diagonal_of(packed), -DAMPING / second_diagonal]
            diagonal.append(
                jnp.where(equal, 1.0 - DAMPING, jnp.where(upper, packed, turned) * scales[-2])
            )
            diagonal.append(
                jnp.where(equal, 1.0 - DAMPING, jnp.where(upper, turned, packed) * scales[-1])
            )
        fill(
            table,
            raw[2 + f, NBLK] + coupling_in[f, 0],
            raw[2 + f, NBLK + 1] + coupling_in[f, 1],
        )
        place(pattern, in_side[f], table, diagonal, scales, ready_high.at[f], ready_low.at[f])
        scaled[f] = jnp.concatenate(scales, axis=1)
        when(exists, f, bases[f].wait_recv)
        widen(basis_in, f, 4 + f)
        share = wide[in_side[f]] * mine[f] + wide[4 + f] * (1.0 - mine[f])
        share = sweeps(-share * scaled[f], f)
        if f == 0:
            share = jnp.where(exists, share, 0.0)
        share_high, share_low = split(share)
        for n in range(2):
            here = (pl.ds(64 * n + 32 * f, 32), pl.ds(f * FD, FD))
            owned_high[here], owned_low[here] = share_high, share_low

    right_side = []
    for f in range(2):
        when(exists, f, products[f].wait_recv)
        right_side.append(product_own[f] + product_in[f])
    right_side[0] = jnp.where(exists, right_side[0], 0.0)
    values = jnp.concatenate(right_side, axis=1)
    contribution = product(values, owned_high[...], owned_low[...], dot_last)
    left = iota((RHS // 2, BLK), 1) < 64
    packed = jnp.where(left, contribution[: RHS // 2], contribution[RHS // 2 :])
    sent_first[...] = packed
    firsts = exchange(plan_peers, lambda peer: sent_first, got_first.at[plan], send_first, recv_first)

    got_first[plan] = packed
    hear(far, 4)
    announce(last, 8)
    for copy in noted:
        copy.wait_recv()
    height = story - lowest
    chosen = []
    for p in range(PLANS):
        for f in range(2):
            kept = jnp.concatenate([flags[p, f : f + 1]] * 2, axis=1)
            other = scatter(p, height + 1 - 2 * (p % 2)) if f == 0 else scatter(p + 1, height)
            chosen.append((scatter(p, height) * kept + other * (1.0 - kept)).astype(BF16))
    chosen = jnp.concatenate(chosen, axis=0)
    weight_high[...] = dot(chosen, columns[:256]).astype(BF16)
    weight_low[...] = dot(chosen, columns[256:]).astype(BF16)
    solved = both_sweeps([-right_side[f] * scaled[f] for f in range(2)])
    solved[0] = jnp.where(exists, solved[0], 0.0)
    for f in range(2):
        averaged[in_side[f]] = solved[f]

    def to_owner(f):
        return pltpu.make_async_remote_copy(
            src_ref=averaged.at[in_side[f]], dst_ref=averaged.at[out_side[f]],
            send_sem=back_send.at[f], recv_sem=back_recv.at[f],
            device_id=in_device[f], device_id_type=MESH,
        )

    backs = [to_owner(f) for f in range(2)]
    when(exists, 0, backs[0].start)

    @pl.when(jnp.logical_not(leaves))
    def _():
        averaged[out_side[0]] = jnp.zeros((RHS, FD), F32)


    for copy in firsts:
        copy.wait_recv()
    halves = ([], [])
    for p in range(0, PLANS, 2):
        first, second = got_first[p], got_first[p + 1]
        halves[0].append(jnp.where(left, first, pltpu.roll(second, 64, 1)))
        halves[1].append(jnp.where(left, pltpu.roll(first, 64, 1), second))
    gathered = jnp.concatenate([jnp.concatenate(half, axis=1) for half in halves], axis=0)
    hear(last, 8)
    quarter = iota((16, BLK), 1) >> 5
    seconds = []
    for n in range(STORIES // 4):
        if n % 2 == 0:
            here = pl.ds(n * BLK, 2 * BLK)
            coarse = product(gathered, weight_high[:, here], weight_low[:, here])
        tile = coarse[:, (n % 2) * BLK : (n % 2 + 1) * BLK]
        turned = [pltpu.roll(tile, 32 * g, 1) if g else tile for g in range(4)]
        for q in range(4):
            message = turned[(3 - q) % 4][48:64]
            for g in range(3):
                message = jnp.where(quarter == g, turned[(g - q) % 4][16 * g : 16 * g + 16], message)
            sent_second[4 * n + q] = message
        if n % 2 == 0:
            continue
        for i in range(4 * n - 4, 4 * n + 4):
            seconds.append(
                pltpu.make_async_remote_copy(
                    src_ref=sent_second.at[i], dst_ref=got_second.at[story], send_sem=send_second.at[i],
                    recv_sem=recv_second.at[story], device_id=(i, plan), device_id_type=MESH,
                )
            )
            pl.when(story != i)(seconds[-1].start)

    def arrival(i):
        return pltpu.make_async_remote_copy(
            src_ref=sent_second.at[i], dst_ref=got_second.at[i], send_sem=send_second.at[i],
            recv_sem=recv_second.at[i], device_id=(i, plan), device_id_type=MESH,
        )

    backs[1].start()
    got_second[story] = sent_second[story]
    for i in range(STORIES):
        pl.when(story != i)(arrival(i).wait_recv)
    total = got_second[0]
    for i in range(1, STORIES):
        total = total + got_second[i]
    parts = [total] + [pltpu.roll(total, BLK - 32 * g, 1) for g in range(1, 4)]
    needed = jnp.concatenate(parts, axis=0)
    needed = jnp.where(iota((RHS, BLK), 1) < 32, needed, 0.0)
    needed_high, needed_low = split(needed)
    needed_high, needed_low = needed_high.astype(F32), needed_low.astype(F32)
    operand = needed_high + pltpu.roll(needed_low, 32, 1) + pltpu.roll(needed_high, 64, 1)
    operand = operand.astype(BF16)
    for s in range(4):
        coarse_part[s] = dot(operand, basis_pack[:, s * FD : (s + 1) * FD])

    for copies in (packs, couplings, products, bases):
        for f in range(2):
            when(leaves, f, copies[f].wait_send)
    for copy in noted + firsts:
        copy.wait_send()
    for i in range(STORIES):
        pl.when(story != i)(seconds[i].wait_send)
    for f in range(2):
        when(exists, f, backs[f].wait_send)
        when(leaves, f, backs[f].wait_recv)


def store(averaged, coarse_part, averaged_out, coarse_part_out, sem):
    copies = []
    for s in range(4):
        copies.append(pltpu.make_async_copy(averaged.at[s], averaged_out.at[s], sem.at[0, s]))
        copies.append(pltpu.make_async_copy(coarse_part.at[s], coarse_part_out.at[s], sem.at[1, s]))
    for copy in copies:
        copy.start()
    for copy in copies:
        copy.wait()


def on_device(schur_blocks, off_pattern, face_owner, residual, coarse_basis, coarse_inverse):
    hbm = pl.BlockSpec(memory_space=pltpu.HBM)
    operands = [
        pltpu.with_memory_space_constraint(operand, pltpu.HBM)
        for operand in (
            schur_blocks.reshape(4, 6, BLK, BLK),
            off_pattern.reshape(4, 2, 2).transpose(1, 2, 0),
            face_owner.reshape(1, 4),
            residual.reshape(4, RHS, FD),
            coarse_basis.reshape(4, KC * NBLK, BLK),
            coarse_inverse,
        )
    ]
    vmem = pl.BlockSpec(memory_space=pltpu.VMEM)
    dma = pltpu.SemaphoreType.DMA
    out = pltpu.VMEM((4, RHS, FD), F32)
    averaged, coarse_part = pl.pallas_call(
        kernel,
        out_shape=(out, out),
        in_specs=[hbm] * 6,
        out_specs=(vmem, vmem),
        scratch_shapes=[
            pltpu.SMEM((2, 2, 4), jnp.int32),
            pltpu.SMEM((1, 4), jnp.int32),
            pltpu.VMEM((4, 6, BLK, BLK), F32),
            pltpu.VMEM((4, RHS, FD), F32),
            pltpu.VMEM((4, KC * NBLK, BLK), F32),
            pltpu.VMEM((5 * ROW, NCOARSE), F32),
            pltpu.VMEM((9, BLK, BLK), F32),
            pltpu.VMEM((FD, FD), BF16),
            pltpu.VMEM((FD, FD), BF16),
            pltpu.VMEM((2, FD, FD), BF16),
            pltpu.VMEM((2, FD, FD), BF16),
            pltpu.VMEM((2, 2 * BLK + 8, BLK), F32),
            pltpu.VMEM((2, 2 * BLK + 8, BLK), F32),
            pltpu.VMEM((2, 2, BLK, BLK), F32),
            pltpu.VMEM((2, RHS, FD), F32),
            pltpu.VMEM((2, RHS, FD), F32),
            pltpu.VMEM((2, RHS, FD), F32),
            pltpu.VMEM((2, KC * NBLK, BLK), F32),
            pltpu.VMEM((6, 32, FD), F32),
            pltpu.VMEM((BLK, 2 * FD), BF16),
            pltpu.VMEM((BLK, 2 * FD), BF16),
            pltpu.VMEM((PLANS * 64, STORIES * 32), BF16),
            pltpu.VMEM((PLANS * 64, STORIES * 32), BF16),
            pltpu.VMEM((BLK, 4 * FD), BF16),
            pltpu.VMEM((8, BLK), F32),
            pltpu.VMEM((PLANS, 8, BLK), F32),
            pltpu.VMEM((RHS // 2, BLK), F32),
            pltpu.VMEM((PLANS, RHS // 2, BLK), F32),
            pltpu.VMEM((STORIES, 16, BLK), F32),
            pltpu.VMEM((STORIES, 16, BLK), F32),
            dma((12,)),
            dma((2, 4)),
            dma((2, 4)),
            dma((2,)),
            dma((2,)),
            dma((PLANS - 1,)),
            dma((PLANS - 1,)),
            dma((PLANS - 1,)),
            dma((PLANS - 1,)),
            dma((STORIES,)),
            dma((STORIES,)),
            pltpu.SemaphoreType.REGULAR,
            pltpu.SemaphoreType.REGULAR,
            pltpu.SemaphoreType.REGULAR,
            pltpu.SemaphoreType.REGULAR,
        ],
        compiler_params=pltpu.CompilerParams(
            collective_id=0, has_side_effects=True, vmem_limit_bytes=40 * 1024 * 1024
        ),
    )(*operands)
    free = pl.BlockSpec(memory_space=pl.ANY)
    out = pltpu.HBM((4, RHS, FD), F32)
    averaged, coarse_part = pl.pallas_call(
        store,
        out_shape=(out, out),
        in_specs=[free, free],
        out_specs=(free, free),
        scratch_shapes=[dma((2, 4))],
    )(*[pltpu.with_memory_space_constraint(value, pltpu.VMEM) for value in (averaged, coarse_part)])
    shape = (1, 1, 4, 1, RHS, FD)
    return averaged.reshape(shape), coarse_part.reshape(shape)


def solution(mesh):
    in_specs = (
        P("story", "plan", None, None, None, None, None),
        P("story", "plan", None, None, None, None),
        P("story", "plan", None, None),
        P("story", "plan", None, None, None, None),
        P("story", "plan", None, None, None, None),
        P(),
    )
    out_specs = (
        P("story", "plan", None, None, None, None),
        P("story", "plan", None, None, None, None),
    )
    return jax.shard_map(
        on_device, mesh=mesh, in_specs=in_specs, out_specs=out_specs, check_vma=False
    )
```

```python
import jax
import jax.numpy as jnp
from jax import lax
from jax.experimental import pallas as pl
from jax.experimental.pallas import tpu as pltpu
from jax.sharding import PartitionSpec as P

ITERS = 6
DAMPING = 0.3
BLK = 128
NBLK = 4
RHS = 64
FD = 512
CPD = 6
KC = 30
STORIES = 16
PLANS = 8
ROW = PLANS * CPD
NCOARSE = STORIES * ROW
MESH = pl.DeviceIdType.MESH
F32 = jnp.float32
BF16 = jnp.bfloat16


def iota(shape, dim):
    return lax.broadcasted_iota(jnp.int32, shape, dim)


def split(value):
    high = value.astype(BF16)
    return high, (value - high.astype(F32)).astype(BF16)


def dot(left, right):
    return jnp.dot(left, right, preferred_element_type=F32)


def dot_last(left, right):
    return lax.dot_general(left, right, (((1,), (1,)), ((), ())), preferred_element_type=F32)


def product(value, high, low, dot=dot):
    rows = value.shape[0]
    first, second = split(value)
    both = dot(jnp.concatenate([first, second], axis=0), high)
    return both[:rows] + both[rows:] + dot(first, low)


def fill(table, first, second):
    zero = jnp.zeros_like(first)
    for a, left in enumerate((zero, first, first.T)):
        for b, right in enumerate((zero, second, second.T)):
            table[3 * a + b] = left + right


def choice(pattern, side, q, t):
    index = 0
    for k in range(2):
        row, column = pattern[k, 0, side], pattern[k, 1, side]
        plain = jnp.where((row == q) & (column == t), 1, 0)
        turned = jnp.where((row == t) & (column == q), 2, 0)
        index = 3 * index + plain + turned
    return index


def place(pattern, side, table, diagonal, scales, high, low):
    for q in range(NBLK):
        for t in range(NBLK):
            if q == t:
                block = diagonal[q]
            else:
                block = table[choice(pattern, side, q, t)]
                if scales is not None:
                    block = block * scales[t]
            here = (pl.ds(q * BLK, BLK), pl.ds(t * BLK, BLK))
            high[here], low[here] = split(block)


def places(dof):
    group = (dof * 43) >> 8
    storey = jnp.where(group == 1, -1, jnp.where(group == 2, 1, 0))
    column = jnp.where(group == 4, 1, jnp.where(group == 3, PLANS - 1, 0))
    return storey, column, dof - CPD * group


def scatter(plan, shift):
    dof, lane = iota((32, 256), 0), iota((32, 256), 1)
    storey, column, member = places(dof)
    target = (storey + shift) * ROW + ((plan + column) & (PLANS - 1)) * CPD + member
    return jnp.where((lane == target) & (dof < KC), 1.0, 0.0)


def gather(plan):
    lane = iota((1, STORIES * 32), 1)
    dof = lane & 31
    storey, column, member = places(dof)
    storey = storey + (lane >> 5)
    target = storey * ROW + ((plan + column) & (PLANS - 1)) * CPD + member
    target = jnp.where((dof < KC) & (storey >= 0) & (storey < STORIES), target, -1)
    return jnp.where(iota((NCOARSE, STORIES * 32), 0) == target, 1.0, 0.0).astype(BF16)


def kernel(
    schur, pattern_far, owner_far, residual, basis, inverse,
    averaged, needed_part, basis_pack,
    pattern, owner, raw, rows, local, slab, table, high, low, ready_high, ready_low,
    pack_out, pack_in, coupling_in, product_out, product_in, product_own, basis_in,
    wide, owned_high, owned_low, weight_high, weight_low, flag, flags,
    sent_first, got_first, sent_second, got_second,
    load_sem, face_send, face_recv, back_send, back_recv,
    send_flag, recv_flag, send_first, recv_first, send_second, recv_second, near, middle, far, last,
):
    story, plan = lax.axis_index("story"), lax.axis_index("plan")
    odd = lax.rem(plan, 2)
    step = 1 - 2 * odd
    in_side = (1 - odd, 3)
    out_side = (odd, 2)
    sides = (out_side[0], out_side[1], in_side[0], in_side[1])
    in_device = ((lax.rem(story + step + STORIES, STORIES), plan), (story, lax.rem(plan + 1, PLANS)))
    out_device = (
        (lax.rem(story - step + STORIES, STORIES), plan),
        (story, lax.rem(plan + PLANS - 1, PLANS)),
    )
    plan_peers = [(story, lax.rem(plan + r, PLANS)) for r in (4, 3, 5, 2, 6, 1, 7)]

    barrier = pltpu.get_barrier_semaphore()

    def around(distance):
        peers = [
            (story >= distance, (lax.rem(story + STORIES - distance, STORIES), plan)),
            (story < STORIES - distance, (lax.rem(story + distance, STORIES), plan)),
        ]
        if distance <= PLANS // 2:
            for r in sorted({distance, PLANS - distance}):
                peers.append((None, (story, lax.rem(plan + r, PLANS))))
        return peers

    def announce(semaphore, distance):
        for condition, peer in around(distance):
            def signal(peer=peer):
                pl.semaphore_signal(semaphore, inc=1, device_id=peer, device_id_type=MESH)

            if condition is None:
                signal()
            else:
                pl.when(condition)(signal)

    def hear(semaphore, distance):
        count = 0
        for condition, _ in around(distance):
            count = count + (1 if condition is None else jnp.where(condition, 1, 0))
        pl.semaphore_wait(semaphore, count)

    announce(barrier, 1)

    small = (
        pltpu.make_async_copy(pattern_far, pattern, load_sem.at[10]),
        pltpu.make_async_copy(owner_far, owner, load_sem.at[11]),
    )
    loads = []
    for k in range(4):
        loads.append(pltpu.make_async_copy(schur.at[sides[k]], raw.at[k], load_sem.at[k]))
        loads.append(pltpu.make_async_copy(residual.at[sides[k]], rows.at[k], load_sem.at[4 + k]))
    loads.append(pltpu.make_async_copy(basis, local, load_sem.at[8]))
    lowest = jnp.clip(story - 2, 0, STORIES - 5)
    loads.append(
        pltpu.make_async_copy(
            inverse.at[pl.ds(pl.multiple_of(lowest * ROW, 8), 5 * ROW)], slab, load_sem.at[9]
        )
    )
    for load in loads[:4]:
        load.start()

    line, lane = iota((BLK, BLK), 0), iota((BLK, BLK), 1)
    upper, equal = line <= lane, line == lane

    def diagonal_of(block):
        return jnp.sum(jnp.where(equal, block, 0.0), axis=0, keepdims=True)

    def to_sharer(f, m, source, target):
        return pltpu.make_async_remote_copy(
            src_ref=source, dst_ref=target, send_sem=face_send.at[f, m], recv_sem=face_recv.at[f, m],
            device_id=out_device[f], device_id_type=MESH,
        )

    def exchange(peers, source, target, send_sem, recv_sem):
        copies = []
        for r, peer in enumerate(peers):
            copies.append(
                pltpu.make_async_remote_copy(
                    src_ref=source(peer), dst_ref=target, send_sem=send_sem.at[r],
                    recv_sem=recv_sem.at[r], device_id=peer, device_id_type=MESH,
                )
            )
            copies[-1].start()
        return copies

    hear(barrier, 1)
    couplings = [
        to_sharer(f, 1, schur.at[out_side[f], pl.ds(NBLK, 2)], coupling_in.at[f]) for f in range(2)
    ]
    packs = [to_sharer(f, 0, pack_out.at[f], pack_in.at[f]) for f in range(2)]
    products = [to_sharer(f, 2, product_out.at[f], product_in.at[f]) for f in range(2)]
    bases = [to_sharer(f, 3, basis.at[out_side[f]], basis_in.at[f]) for f in range(2)]
    exists = jnp.where(odd == 0, story < STORIES - 1, story > 0)
    leaves = jnp.where(odd == 0, story > 0, story < STORIES - 1)

    def when(condition, f, action):
        if f == 0:
            pl.when(condition)(action)
        else:
            action()

    for f in range(2):
        when(leaves, f, couplings[f].start)
    for load in list(small) + loads[4:]:
        load.start()

    for f in range(2):
        loads[2 * f].wait()
        for h in range(2):
            first, second = raw[f, 2 * h], raw[f, 2 * h + 1]
            pack_out[f, h * BLK : (h + 1) * BLK] = jnp.where(upper, first, second)
            pack_out[f, 2 * BLK + h : 2 * BLK + h + 1] = diagonal_of(second)
        pack_out[f, 2 * BLK + 2 : 2 * BLK + 8] = jnp.zeros((6, BLK), F32)
        when(leaves, f, packs[f].start)
        when(leaves, f, bases[f].start)
    announce(near, 1)

    for copy in small:
        copy.wait()
    mine = [owner[0, in_side[f]].astype(F32) for f in range(2)]
    for f in range(2):
        flag[f : f + 1] = jnp.full((1, BLK), mine[f], F32)
    flag[2:8] = jnp.zeros((6, BLK), F32)
    flags[plan] = flag[...]

    for k in range(4):
        if k >= 2:
            loads[2 * k].wait()
        loads[2 * k + 1].wait()
        fill(table, raw[k, NBLK], raw[k, NBLK + 1])
        place(pattern, sides[k], table, [raw[k, n] for n in range(NBLK)], None, high, low)
        target = product_out.at[k] if k < 2 else product_own.at[k - 2]
        target[...] = product(rows[k], high[...], low[...])
        if k < 2:
            when(leaves, k, products[k].start)
    hear(near, 1)
    announce(middle, 2)

    present = (jnp.where(story > 0, 1.0, 0.0), jnp.where(story < STORIES - 1, 1.0, 0.0), 1.0, 1.0)
    loads[8].wait()
    wide[...] = jnp.zeros_like(wide)

    def widen(source, s, target):
        for n in range(NBLK):
            wide[target, 0:KC, n * BLK : (n + 1) * BLK] = source[s, pl.ds(n, KC, stride=NBLK)]

    for s in range(4):
        widen(local, s, s)
        basis_high, basis_low = split(wide[s] * present[s])
        here = pl.ds(s * FD, FD)
        basis_pack[:, here] = jnp.concatenate(
            [basis_high, basis_high, basis_low, jnp.zeros_like(basis_low)], axis=0
        )

    loads[9].wait()
    slab_high, slab_low = split(jnp.concatenate([slab[...], jnp.zeros((16, NCOARSE), F32)], axis=0))
    columns = dot(jnp.concatenate([slab_high, slab_low], axis=0), gather(plan)).astype(BF16)
    hear(middle, 2)
    announce(far, 4)
    noted = exchange(plan_peers, lambda peer: flag, flags.at[plan], send_flag, recv_flag)
    def sweeps(start, f):
        values = start
        for _ in range(ITERS - 1):
            values = start + product(values, ready_high[f], ready_low[f])
        return values

    def both_sweeps(start):
        values = start
        for _ in range(ITERS - 1):
            values = [start[f] + product(values[f], ready_high[f], ready_low[f]) for f in range(2)]
        return values

    owned_high[...] = jnp.zeros_like(owned_high)
    owned_low[...] = jnp.zeros_like(owned_low)
    scaled = [None, None]
    for f in (1, 0):
        when(exists, f, packs[f].wait_recv)
        when(exists, f, couplings[f].wait_recv)
        diagonal, scales = [], []
        for h in range(2):
            first, second = raw[2 + f, 2 * h], raw[2 + f, 2 * h + 1]
            packed = jnp.where(upper, first, second) + pack_in[f, h * BLK : (h + 1) * BLK]
            turned = packed.T
            second_diagonal = diagonal_of(second) + pack_in[f, 2 * BLK + h : 2 * BLK + h + 1]
            scales += [-DAMPING / diagonal_of(packed), -DAMPING / second_diagonal]
            diagonal.append(
                jnp.where(equal, 1.0 - DAMPING, jnp.where(upper, packed, turned) * scales[-2])
            )
            diagonal.append(
                jnp.where(equal, 1.0 - DAMPING, jnp.where(upper, turned, packed) * scales[-1])
            )
        fill(
            table,
            raw[2 + f, NBLK] + coupling_in[f, 0],
            raw[2 + f, NBLK + 1] + coupling_in[f, 1],
        )
        place(pattern, in_side[f], table, diagonal, scales, ready_high.at[f], ready_low.at[f])
        scaled[f] = jnp.concatenate(scales, axis=1)
        when(exists, f, bases[f].wait_recv)
        widen(basis_in, f, 4 + f)
        share = wide[in_side[f]] * mine[f] + wide[4 + f] * (1.0 - mine[f])
        share = sweeps(-share * scaled[f], f)
        if f == 0:
            share = jnp.where(exists, share, 0.0)
        share_high, share_low = split(share)
        for n in range(2):
            here = (pl.ds(64 * n + 32 * f, 32), pl.ds(f * FD, FD))
            owned_high[here], owned_low[here] = share_high, share_low

    right_side, contribution = [None, None], 0.0
    for f in (1, 0):
        when(exists, f, products[f].wait_recv)
        right_side[f] = product_own[f] + product_in[f]
        if f == 0:
            right_side[f] = jnp.where(exists, right_side[f], 0.0)
        here = pl.ds(f * FD, FD)
        contribution = contribution + product(
            right_side[f], owned_high[:, here], owned_low[:, here], dot_last
        )
    left = iota((RHS // 2, BLK), 1) < 64
    packed = jnp.where(left, contribution[: RHS // 2], contribution[RHS // 2 :])
    sent_first[...] = packed
    firsts = exchange(plan_peers, lambda peer: sent_first, got_first.at[plan], send_first, recv_first)

    got_first[plan] = packed
    hear(far, 4)
    announce(last, 8)
    for copy in noted:
        copy.wait_recv()
    height = story - lowest
    chosen = []
    for p in range(PLANS):
        for f in range(2):
            kept = jnp.concatenate([flags[p, f : f + 1]] * 2, axis=1)
            other = scatter(p, height + 1 - 2 * (p % 2)) if f == 0 else scatter(p + 1, height)
            chosen.append((scatter(p, height) * kept + other * (1.0 - kept)).astype(BF16))
    chosen = jnp.concatenate(chosen, axis=0)
    weight_high[...] = dot(chosen, columns[:256]).astype(BF16)
    weight_low[...] = dot(chosen, columns[256:]).astype(BF16)
    solved = both_sweeps([-right_side[f] * scaled[f] for f in range(2)])
    solved[0] = jnp.where(exists, solved[0], 0.0)
    for f in range(2):
        averaged[in_side[f]] = solved[f]

    def to_owner(f):
        return pltpu.make_async_remote_copy(
            src_ref=averaged.at[in_side[f]], dst_ref=averaged.at[out_side[f]],
            send_sem=back_send.at[f], recv_sem=back_recv.at[f],
            device_id=in_device[f], device_id_type=MESH,
        )

    backs = [to_owner(f) for f in range(2)]
    when(exists, 0, backs[0].start)

    @pl.when(jnp.logical_not(leaves))
    def _():
        averaged[out_side[0]] = jnp.zeros((RHS, FD), F32)


    for copy in firsts:
        copy.wait_recv()
    halves = ([], [])
    for p in range(0, PLANS, 2):
        first, second = got_first[p], got_first[p + 1]
        halves[0].append(jnp.where(left, first, pltpu.roll(second, 64, 1)))
        halves[1].append(jnp.where(left, pltpu.roll(first, 64, 1), second))
    gathered = jnp.concatenate([jnp.concatenate(half, axis=1) for half in halves], axis=0)
    hear(last, 8)
    quarter = iota((16, BLK), 1) >> 5
    seconds = []
    for n in range(STORIES // 4):
        if n % 2 == 0:
            here = pl.ds(n * BLK, 2 * BLK)
            coarse = product(gathered, weight_high[:, here], weight_low[:, here])
        tile = coarse[:, (n % 2) * BLK : (n % 2 + 1) * BLK]
        turned = [pltpu.roll(tile, 32 * g, 1) if g else tile for g in range(4)]
        for q in range(4):
            message = turned[(3 - q) % 4][48:64]
            for g in range(3):
                message = jnp.where(quarter == g, turned[(g - q) % 4][16 * g : 16 * g + 16], message)
            sent_second[4 * n + q] = message
        if n % 2 == 0:
            continue
        for i in range(4 * n - 4, 4 * n + 4):
            seconds.append(
                pltpu.make_async_remote_copy(
                    src_ref=sent_second.at[i], dst_ref=got_second.at[story], send_sem=send_second.at[i],
                    recv_sem=recv_second.at[story], device_id=(i, plan), device_id_type=MESH,
                )
            )
            pl.when(story != i)(seconds[-1].start)

    def arrival(i):
        return pltpu.make_async_remote_copy(
            src_ref=sent_second.at[i], dst_ref=got_second.at[i], send_sem=send_second.at[i],
            recv_sem=recv_second.at[i], device_id=(i, plan), device_id_type=MESH,
        )

    backs[1].start()
    got_second[story] = sent_second[story]
    for i in range(STORIES):
        pl.when(story != i)(arrival(i).wait_recv)
    total = got_second[0]
    for i in range(1, STORIES):
        total = total + got_second[i]
    parts = [total] + [pltpu.roll(total, BLK - 32 * g, 1) for g in range(1, 4)]
    needed = jnp.concatenate(parts, axis=0)
    needed = jnp.where(iota((RHS, BLK), 1) < 32, needed, 0.0)
    needed_high, needed_low = split(needed)
    needed_high, needed_low = needed_high.astype(F32), needed_low.astype(F32)
    operand = needed_high + pltpu.roll(needed_low, 32, 1) + pltpu.roll(needed_high, 64, 1)
    needed_part[...] = operand.astype(BF16)
    for copies in (packs, couplings, products, bases):
        for f in range(2):
            when(leaves, f, copies[f].wait_send)
    for copy in noted + firsts:
        copy.wait_send()
    for i in range(STORIES):
        pl.when(story != i)(seconds[i].wait_send)
    for f in range(2):
        when(exists, f, backs[f].wait_send)
        when(leaves, f, backs[f].wait_recv)


def store(averaged, needed, basis_pack, averaged_out, coarse_part_out, result, sem):
    copies = [pltpu.make_async_copy(averaged.at[s], averaged_out.at[s], sem.at[0, s]) for s in range(4)]
    for copy in copies:
        copy.start()
    for s in range(4):
        result[s] = dot(needed[...], basis_pack[:, s * FD : (s + 1) * FD])
        copies.append(pltpu.make_async_copy(result.at[s], coarse_part_out.at[s], sem.at[1, s]))
        copies[-1].start()
    for copy in copies:
        copy.wait()


def on_device(schur_blocks, off_pattern, face_owner, residual, coarse_basis, coarse_inverse):
    hbm = pl.BlockSpec(memory_space=pltpu.HBM)
    operands = [
        pltpu.with_memory_space_constraint(operand, pltpu.HBM)
        for operand in (
            schur_blocks.reshape(4, 6, BLK, BLK),
            off_pattern.reshape(4, 2, 2).transpose(1, 2, 0),
            face_owner.reshape(1, 4),
            residual.reshape(4, RHS, FD),
            coarse_basis.reshape(4, KC * NBLK, BLK),
            coarse_inverse,
        )
    ]
    vmem = pl.BlockSpec(memory_space=pltpu.VMEM)
    dma = pltpu.SemaphoreType.DMA
    out = pltpu.VMEM((4, RHS, FD), F32)
    averaged, needed, basis_pack = pl.pallas_call(
        kernel,
        out_shape=(out, pltpu.VMEM((RHS, BLK), BF16), pltpu.VMEM((BLK, 4 * FD), BF16)),
        in_specs=[hbm] * 6,
        out_specs=(vmem, vmem, vmem),
        scratch_shapes=[
            pltpu.SMEM((2, 2, 4), jnp.int32),
            pltpu.SMEM((1, 4), jnp.int32),
            pltpu.VMEM((4, 6, BLK, BLK), F32),
            pltpu.VMEM((4, RHS, FD), F32),
            pltpu.VMEM((4, KC * NBLK, BLK), F32),
            pltpu.VMEM((5 * ROW, NCOARSE), F32),
            pltpu.VMEM((9, BLK, BLK), F32),
            pltpu.VMEM((FD, FD), BF16),
            pltpu.VMEM((FD, FD), BF16),
            pltpu.VMEM((2, FD, FD), BF16),
            pltpu.VMEM((2, FD, FD), BF16),
            pltpu.VMEM((2, 2 * BLK + 8, BLK), F32),
            pltpu.VMEM((2, 2 * BLK + 8, BLK), F32),
            pltpu.VMEM((2, 2, BLK, BLK), F32),
            pltpu.VMEM((2, RHS, FD), F32),
            pltpu.VMEM((2, RHS, FD), F32),
            pltpu.VMEM((2, RHS, FD), F32),
            pltpu.VMEM((2, KC * NBLK, BLK), F32),
            pltpu.VMEM((6, 32, FD), F32),
            pltpu.VMEM((BLK, 2 * FD), BF16),
            pltpu.VMEM((BLK, 2 * FD), BF16),
            pltpu.VMEM((PLANS * 64, STORIES * 32), BF16),
            pltpu.VMEM((PLANS * 64, STORIES * 32), BF16),
            pltpu.VMEM((8, BLK), F32),
            pltpu.VMEM((PLANS, 8, BLK), F32),
            pltpu.VMEM((RHS // 2, BLK), F32),
            pltpu.VMEM((PLANS, RHS // 2, BLK), F32),
            pltpu.VMEM((STORIES, 16, BLK), F32),
            pltpu.VMEM((STORIES, 16, BLK), F32),
            dma((12,)),
            dma((2, 4)),
            dma((2, 4)),
            dma((2,)),
            dma((2,)),
            dma((PLANS - 1,)),
            dma((PLANS - 1,)),
            dma((PLANS - 1,)),
            dma((PLANS - 1,)),
            dma((STORIES,)),
            dma((STORIES,)),
            pltpu.SemaphoreType.REGULAR,
            pltpu.SemaphoreType.REGULAR,
            pltpu.SemaphoreType.REGULAR,
            pltpu.SemaphoreType.REGULAR,
        ],
        compiler_params=pltpu.CompilerParams(
            collective_id=0, has_side_effects=True, vmem_limit_bytes=40 * 1024 * 1024
        ),
    )(*operands)
    free = pl.BlockSpec(memory_space=pl.ANY)
    out = pltpu.HBM((4, RHS, FD), F32)
    averaged, coarse_part = pl.pallas_call(
        store,
        out_shape=(out, out),
        in_specs=[free, vmem, vmem],
        out_specs=(free, free),
        scratch_shapes=[pltpu.VMEM((4, RHS, FD), F32), dma((2, 4))],
        compiler_params=pltpu.CompilerParams(vmem_limit_bytes=16 * 1024 * 1024),
    )(*[pltpu.with_memory_space_constraint(value, pltpu.VMEM) for value in (averaged, needed, basis_pack)])
    shape = (1, 1, 4, 1, RHS, FD)
    return averaged.reshape(shape), coarse_part.reshape(shape)


def solution(mesh):
    in_specs = (
        P("story", "plan", None, None, None, None, None),
        P("story", "plan", None, None, None, None),
        P("story", "plan", None, None),
        P("story", "plan", None, None, None, None),
        P("story", "plan", None, None, None, None),
        P(),
    )
    out_specs = (
        P("story", "plan", None, None, None, None),
        P("story", "plan", None, None, None, None),
    )
    return jax.shard_map(
        on_device, mesh=mesh, in_specs=in_specs, out_specs=out_specs, check_vma=False
    )
```

```python
import jax
import jax.numpy as jnp
from jax import lax
from jax.experimental import pallas as pl
from jax.experimental.pallas import tpu as pltpu
from jax.sharding import PartitionSpec as P

ITERS = 6
DAMPING = 0.3
BLK = 128
NBLK = 4
RHS = 64
FD = 512
CPD = 6
KC = 30
STORIES = 16
PLANS = 8
ROW = PLANS * CPD
NCOARSE = STORIES * ROW
MESH = pl.DeviceIdType.MESH
F32 = jnp.float32
BF16 = jnp.bfloat16


def iota(shape, dim):
    return lax.broadcasted_iota(jnp.int32, shape, dim)


def split(value):
    high = value.astype(BF16)
    return high, (value - high.astype(F32)).astype(BF16)


def dot(left, right):
    return jnp.dot(left, right, preferred_element_type=F32)


def dot_last(left, right):
    return lax.dot_general(left, right, (((1,), (1,)), ((), ())), preferred_element_type=F32)


def product(value, high, low, dot=dot):
    rows = value.shape[0]
    first, second = split(value)
    both = dot(jnp.concatenate([first, second], axis=0), high)
    return both[:rows] + both[rows:] + dot(first, low)


def fill(table, first, second):
    zero = jnp.zeros_like(first)
    for a, left in enumerate((zero, first, first.T)):
        for b, right in enumerate((zero, second, second.T)):
            table[3 * a + b] = left + right


def choice(pattern, side, q, t):
    index = 0
    for k in range(2):
        row, column = pattern[k, 0, side], pattern[k, 1, side]
        plain = jnp.where((row == q) & (column == t), 1, 0)
        turned = jnp.where((row == t) & (column == q), 2, 0)
        index = 3 * index + plain + turned
    return index


def place(pattern, side, table, diagonal, scales, high, low):
    for q in range(NBLK):
        for t in range(NBLK):
            if q == t:
                block = diagonal[q]
            else:
                block = table[choice(pattern, side, q, t)]
                if scales is not None:
                    block = block * scales[t]
            here = (pl.ds(q * BLK, BLK), pl.ds(t * BLK, BLK))
            high[here], low[here] = split(block)


def places(dof):
    group = (dof * 43) >> 8
    storey = jnp.where(group == 1, -1, jnp.where(group == 2, 1, 0))
    column = jnp.where(group == 4, 1, jnp.where(group == 3, PLANS - 1, 0))
    return storey, column, dof - CPD * group


def scatter(plan, shift):
    dof, lane = iota((32, 256), 0), iota((32, 256), 1)
    storey, column, member = places(dof)
    target = (storey + shift) * ROW + ((plan + column) & (PLANS - 1)) * CPD + member
    return jnp.where((lane == target) & (dof < KC), 1.0, 0.0)


def gather(plan):
    lane = iota((1, STORIES * 32), 1)
    dof = lane & 31
    storey, column, member = places(dof)
    storey = storey + (lane >> 5)
    target = storey * ROW + ((plan + column) & (PLANS - 1)) * CPD + member
    target = jnp.where((dof < KC) & (storey >= 0) & (storey < STORIES), target, -1)
    return jnp.where(iota((NCOARSE, STORIES * 32), 0) == target, 1.0, 0.0).astype(BF16)


def kernel(
    schur, pattern_far, owner_far, residual, basis, inverse,
    averaged, needed_part, basis_pack,
    pattern, owner, raw, rows, local, slab, table, high, low, ready_high, ready_low,
    pack_out, pack_in, coupling_in, product_out, product_in, product_own, basis_in,
    wide, owned_high, owned_low, weight_high, weight_low, flag, flags,
    sent_first, got_first, sent_second, got_second,
    load_sem, face_send, face_recv, back_send, back_recv,
    send_flag, recv_flag, send_first, recv_first, send_second, recv_second, near, middle, far, last,
):
    story, plan = lax.axis_index("story"), lax.axis_index("plan")
    odd = lax.rem(plan, 2)
    step = 1 - 2 * odd
    in_side = (1 - odd, 3)
    out_side = (odd, 2)
    sides = (out_side[0], out_side[1], in_side[0], in_side[1])
    in_device = ((lax.rem(story + step + STORIES, STORIES), plan), (story, lax.rem(plan + 1, PLANS)))
    out_device = (
        (lax.rem(story - step + STORIES, STORIES), plan),
        (story, lax.rem(plan + PLANS - 1, PLANS)),
    )
    plan_peers = [(story, lax.rem(plan + r, PLANS)) for r in (4, 3, 5, 2, 6, 1, 7)]

    barrier = pltpu.get_barrier_semaphore()

    def around(distance):
        peers = [
            (story >= distance, (lax.rem(story + STORIES - distance, STORIES), plan)),
            (story < STORIES - distance, (lax.rem(story + distance, STORIES), plan)),
        ]
        if distance <= PLANS // 2:
            for r in sorted({distance, PLANS - distance}):
                peers.append((None, (story, lax.rem(plan + r, PLANS))))
        return peers

    def announce(semaphore, distance):
        for condition, peer in around(distance):
            def signal(peer=peer):
                pl.semaphore_signal(semaphore, inc=1, device_id=peer, device_id_type=MESH)

            if condition is None:
                signal()
            else:
                pl.when(condition)(signal)

    def hear(semaphore, distance):
        count = 0
        for condition, _ in around(distance):
            count = count + (1 if condition is None else jnp.where(condition, 1, 0))
        pl.semaphore_wait(semaphore, count)

    announce(barrier, 1)

    small = (
        pltpu.make_async_copy(pattern_far, pattern, load_sem.at[10]),
        pltpu.make_async_copy(owner_far, owner, load_sem.at[11]),
    )
    loads = []
    for k in range(4):
        loads.append(pltpu.make_async_copy(schur.at[sides[k]], raw.at[k], load_sem.at[k]))
        loads.append(pltpu.make_async_copy(residual.at[sides[k]], rows.at[k], load_sem.at[4 + k]))
    loads.append(pltpu.make_async_copy(basis, local, load_sem.at[8]))
    lowest = jnp.clip(story - 2, 0, STORIES - 5)
    loads.append(
        pltpu.make_async_copy(
            inverse.at[pl.ds(pl.multiple_of(lowest * ROW, 8), 5 * ROW)], slab, load_sem.at[9]
        )
    )
    for load in loads[:4]:
        load.start()

    line, lane = iota((BLK, BLK), 0), iota((BLK, BLK), 1)
    upper, equal = line <= lane, line == lane

    def diagonal_of(block):
        return jnp.sum(jnp.where(equal, block, 0.0), axis=0, keepdims=True)

    def to_sharer(f, m, source, target):
        return pltpu.make_async_remote_copy(
            src_ref=source, dst_ref=target, send_sem=face_send.at[f, m], recv_sem=face_recv.at[f, m],
            device_id=out_device[f], device_id_type=MESH,
        )

    def exchange(peers, source, target, send_sem, recv_sem):
        copies = []
        for r, peer in enumerate(peers):
            copies.append(
                pltpu.make_async_remote_copy(
                    src_ref=source(peer), dst_ref=target, send_sem=send_sem.at[r],
                    recv_sem=recv_sem.at[r], device_id=peer, device_id_type=MESH,
                )
            )
            copies[-1].start()
        return copies

    hear(barrier, 1)
    couplings = [
        to_sharer(f, 1, schur.at[out_side[f], pl.ds(NBLK, 2)], coupling_in.at[f]) for f in range(2)
    ]
    packs = [to_sharer(f, 0, pack_out.at[f], pack_in.at[f]) for f in range(2)]
    products = [to_sharer(f, 2, product_out.at[f], product_in.at[f]) for f in range(2)]
    bases = [to_sharer(f, 3, basis.at[out_side[f]], basis_in.at[f]) for f in range(2)]
    exists = jnp.where(odd == 0, story < STORIES - 1, story > 0)
    leaves = jnp.where(odd == 0, story > 0, story < STORIES - 1)

    def when(condition, f, action):
        if f == 0:
            pl.when(condition)(action)
        else:
            action()

    for f in range(2):
        when(leaves, f, couplings[f].start)
    for load in list(small) + loads[4:]:
        load.start()

    for f in range(2):
        loads[2 * f].wait()
        for h in range(2):
            first, second = raw[f, 2 * h], raw[f, 2 * h + 1]
            pack_out[f, h * BLK : (h + 1) * BLK] = jnp.where(upper, first, second)
            pack_out[f, 2 * BLK + h : 2 * BLK + h + 1] = diagonal_of(second)
        pack_out[f, 2 * BLK + 2 : 2 * BLK + 8] = jnp.zeros((6, BLK), F32)
        when(leaves, f, packs[f].start)
        when(leaves, f, bases[f].start)
    announce(near, 1)

    for copy in small:
        copy.wait()
    mine = [owner[0, in_side[f]].astype(F32) for f in range(2)]
    for f in range(2):
        flag[f : f + 1] = jnp.full((1, BLK), mine[f], F32)
    flag[2:8] = jnp.zeros((6, BLK), F32)
    flags[plan] = flag[...]

    for k in range(4):
        if k >= 2:
            loads[2 * k].wait()
        loads[2 * k + 1].wait()
        fill(table, raw[k, NBLK], raw[k, NBLK + 1])
        place(pattern, sides[k], table, [raw[k, n] for n in range(NBLK)], None, high, low)
        target = product_out.at[k] if k < 2 else product_own.at[k - 2]
        target[...] = product(rows[k], high[...], low[...])
        if k < 2:
            when(leaves, k, products[k].start)
    hear(near, 1)
    announce(middle, 2)

    present = (jnp.where(story > 0, 1.0, 0.0), jnp.where(story < STORIES - 1, 1.0, 0.0), 1.0, 1.0)
    loads[8].wait()
    wide[...] = jnp.zeros_like(wide)

    def widen(source, s, target):
        for n in range(NBLK):
            wide[target, 0:KC, n * BLK : (n + 1) * BLK] = source[s, pl.ds(n, KC, stride=NBLK)]

    for s in range(4):
        widen(local, s, s)
        basis_high, basis_low = split(wide[s] * present[s])
        here = pl.ds(s * FD, FD)
        basis_pack[:, here] = jnp.concatenate(
            [basis_high, basis_high, basis_low, jnp.zeros_like(basis_low)], axis=0
        )

    loads[9].wait()
    slab_high, slab_low = split(jnp.concatenate([slab[...], jnp.zeros((16, NCOARSE), F32)], axis=0))
    columns = dot(jnp.concatenate([slab_high, slab_low], axis=0), gather(plan)).astype(BF16)
    hear(middle, 2)
    announce(far, 4)
    noted = exchange(plan_peers, lambda peer: flag, flags.at[plan], send_flag, recv_flag)
    def sweeps(start, f):
        values = start
        for _ in range(ITERS - 1):
            values = start + product(values, ready_high[f], ready_low[f])
        return values

    def both_sweeps(start):
        values = start
        for _ in range(ITERS - 1):
            values = [start[f] + product(values[f], ready_high[f], ready_low[f]) for f in range(2)]
        return values

    owned_high[...] = jnp.zeros_like(owned_high)
    owned_low[...] = jnp.zeros_like(owned_low)
    scaled = [None, None]
    for f in (1, 0):
        when(exists, f, packs[f].wait_recv)
        when(exists, f, couplings[f].wait_recv)
        diagonal, scales = [], []
        for h in range(2):
            first, second = raw[2 + f, 2 * h], raw[2 + f, 2 * h + 1]
            packed = jnp.where(upper, first, second) + pack_in[f, h * BLK : (h + 1) * BLK]
            turned = packed.T
            second_diagonal = diagonal_of(second) + pack_in[f, 2 * BLK + h : 2 * BLK + h + 1]
            scales += [-DAMPING / diagonal_of(packed), -DAMPING / second_diagonal]
            diagonal.append(
                jnp.where(equal, 1.0 - DAMPING, jnp.where(upper, packed, turned) * scales[-2])
            )
            diagonal.append(
                jnp.where(equal, 1.0 - DAMPING, jnp.where(upper, turned, packed) * scales[-1])
            )
        fill(
            table,
            raw[2 + f, NBLK] + coupling_in[f, 0],
            raw[2 + f, NBLK + 1] + coupling_in[f, 1],
        )
        place(pattern, in_side[f], table, diagonal, scales, ready_high.at[f], ready_low.at[f])
        scaled[f] = jnp.concatenate(scales, axis=1)
        when(exists, f, bases[f].wait_recv)
        widen(basis_in, f, 4 + f)
        share = wide[in_side[f]] * mine[f] + wide[4 + f] * (1.0 - mine[f])
        share = sweeps(-share * scaled[f], f)
        if f == 0:
            share = jnp.where(exists, share, 0.0)
        share_high, share_low = split(share)
        for n in range(2):
            here = (pl.ds(64 * n + 32 * f, 32), pl.ds(f * FD, FD))
            owned_high[here], owned_low[here] = share_high, share_low

    right_side, contribution = [None, None], 0.0
    for f in (1, 0):
        when(exists, f, products[f].wait_recv)
        right_side[f] = product_own[f] + product_in[f]
        if f == 0:
            right_side[f] = jnp.where(exists, right_side[f], 0.0)
        here = pl.ds(f * FD, FD)
        contribution = contribution + product(
            right_side[f], owned_high[:, here], owned_low[:, here], dot_last
        )
    left = iota((RHS // 2, BLK), 1) < 64
    packed = jnp.where(left, contribution[: RHS // 2], contribution[RHS // 2 :])
    sent_first[...] = packed
    firsts = exchange(plan_peers, lambda peer: sent_first, got_first.at[plan], send_first, recv_first)

    got_first[plan] = packed
    hear(far, 4)
    announce(last, 8)
    for copy in noted:
        copy.wait_recv()
    height = story - lowest
    chosen = []
    for p in range(PLANS):
        for f in range(2):
            kept = jnp.concatenate([flags[p, f : f + 1]] * 2, axis=1)
            other = scatter(p, height + 1 - 2 * (p % 2)) if f == 0 else scatter(p + 1, height)
            chosen.append((scatter(p, height) * kept + other * (1.0 - kept)).astype(BF16))
    chosen = jnp.concatenate(chosen, axis=0)
    weight_high[...] = dot(chosen, columns[:256]).astype(BF16)
    weight_low[...] = dot(chosen, columns[256:]).astype(BF16)
    solved = both_sweeps([-right_side[f] * scaled[f] for f in range(2)])
    solved[0] = jnp.where(exists, solved[0], 0.0)
    for f in range(2):
        averaged[in_side[f]] = solved[f]

    def to_owner(f):
        return pltpu.make_async_remote_copy(
            src_ref=averaged.at[in_side[f]], dst_ref=averaged.at[out_side[f]],
            send_sem=back_send.at[f], recv_sem=back_recv.at[f],
            device_id=in_device[f], device_id_type=MESH,
        )

    backs = [to_owner(f) for f in range(2)]
    when(exists, 0, backs[0].start)

    @pl.when(jnp.logical_not(leaves))
    def _():
        averaged[out_side[0]] = jnp.zeros((RHS, FD), F32)


    for copy in firsts:
        copy.wait_recv()
    halves = ([], [])
    for p in range(0, PLANS, 2):
        first, second = got_first[p], got_first[p + 1]
        halves[0].append(jnp.where(left, first, pltpu.roll(second, 64, 1)))
        halves[1].append(jnp.where(left, pltpu.roll(first, 64, 1), second))
    gathered = jnp.concatenate([jnp.concatenate(half, axis=1) for half in halves], axis=0)
    hear(last, 8)
    quarter = iota((16, BLK), 1) >> 5
    seconds = []
    for n in range(STORIES // 4):
        if n % 2 == 0:
            here = pl.ds(n * BLK, 2 * BLK)
            coarse = product(gathered, weight_high[:, here], weight_low[:, here])
        tile = coarse[:, (n % 2) * BLK : (n % 2 + 1) * BLK]
        turned = [pltpu.roll(tile, 32 * g, 1) if g else tile for g in range(4)]
        for q in range(4):
            message = turned[(3 - q) % 4][48:64]
            for g in range(3):
                message = jnp.where(quarter == g, turned[(g - q) % 4][16 * g : 16 * g + 16], message)
            sent_second[4 * n + q] = message
        if n % 2 == 0:
            continue
        for i in range(4 * n - 4, 4 * n + 4):
            seconds.append(
                pltpu.make_async_remote_copy(
                    src_ref=sent_second.at[i], dst_ref=got_second.at[story], send_sem=send_second.at[i],
                    recv_sem=recv_second.at[story], device_id=(i, plan), device_id_type=MESH,
                )
            )
            pl.when(story != i)(seconds[-1].start)

    def arrival(i):
        return pltpu.make_async_remote_copy(
            src_ref=sent_second.at[i], dst_ref=got_second.at[i], send_sem=send_second.at[i],
            recv_sem=recv_second.at[i], device_id=(i, plan), device_id_type=MESH,
        )

    backs[1].start()
    got_second[story] = sent_second[story]
    for copies in (packs, couplings, products, bases):
        for f in range(2):
            when(leaves, f, copies[f].wait_send)
    for copy in noted + firsts:
        copy.wait_send()
    for i in range(STORIES):
        pl.when(story != i)(seconds[i].wait_send)
    for i in range(STORIES):
        pl.when(story != i)(arrival(i).wait_recv)
    total = got_second[0]
    for i in range(1, STORIES):
        total = total + got_second[i]
    parts = [total] + [pltpu.roll(total, BLK - 32 * g, 1) for g in range(1, 4)]
    needed = jnp.concatenate(parts, axis=0)
    needed = jnp.where(iota((RHS, BLK), 1) < 32, needed, 0.0)
    needed_high, needed_low = split(needed)
    needed_high, needed_low = needed_high.astype(F32), needed_low.astype(F32)
    operand = needed_high + pltpu.roll(needed_low, 32, 1) + pltpu.roll(needed_high, 64, 1)
    needed_part[...] = operand.astype(BF16)
    for f in range(2):
        when(exists, f, backs[f].wait_send)
        when(leaves, f, backs[f].wait_recv)


def store(averaged, needed, basis_pack, averaged_out, coarse_part_out, result, sem):
    copies = [pltpu.make_async_copy(averaged.at[s], averaged_out.at[s], sem.at[0, s]) for s in range(4)]
    for copy in copies:
        copy.start()
    for s in range(4):
        result[s] = dot(needed[...], basis_pack[:, s * FD : (s + 1) * FD])
        copies.append(pltpu.make_async_copy(result.at[s], coarse_part_out.at[s], sem.at[1, s]))
        copies[-1].start()
    for copy in copies:
        copy.wait()


def on_device(schur_blocks, off_pattern, face_owner, residual, coarse_basis, coarse_inverse):
    hbm = pl.BlockSpec(memory_space=pltpu.HBM)
    operands = [
        pltpu.with_memory_space_constraint(operand, pltpu.HBM)
        for operand in (
            schur_blocks.reshape(4, 6, BLK, BLK),
            off_pattern.reshape(4, 2, 2).transpose(1, 2, 0),
            face_owner.reshape(1, 4),
            residual.reshape(4, RHS, FD),
            coarse_basis.reshape(4, KC * NBLK, BLK),
            coarse_inverse,
        )
    ]
    vmem = pl.BlockSpec(memory_space=pltpu.VMEM)
    dma = pltpu.SemaphoreType.DMA
    out = pltpu.VMEM((4, RHS, FD), F32)
    averaged, needed, basis_pack = pl.pallas_call(
        kernel,
        out_shape=(out, pltpu.VMEM((RHS, BLK), BF16), pltpu.VMEM((BLK, 4 * FD), BF16)),
        in_specs=[hbm] * 6,
        out_specs=(vmem, vmem, vmem),
        scratch_shapes=[
            pltpu.SMEM((2, 2, 4), jnp.int32),
            pltpu.SMEM((1, 4), jnp.int32),
            pltpu.VMEM((4, 6, BLK, BLK), F32),
            pltpu.VMEM((4, RHS, FD), F32),
            pltpu.VMEM((4, KC * NBLK, BLK), F32),
            pltpu.VMEM((5 * ROW, NCOARSE), F32),
            pltpu.VMEM((9, BLK, BLK), F32),
            pltpu.VMEM((FD, FD), BF16),
            pltpu.VMEM((FD, FD), BF16),
            pltpu.VMEM((2, FD, FD), BF16),
            pltpu.VMEM((2, FD, FD), BF16),
            pltpu.VMEM((2, 2 * BLK + 8, BLK), F32),
            pltpu.VMEM((2, 2 * BLK + 8, BLK), F32),
            pltpu.VMEM((2, 2, BLK, BLK), F32),
            pltpu.VMEM((2, RHS, FD), F32),
            pltpu.VMEM((2, RHS, FD), F32),
            pltpu.VMEM((2, RHS, FD), F32),
            pltpu.VMEM((2, KC * NBLK, BLK), F32),
            pltpu.VMEM((6, 32, FD), F32),
            pltpu.VMEM((BLK, 2 * FD), BF16),
            pltpu.VMEM((BLK, 2 * FD), BF16),
            pltpu.VMEM((PLANS * 64, STORIES * 32), BF16),
            pltpu.VMEM((PLANS * 64, STORIES * 32), BF16),
            pltpu.VMEM((8, BLK), F32),
            pltpu.VMEM((PLANS, 8, BLK), F32),
            pltpu.VMEM((RHS // 2, BLK), F32),
            pltpu.VMEM((PLANS, RHS // 2, BLK), F32),
            pltpu.VMEM((STORIES, 16, BLK), F32),
            pltpu.VMEM((STORIES, 16, BLK), F32),
            dma((12,)),
            dma((2, 4)),
            dma((2, 4)),
            dma((2,)),
            dma((2,)),
            dma((PLANS - 1,)),
            dma((PLANS - 1,)),
            dma((PLANS - 1,)),
            dma((PLANS - 1,)),
            dma((STORIES,)),
            dma((STORIES,)),
            pltpu.SemaphoreType.REGULAR,
            pltpu.SemaphoreType.REGULAR,
            pltpu.SemaphoreType.REGULAR,
            pltpu.SemaphoreType.REGULAR,
        ],
        compiler_params=pltpu.CompilerParams(
            collective_id=0, has_side_effects=True, vmem_limit_bytes=40 * 1024 * 1024
        ),
    )(*operands)
    free = pl.BlockSpec(memory_space=pl.ANY)
    out = pltpu.HBM((4, RHS, FD), F32)
    averaged, coarse_part = pl.pallas_call(
        store,
        out_shape=(out, out),
        in_specs=[free, vmem, vmem],
        out_specs=(free, free),
        scratch_shapes=[pltpu.VMEM((4, RHS, FD), F32), dma((2, 4))],
        compiler_params=pltpu.CompilerParams(vmem_limit_bytes=16 * 1024 * 1024),
    )(*[pltpu.with_memory_space_constraint(value, pltpu.VMEM) for value in (averaged, needed, basis_pack)])
    shape = (1, 1, 4, 1, RHS, FD)
    return averaged.reshape(shape), coarse_part.reshape(shape)


def solution(mesh):
    in_specs = (
        P("story", "plan", None, None, None, None, None),
        P("story", "plan", None, None, None, None),
        P("story", "plan", None, None),
        P("story", "plan", None, None, None, None),
        P("story", "plan", None, None, None, None),
        P(),
    )
    out_specs = (
        P("story", "plan", None, None, None, None),
        P("story", "plan", None, None, None, None),
    )
    return jax.shard_map(
        on_device, mesh=mesh, in_specs=in_specs, out_specs=out_specs, check_vma=False
    )
```

```python
import jax
import jax.numpy as jnp
from jax import lax
from jax.experimental import pallas as pl
from jax.experimental.pallas import tpu as pltpu
from jax.sharding import PartitionSpec as P

ITERS = 6
DAMPING = 0.3
BLK = 128
NBLK = 4
RHS = 64
FD = 512
CPD = 6
KC = 30
STORIES = 16
PLANS = 8
ROW = PLANS * CPD
NCOARSE = STORIES * ROW
MESH = pl.DeviceIdType.MESH
F32 = jnp.float32
BF16 = jnp.bfloat16


def iota(shape, dim):
    return lax.broadcasted_iota(jnp.int32, shape, dim)


def split(value):
    high = value.astype(BF16)
    return high, (value - high.astype(F32)).astype(BF16)


def dot(left, right):
    return jnp.dot(left, right, preferred_element_type=F32)


def dot_last(left, right):
    return lax.dot_general(left, right, (((1,), (1,)), ((), ())), preferred_element_type=F32)


def product(value, high, low, dot=dot):
    rows = value.shape[0]
    first, second = split(value)
    both = dot(jnp.concatenate([first, second], axis=0), high)
    return both[:rows] + both[rows:] + dot(first, low)


def fill(table, first, second):
    zero = jnp.zeros_like(first)
    for a, left in enumerate((zero, first, first.T)):
        for b, right in enumerate((zero, second, second.T)):
            table[3 * a + b] = left + right


def choice(pattern, side, q, t):
    index = 0
    for k in range(2):
        row, column = pattern[k, 0, side], pattern[k, 1, side]
        plain = jnp.where((row == q) & (column == t), 1, 0)
        turned = jnp.where((row == t) & (column == q), 2, 0)
        index = 3 * index + plain + turned
    return index


def place(pattern, side, table, diagonal, scales, high, low):
    for q in range(NBLK):
        for t in range(NBLK):
            if q == t:
                block = diagonal[q]
            else:
                block = table[choice(pattern, side, q, t)]
                if scales is not None:
                    block = block * scales[t]
            here = (pl.ds(q * BLK, BLK), pl.ds(t * BLK, BLK))
            high[here], low[here] = split(block)


def places(dof):
    group = (dof * 43) >> 8
    storey = jnp.where(group == 1, -1, jnp.where(group == 2, 1, 0))
    column = jnp.where(group == 4, 1, jnp.where(group == 3, PLANS - 1, 0))
    return storey, column, dof - CPD * group


def scatter(plan, shift):
    dof, lane = iota((32, 256), 0), iota((32, 256), 1)
    storey, column, member = places(dof)
    target = (storey + shift) * ROW + ((plan + column) & (PLANS - 1)) * CPD + member
    return jnp.where((lane == target) & (dof < KC), 1.0, 0.0)


def gather(plan):
    lane = iota((1, STORIES * 32), 1)
    dof = lane & 31
    storey, column, member = places(dof)
    storey = storey + (lane >> 5)
    target = storey * ROW + ((plan + column) & (PLANS - 1)) * CPD + member
    target = jnp.where((dof < KC) & (storey >= 0) & (storey < STORIES), target, -1)
    return jnp.where(iota((NCOARSE, STORIES * 32), 0) == target, 1.0, 0.0).astype(BF16)


def kernel(
    schur, pattern_far, owner_far, residual, basis, inverse,
    averaged, needed_part, basis_pack,
    pattern, owner, raw, rows, local, slab, table, high, low, ready_high, ready_low,
    pack_out, pack_in, coupling_in, product_out, product_in, product_own, basis_in,
    wide, owned_high, owned_low, weight_high, weight_low, flag, flags,
    sent_first, got_first, sent_second, got_second,
    load_sem, face_send, face_recv, back_send, back_recv,
    send_flag, recv_flag, send_first, recv_first, send_second, recv_second, near, middle, far, last,
):
    story, plan = lax.axis_index("story"), lax.axis_index("plan")
    odd = lax.rem(plan, 2)
    step = 1 - 2 * odd
    in_side = (1 - odd, 3)
    out_side = (odd, 2)
    sides = (out_side[0], out_side[1], in_side[0], in_side[1])
    in_device = ((lax.rem(story + step + STORIES, STORIES), plan), (story, lax.rem(plan + 1, PLANS)))
    out_device = (
        (lax.rem(story - step + STORIES, STORIES), plan),
        (story, lax.rem(plan + PLANS - 1, PLANS)),
    )
    plan_peers = [(story, lax.rem(plan + r, PLANS)) for r in (4, 3, 5, 2, 6, 1, 7)]

    barrier = pltpu.get_barrier_semaphore()

    def around(distance):
        peers = [
            (story >= distance, (lax.rem(story + STORIES - distance, STORIES), plan)),
            (story < STORIES - distance, (lax.rem(story + distance, STORIES), plan)),
        ]
        if distance <= PLANS // 2:
            for r in sorted({distance, PLANS - distance}):
                peers.append((None, (story, lax.rem(plan + r, PLANS))))
        return peers

    def announce(semaphore, distance):
        for condition, peer in around(distance):
            def signal(peer=peer):
                pl.semaphore_signal(semaphore, inc=1, device_id=peer, device_id_type=MESH)

            if condition is None:
                signal()
            else:
                pl.when(condition)(signal)

    def hear(semaphore, distance):
        count = 0
        for condition, _ in around(distance):
            count = count + (1 if condition is None else jnp.where(condition, 1, 0))
        pl.semaphore_wait(semaphore, count)

    announce(barrier, 1)

    small = (
        pltpu.make_async_copy(pattern_far, pattern, load_sem.at[10]),
        pltpu.make_async_copy(owner_far, owner, load_sem.at[11]),
    )
    loads = []
    for k in range(4):
        loads.append(pltpu.make_async_copy(schur.at[sides[k]], raw.at[k], load_sem.at[k]))
        loads.append(pltpu.make_async_copy(residual.at[sides[k]], rows.at[k], load_sem.at[4 + k]))
    loads.append(pltpu.make_async_copy(basis, local, load_sem.at[8]))
    lowest = jnp.clip(story - 2, 0, STORIES - 5)
    loads.append(
        pltpu.make_async_copy(
            inverse.at[pl.ds(pl.multiple_of(lowest * ROW, 8), 5 * ROW)], slab, load_sem.at[9]
        )
    )
    for load in loads[:4]:
        load.start()

    line, lane = iota((BLK, BLK), 0), iota((BLK, BLK), 1)
    upper, equal = line <= lane, line == lane

    def diagonal_of(block):
        return jnp.sum(jnp.where(equal, block, 0.0), axis=0, keepdims=True)

    def to_sharer(f, m, source, target):
        return pltpu.make_async_remote_copy(
            src_ref=source, dst_ref=target, send_sem=face_send.at[f, m], recv_sem=face_recv.at[f, m],
            device_id=out_device[f], device_id_type=MESH,
        )

    def exchange(peers, source, target, send_sem, recv_sem):
        copies = []
        for r, peer in enumerate(peers):
            copies.append(
                pltpu.make_async_remote_copy(
                    src_ref=source(peer), dst_ref=target, send_sem=send_sem.at[r],
                    recv_sem=recv_sem.at[r], device_id=peer, device_id_type=MESH,
                )
            )
            copies[-1].start()
        return copies

    hear(barrier, 1)
    couplings = [
        to_sharer(f, 1, schur.at[out_side[f], pl.ds(NBLK, 2)], coupling_in.at[f]) for f in range(2)
    ]
    packs = [to_sharer(f, 0, pack_out.at[f], pack_in.at[f]) for f in range(2)]
    products = [to_sharer(f, 2, product_out.at[f], product_in.at[f]) for f in range(2)]
    bases = [to_sharer(f, 3, basis.at[out_side[f]], basis_in.at[f]) for f in range(2)]
    exists = jnp.where(odd == 0, story < STORIES - 1, story > 0)
    leaves = jnp.where(odd == 0, story > 0, story < STORIES - 1)

    def when(condition, f, action):
        if f == 0:
            pl.when(condition)(action)
        else:
            action()

    for f in range(2):
        when(leaves, f, couplings[f].start)
    for load in list(small) + loads[4:]:
        load.start()

    for f in range(2):
        loads[2 * f].wait()
        for h in range(2):
            first, second = raw[f, 2 * h], raw[f, 2 * h + 1]
            pack_out[f, h * BLK : (h + 1) * BLK] = jnp.where(upper, first, second)
            pack_out[f, 2 * BLK + h : 2 * BLK + h + 1] = diagonal_of(second)
        pack_out[f, 2 * BLK + 2 : 2 * BLK + 8] = jnp.zeros((6, BLK), F32)
        when(leaves, f, packs[f].start)
        when(leaves, f, bases[f].start)
    announce(near, 1)

    for copy in small:
        copy.wait()
    mine = [owner[0, in_side[f]].astype(F32) for f in range(2)]
    for f in range(2):
        flag[f : f + 1] = jnp.full((1, BLK), mine[f], F32)
    flag[2:8] = jnp.zeros((6, BLK), F32)
    flags[plan] = flag[...]

    for k in range(4):
        if k >= 2:
            loads[2 * k].wait()
        loads[2 * k + 1].wait()
        fill(table, raw[k, NBLK], raw[k, NBLK + 1])
        place(pattern, sides[k], table, [raw[k, n] for n in range(NBLK)], None, high, low)
        target = product_out.at[k] if k < 2 else product_own.at[k - 2]
        target[...] = product(rows[k], high[...], low[...])
        if k < 2:
            when(leaves, k, products[k].start)
    hear(near, 1)
    announce(middle, 2)

    present = (jnp.where(story > 0, 1.0, 0.0), jnp.where(story < STORIES - 1, 1.0, 0.0), 1.0, 1.0)
    loads[8].wait()
    wide[...] = jnp.zeros_like(wide)

    def widen(source, s, target):
        for n in range(NBLK):
            wide[target, 0:KC, n * BLK : (n + 1) * BLK] = source[s, pl.ds(n, KC, stride=NBLK)]

    for s in range(4):
        widen(local, s, s)
        basis_high, basis_low = split(wide[s] * present[s])
        here = pl.ds(s * FD, FD)
        basis_pack[:, here] = jnp.concatenate(
            [basis_high, basis_high, basis_low, jnp.zeros_like(basis_low)], axis=0
        )

    loads[9].wait()
    slab_high, slab_low = split(jnp.concatenate([slab[...], jnp.zeros((16, NCOARSE), F32)], axis=0))
    columns = dot(jnp.concatenate([slab_high, slab_low], axis=0), gather(plan)).astype(BF16)
    hear(middle, 2)
    announce(far, 4)
    noted = exchange(plan_peers, lambda peer: flag, flags.at[plan], send_flag, recv_flag)
    def sweeps(start, f):
        values = start
        for _ in range(ITERS - 1):
            values = start + product(values, ready_high[f], ready_low[f])
        return values

    def both_sweeps(start):
        values = start
        for _ in range(ITERS - 1):
            values = [start[f] + product(values[f], ready_high[f], ready_low[f]) for f in range(2)]
        return values

    owned_high[...] = jnp.zeros_like(owned_high)
    owned_low[...] = jnp.zeros_like(owned_low)
    scaled = [None, None]
    for f in (1, 0):
        when(exists, f, packs[f].wait_recv)
        when(exists, f, couplings[f].wait_recv)
        diagonal, scales = [], []
        for h in range(2):
            first, second = raw[2 + f, 2 * h], raw[2 + f, 2 * h + 1]
            packed = jnp.where(upper, first, second) + pack_in[f, h * BLK : (h + 1) * BLK]
            turned = packed.T
            second_diagonal = diagonal_of(second) + pack_in[f, 2 * BLK + h : 2 * BLK + h + 1]
            scales += [-DAMPING / diagonal_of(packed), -DAMPING / second_diagonal]
            diagonal.append(
                jnp.where(equal, 1.0 - DAMPING, jnp.where(upper, packed, turned) * scales[-2])
            )
            diagonal.append(
                jnp.where(equal, 1.0 - DAMPING, jnp.where(upper, turned, packed) * scales[-1])
            )
        fill(
            table,
            raw[2 + f, NBLK] + coupling_in[f, 0],
            raw[2 + f, NBLK + 1] + coupling_in[f, 1],
        )
        place(pattern, in_side[f], table, diagonal, scales, ready_high.at[f], ready_low.at[f])
        scaled[f] = jnp.concatenate(scales, axis=1)
        when(exists, f, bases[f].wait_recv)
        widen(basis_in, f, 4 + f)
        share = wide[in_side[f]] * mine[f] + wide[4 + f] * (1.0 - mine[f])
        share = sweeps(-share * scaled[f], f)
        if f == 0:
            share = jnp.where(exists, share, 0.0)
        share_high, share_low = split(share)
        for n in range(2):
            here = (pl.ds(64 * n + 32 * f, 32), pl.ds(f * FD, FD))
            owned_high[here], owned_low[here] = share_high, share_low

    right_side, contribution = [None, None], 0.0
    for f in (1, 0):
        when(exists, f, products[f].wait_recv)
        right_side[f] = product_own[f] + product_in[f]
        if f == 0:
            right_side[f] = jnp.where(exists, right_side[f], 0.0)
        here = pl.ds(f * FD, FD)
        contribution = contribution + product(
            right_side[f], owned_high[:, here], owned_low[:, here], dot_last
        )
    left = iota((RHS // 2, BLK), 1) < 64
    packed = jnp.where(left, contribution[: RHS // 2], contribution[RHS // 2 :])
    sent_first[...] = packed
    firsts = exchange(plan_peers, lambda peer: sent_first, got_first.at[plan], send_first, recv_first)

    got_first[plan] = packed
    hear(far, 4)
    announce(last, 8)
    for copy in noted:
        copy.wait_recv()
    height = story - lowest
    chosen = []
    for p in range(PLANS):
        for f in range(2):
            kept = jnp.concatenate([flags[p, f : f + 1]] * 2, axis=1)
            other = scatter(p, height + 1 - 2 * (p % 2)) if f == 0 else scatter(p + 1, height)
            chosen.append((scatter(p, height) * kept + other * (1.0 - kept)).astype(BF16))
    chosen = jnp.concatenate(chosen, axis=0)
    weight_high[...] = dot(chosen, columns[:256]).astype(BF16)
    weight_low[...] = dot(chosen, columns[256:]).astype(BF16)
    solved = both_sweeps([-right_side[f] * scaled[f] for f in range(2)])
    solved[0] = jnp.where(exists, solved[0], 0.0)
    for f in range(2):
        averaged[in_side[f]] = solved[f]

    def to_owner(f):
        return pltpu.make_async_remote_copy(
            src_ref=averaged.at[in_side[f]], dst_ref=averaged.at[out_side[f]],
            send_sem=back_send.at[f], recv_sem=back_recv.at[f],
            device_id=in_device[f], device_id_type=MESH,
        )

    backs = [to_owner(f) for f in range(2)]
    when(exists, 0, backs[0].start)

    @pl.when(jnp.logical_not(leaves))
    def _():
        averaged[out_side[0]] = jnp.zeros((RHS, FD), F32)


    for copy in firsts:
        copy.wait_recv()
    halves = ([], [])
    for p in range(0, PLANS, 2):
        first, second = got_first[p], got_first[p + 1]
        halves[0].append(jnp.where(left, first, pltpu.roll(second, 64, 1)))
        halves[1].append(jnp.where(left, pltpu.roll(first, 64, 1), second))
    gathered = jnp.concatenate([jnp.concatenate(half, axis=1) for half in halves], axis=0)
    hear(last, 8)
    quarter = iota((16, BLK), 1) >> 5
    seconds = []
    for n in range(STORIES // 4):
        if n % 2 == 0:
            here = pl.ds(n * BLK, 2 * BLK)
            coarse = product(gathered, weight_high[:, here], weight_low[:, here])
        tile = coarse[:, (n % 2) * BLK : (n % 2 + 1) * BLK]
        turned = [pltpu.roll(tile, 32 * g, 1) if g else tile for g in range(4)]
        for q in range(4):
            message = turned[(3 - q) % 4][48:64]
            for g in range(3):
                message = jnp.where(quarter == g, turned[(g - q) % 4][16 * g : 16 * g + 16], message)
            sent_second[4 * n + q] = message
        if n % 2 == 0:
            continue
        for i in range(4 * n - 4, 4 * n + 4):
            seconds.append(
                pltpu.make_async_remote_copy(
                    src_ref=sent_second.at[i], dst_ref=got_second.at[story], send_sem=send_second.at[i],
                    recv_sem=recv_second.at[story], device_id=(i, plan), device_id_type=MESH,
                )
            )
            pl.when(story != i)(seconds[-1].start)

    def arrival(i):
        return pltpu.make_async_remote_copy(
            src_ref=sent_second.at[i], dst_ref=got_second.at[i], send_sem=send_second.at[i],
            recv_sem=recv_second.at[i], device_id=(i, plan), device_id_type=MESH,
        )

    backs[1].start()
    got_second[story] = sent_second[story]
    for copies in (packs, couplings, products, bases):
        for f in range(2):
            when(leaves, f, copies[f].wait_send)
    for copy in noted + firsts:
        copy.wait_send()
    for i in range(STORIES):
        pl.when(story != i)(seconds[i].wait_send)
    for i in range(STORIES):
        pl.when(story != i)(arrival(i).wait_recv)
    total = got_second[0]
    for i in range(1, STORIES):
        total = total + got_second[i]
    parts = [total] + [pltpu.roll(total, BLK - 32 * g, 1) for g in range(1, 4)]
    needed = jnp.concatenate(parts, axis=0)
    needed = jnp.where(iota((RHS, BLK), 1) < 32, needed, 0.0)
    needed_high, needed_low = split(needed)
    needed_high, needed_low = needed_high.astype(F32), needed_low.astype(F32)
    operand = needed_high + pltpu.roll(needed_low, 32, 1) + pltpu.roll(needed_high, 64, 1)
    needed_part[...] = operand.astype(BF16)
    for f in range(2):
        when(exists, f, backs[f].wait_send)
        when(leaves, f, backs[f].wait_recv)


def store(averaged, needed, basis_pack, averaged_out, coarse_part_out, result, sem):
    copies = [pltpu.make_async_copy(averaged, averaged_out, sem.at[0, 0])]
    copies[0].start()
    for s in range(4):
        result[s] = dot(needed[...], basis_pack[:, s * FD : (s + 1) * FD])
        copies.append(pltpu.make_async_copy(result.at[s], coarse_part_out.at[s], sem.at[1, s]))
        copies[-1].start()
    for copy in copies:
        copy.wait()


def on_device(schur_blocks, off_pattern, face_owner, residual, coarse_basis, coarse_inverse):
    hbm = pl.BlockSpec(memory_space=pltpu.HBM)
    operands = [
        pltpu.with_memory_space_constraint(operand, pltpu.HBM)
        for operand in (
            schur_blocks.reshape(4, 6, BLK, BLK),
            off_pattern.reshape(4, 2, 2).transpose(1, 2, 0),
            face_owner.reshape(1, 4),
            residual.reshape(4, RHS, FD),
            coarse_basis.reshape(4, KC * NBLK, BLK),
            coarse_inverse,
        )
    ]
    vmem = pl.BlockSpec(memory_space=pltpu.VMEM)
    dma = pltpu.SemaphoreType.DMA
    out = pltpu.VMEM((4, RHS, FD), F32)
    averaged, needed, basis_pack = pl.pallas_call(
        kernel,
        out_shape=(out, pltpu.VMEM((RHS, BLK), BF16), pltpu.VMEM((BLK, 4 * FD), BF16)),
        in_specs=[hbm] * 6,
        out_specs=(vmem, vmem, vmem),
        scratch_shapes=[
            pltpu.SMEM((2, 2, 4), jnp.int32),
            pltpu.SMEM((1, 4), jnp.int32),
            pltpu.VMEM((4, 6, BLK, BLK), F32),
            pltpu.VMEM((4, RHS, FD), F32),
            pltpu.VMEM((4, KC * NBLK, BLK), F32),
            pltpu.VMEM((5 * ROW, NCOARSE), F32),
            pltpu.VMEM((9, BLK, BLK), F32),
            pltpu.VMEM((FD, FD), BF16),
            pltpu.VMEM((FD, FD), BF16),
            pltpu.VMEM((2, FD, FD), BF16),
            pltpu.VMEM((2, FD, FD), BF16),
            pltpu.VMEM((2, 2 * BLK + 8, BLK), F32),
            pltpu.VMEM((2, 2 * BLK + 8, BLK), F32),
            pltpu.VMEM((2, 2, BLK, BLK), F32),
            pltpu.VMEM((2, RHS, FD), F32),
            pltpu.VMEM((2, RHS, FD), F32),
            pltpu.VMEM((2, RHS, FD), F32),
            pltpu.VMEM((2, KC * NBLK, BLK), F32),
            pltpu.VMEM((6, 32, FD), F32),
            pltpu.VMEM((BLK, 2 * FD), BF16),
            pltpu.VMEM((BLK, 2 * FD), BF16),
            pltpu.VMEM((PLANS * 64, STORIES * 32), BF16),
            pltpu.VMEM((PLANS * 64, STORIES * 32), BF16),
            pltpu.VMEM((8, BLK), F32),
            pltpu.VMEM((PLANS, 8, BLK), F32),
            pltpu.VMEM((RHS // 2, BLK), F32),
            pltpu.VMEM((PLANS, RHS // 2, BLK), F32),
            pltpu.VMEM((STORIES, 16, BLK), F32),
            pltpu.VMEM((STORIES, 16, BLK), F32),
            dma((12,)),
            dma((2, 4)),
            dma((2, 4)),
            dma((2,)),
            dma((2,)),
            dma((PLANS - 1,)),
            dma((PLANS - 1,)),
            dma((PLANS - 1,)),
            dma((PLANS - 1,)),
            dma((STORIES,)),
            dma((STORIES,)),
            pltpu.SemaphoreType.REGULAR,
            pltpu.SemaphoreType.REGULAR,
            pltpu.SemaphoreType.REGULAR,
            pltpu.SemaphoreType.REGULAR,
        ],
        compiler_params=pltpu.CompilerParams(
            collective_id=0, has_side_effects=True, vmem_limit_bytes=40 * 1024 * 1024
        ),
    )(*operands)
    free = pl.BlockSpec(memory_space=pl.ANY)
    out = pltpu.HBM((4, RHS, FD), F32)
    averaged, coarse_part = pl.pallas_call(
        store,
        out_shape=(out, out),
        in_specs=[free, vmem, vmem],
        out_specs=(free, free),
        scratch_shapes=[pltpu.VMEM((4, RHS, FD), F32), dma((2, 4))],
        compiler_params=pltpu.CompilerParams(vmem_limit_bytes=16 * 1024 * 1024),
    )(*[pltpu.with_memory_space_constraint(value, pltpu.VMEM) for value in (averaged, needed, basis_pack)])
    shape = (1, 1, 4, 1, RHS, FD)
    return averaged.reshape(shape), coarse_part.reshape(shape)


def solution(mesh):
    in_specs = (
        P("story", "plan", None, None, None, None, None),
        P("story", "plan", None, None, None, None),
        P("story", "plan", None, None),
        P("story", "plan", None, None, None, None),
        P("story", "plan", None, None, None, None),
        P(),
    )
    out_specs = (
        P("story", "plan", None, None, None, None),
        P("story", "plan", None, None, None, None),
    )
    return jax.shard_map(
        on_device, mesh=mesh, in_specs=in_specs, out_specs=out_specs, check_vma=False
    )
```
